512 devices in a mesh: blk: 32 (over y_lo, z, core), qgroup: 16 (over x, y_hi).
Axes of the slice: x: 4, y: 8 (y_hi: 4, y_lo: 2; y = y_hi * 2 + y_lo), z: 8, core: 2. Of those that a mesh axis runs over, the one named last changes fastest.
Arguments:
- queries: bfloat16 [16, 256, 4096], P('qgroup', 'blk'), may hold values from -6 to 6
- passages: bfloat16 [8192, 4096], P('blk'), may hold values from -6 to 6
- teacher: float32 [16, 256, 8192], P('qgroup', None, 'blk'), may hold values from -20 to 340
- teacher_rows: int32 [16, 256], P('qgroup', 'blk'), may hold values from 0 to 255, each once within a row
- positives: int32 [16, 256], P('qgroup', 'blk'), may hold values from 0 to 8191
Outputs:
- loss: float32 [16, 256], P('qgroup', 'blk')
- query_grads: bfloat16 [16, 256, 4096], P('qgroup', 'blk')
- passage_grads: bfloat16 [8192, 4096], P('blk', 'qgroup')
The draws below stay inside these ranges and needn't reach their ends.
Inputs may be any that keep to these rules, and one draw needn't show every extreme that they name: Each group's row of teacher_rows lists all 256 teacher rows once.
All inputs are finite; a program needn't handle non-finite values.
Results may differ from the reference program's by a relative error of at most 0.0051.
Values may be sent and summed in bfloat16 or wider, within the bound.
No kernel may reach another device: no remote copies, remote signals or barrier semaphores. Data moves between devices by JAX's collectives and lax.ppermute only.
A program may use at most 64 MiB of HBM per device.

```python
import jax
import jax.numpy as jnp
from jax import lax

D = 4096
QG_ROWS = 256
NP = 8192
QGROUPS = 16


def passage_parts(key, low, high):
    scale_key, noise_key = jax.random.split(key)
    noise = jnp.clip(jax.random.normal(noise_key, (NP, D), jnp.float32), -6.0, 6.0)
    index = jnp.arange(NP, dtype=jnp.float32)
    spread = jnp.exp(jax.random.uniform(scale_key, (NP,), jnp.float32, jnp.log(low), jnp.log(high)))
    sigma = jnp.exp(jnp.log(3.0) * index / NP) * spread
    return (noise, sigma)


def draw_passages(key, part):
    low, high = (0.5, 1.0)
    noise, sigma = passage_parts(key, low, high)
    values = noise * (sigma / jnp.sqrt(float(D)))[:, None]
    return values.astype(jnp.bfloat16)


def draw_queries(key, part):
    row_low, row_high, lift = (0.5, 1.5, 0.0)
    key = jax.random.fold_in(key, 5)
    own_key = jax.random.fold_in(key, 0)
    flag_key = jax.random.fold_in(key, 4)
    scale_key = jax.random.fold_in(key, 5)
    root = jnp.sqrt(float(D))
    own = jnp.clip(jax.random.normal(own_key, (QGROUPS, QG_ROWS, D), jnp.float32), -6.0, 6.0) / root
    row_scale = jnp.exp(jax.random.uniform(scale_key, (QGROUPS, QG_ROWS, 1), jnp.float32, jnp.log(row_low), jnp.log(row_high)))
    own = own * row_scale
    flag = (jax.random.randint(flag_key, (QGROUPS, QG_ROWS), 0, 16) == 0).astype(jnp.float32) * lift
    flag = flag[..., None]
    values = own * (1.0 - flag)
    return jnp.clip(values, -6.0, 6.0).astype(jnp.bfloat16)


def draw_teacher(key, part):
    key = jax.random.fold_in(key, 7)
    base_key = jax.random.fold_in(key, 0)
    base = jnp.clip(3.0 * jax.random.normal(base_key, (QGROUPS, QG_ROWS, NP), jnp.float32), -18.0, 18.0)
    return base


def place_ends(drawn, rng, least, high):
    place = [jax.random.randint(jax.random.fold_in(rng, axis), (), 0, length) for axis, length in enumerate(drawn.shape)]
    longest = drawn.shape.index(max(drawn.shape))
    next_to = place[:longest] + [(place[longest] + 1) % drawn.shape[longest]] + place[longest + 1:]
    return drawn.at[tuple(place)].set(least).at[tuple(next_to)].set(high)


def setup_inputs(seed: int = 0) -> dict:
    seeds = jax.random.split(jax.random.key(seed), 6)
    return {
        "queries": draw_queries(jax.random.fold_in(seeds[5], 71), 0),
        "passages": draw_passages(jax.random.fold_in(seeds[5], 71), 0),
        "teacher": draw_teacher(jax.random.fold_in(seeds[5], 71), 0),
        "teacher_rows": jax.vmap(lambda own: jax.random.permutation(own, QG_ROWS))(jax.random.split(seeds[3], QGROUPS)).reshape((QGROUPS, QG_ROWS)).astype(jnp.int32),
        "positives": place_ends(jax.random.randint(seeds[4], (QGROUPS, QG_ROWS), 0, NP), jax.random.fold_in(seeds[4], 1), 0, NP - 1).astype(jnp.int32),
    }


inv_temp = 50.0


def log_softmax_rows(values):
    top = jnp.max(values, axis=1, keepdims=True)
    total = jnp.sum(jnp.exp(values - top), axis=1, keepdims=True)
    return values - top - jnp.log(total)


def reference(queries, passages, teacher, teacher_rows, positives):
    def group_step(carry, inputs):
        group_query, teacher_table, row_index, positive = inputs
        scores = jnp.dot(group_query, passages.T, preferred_element_type=jnp.float32) * inv_temp
        log_student = log_softmax_rows(scores)
        student_prob = jnp.exp(log_student)
        teacher_logits = jnp.take(teacher_table, row_index.astype(jnp.int32), axis=0)
        log_teacher = log_softmax_rows(teacher_logits)
        teacher_prob = jnp.exp(log_teacher)
        columns = jnp.arange(NP, dtype=jnp.int32)
        onehot = columns[None, :] == positive.astype(jnp.int32)[:, None]
        own_term = jnp.sum(jnp.where(onehot, log_student, 0.0), axis=1)
        loss_rows = jnp.sum(teacher_prob * (log_teacher - log_student), axis=1) - own_term
        score_grads = (inv_temp * (2.0 * student_prob - teacher_prob - onehot.astype(jnp.float32))).astype(jnp.bfloat16)
        query_total = jnp.dot(score_grads, passages, preferred_element_type=jnp.float32)
        passage_term = lax.dot_general(score_grads, group_query, (((0,), (0,)), ((), ())), preferred_element_type=jnp.float32)
        carry = carry + lax.optimization_barrier(passage_term.astype(jnp.bfloat16)).astype(jnp.float32)
        return carry, (loss_rows, query_total.astype(jnp.bfloat16))

    passage_total, outputs = lax.scan(group_step, jnp.zeros((NP, D), jnp.float32), (queries, teacher, teacher_rows, positives))
    loss, query_grads = outputs
    return loss, query_grads, passage_total.astype(jnp.bfloat16)
```

```python
import jax
import jax.numpy as jnp
from jax import lax
from jax.sharding import Mesh, PartitionSpec as P

inv_temp = 50.0
YL, CORES, X = 2, 2, 4
LANES = 128
CHIPS = ("yl", "z")
f32, bf16 = jnp.float32, jnp.bfloat16


def swap_cores(value):
    return lax.ppermute(value, "core", [(0, 1), (1, 0)])


def per_device(queries, passages, teacher, teacher_rows, positives):
    own_rows, depth = queries.shape[1:]
    block_rows = passages.shape[0]
    chips = lax.axis_size("yl") * lax.axis_size("z")
    x_size, yh_size = lax.axis_size("x"), lax.axis_size("yh")
    rows = chips * own_rows
    chip = lax.axis_index("yl") * lax.axis_size("z") + lax.axis_index("z")
    core = lax.axis_index("core")

    indices = jnp.stack(
        [teacher_rows[0], positives[0] // 256, positives[0] % 256], axis=1
    ).astype(bf16)
    sent = jnp.concatenate(
        [queries[0], jnp.pad(indices, ((0, 0), (0, LANES - indices.shape[1])))], axis=1
    )
    passages_other = swap_cores(passages)
    teacher_other = swap_cores(teacher[0])
    gathered = lax.all_to_all(
        jnp.broadcast_to(sent[None], (chips,) + sent.shape), CHIPS, 0, 0, tiled=True
    ).reshape(rows, depth + LANES)
    query = gathered[:, :depth]
    query_other = swap_cores(query)
    codes = gathered[:, depth : depth + LANES].astype(f32).T
    row_index = codes[0:1].astype(jnp.int32)
    positive = codes[1:2].astype(jnp.int32) * 256 + codes[2:3].astype(jnp.int32)

    pick = (lax.broadcasted_iota(jnp.int32, (teacher.shape[1], rows), 0) == row_index).astype(f32)

    def columns(block, logits, which):
        scores = inv_temp * lax.dot_general(
            block, query, (((1,), (1,)), ((), ())), preferred_element_type=f32
        )
        picked = lax.dot_general(
            logits, pick, (((0,), (0,)), ((), ())),
            precision=lax.Precision.HIGHEST, preferred_element_type=f32,
        )
        place = (chip * CORES + which) * block_rows
        onehot = lax.broadcasted_iota(jnp.int32, (block_rows, rows), 0) + place == positive
        return scores, picked, onehot

    parts = [columns(passages, teacher[0], core), columns(passages_other, teacher_other, 1 - core)]
    top_student = jnp.maximum(*[jnp.max(s, axis=0, keepdims=True) for s, _, _ in parts])
    top_teacher = jnp.maximum(*[jnp.max(t, axis=0, keepdims=True) for _, t, _ in parts])
    sums = []
    for s, t, hot in parts:
        below_s, below_t = s - top_student, t - top_teacher
        weight = jnp.exp(below_t)
        sums.append(
            [
                jnp.sum(v, axis=0, keepdims=True)
                for v in (jnp.exp(below_s), weight, weight * (below_t - below_s), jnp.where(hot, s, 0.0))
            ]
        )
    sums = [a + b for a, b in zip(*sums)]
    stats = jnp.concatenate([top_student, top_teacher] + sums + [jnp.zeros((2, rows), f32)], axis=0)
    stats = lax.all_to_all(
        jnp.broadcast_to(stats[None], (chips,) + stats.shape), CHIPS, 0, 0, tiled=True
    )
    tops_s, tops_t, sums_s, sums_t, cross, hits = (stats[:, i] for i in range(6))
    top_s, top_t = jnp.max(tops_s, axis=0, keepdims=True), jnp.max(tops_t, axis=0, keepdims=True)
    lower_s, lower_t = tops_s - top_s, tops_t - top_t
    total_s = jnp.sum(jnp.exp(lower_s) * sums_s, axis=0, keepdims=True)
    weight_t = jnp.exp(lower_t)
    total_t = jnp.sum(weight_t * sums_t, axis=0, keepdims=True)
    cross = jnp.sum(weight_t * (cross + (lower_t - lower_s) * sums_t), axis=0, keepdims=True)
    hit = jnp.sum(hits, axis=0, keepdims=True)
    log_s = jnp.log(total_s)
    losses = cross / total_t - jnp.log(total_t) + log_s - (hit - top_s - log_s)
    loss = lax.dynamic_slice_in_dim(losses[0], chip * own_rows, own_rows)

    scale_s, scale_t = 2.0 * inv_temp / total_s, inv_temp / total_t
    grads, grads_other = (
        (jnp.exp(s - top_s) * scale_s - jnp.exp(t - top_t) * scale_t - jnp.where(hot, inv_temp, 0.0)).astype(bf16)
        for s, t, hot in parts
    )
    grads_back = swap_cores(grads_other)

    query_part = sum(
        lax.dot_general(a, b, (((0,), (0,)), ((), ())), preferred_element_type=f32)
        for a, b in ((grads, passages), (grads_other, passages_other))
    )
    query_parts = lax.all_to_all(
        query_part.astype(bf16).reshape(chips, own_rows, depth), CHIPS, 0, 0, tiled=True
    )
    query_total = jnp.sum(query_parts.astype(f32), axis=0)

    passage_part = jnp.dot(grads, query, preferred_element_type=f32) + jnp.dot(
        grads_back, query_other, preferred_element_type=f32
    )
    passage_part = passage_part.astype(bf16).reshape(block_rows, x_size, depth // x_size).transpose(1, 0, 2)
    passage_part = lax.all_to_all(passage_part, "x", 0, 0, tiled=True)
    passage_part = jnp.sum(passage_part.astype(f32), axis=0).astype(bf16)
    passage_part = passage_part.reshape(block_rows, yh_size, -1).transpose(1, 0, 2)
    passage_part = lax.all_to_all(passage_part, "yh", 0, 0, tiled=True)
    passage_total = jnp.sum(passage_part.astype(f32), axis=0)
    return loss[None], query_total.astype(bf16)[None], passage_total.astype(bf16)


def solution(mesh):
    blk, qgroup = mesh.devices.shape
    split = Mesh(
        mesh.devices.reshape(YL, blk // (YL * CORES), CORES, X, qgroup // X),
        ("yl", "z", "core", "x", "yh"),
    )
    blk, qgroup = ("yl", "z", "core"), ("x", "yh")
    in_specs = (
        P(qgroup, blk, None),
        P(blk, None),
        P(qgroup, None, blk),
        P(qgroup, blk),
        P(qgroup, blk),
    )
    out_specs = (P(qgroup, blk), P(qgroup, blk, None), P(blk, qgroup))
    return jax.shard_map(per_device, mesh=split, in_specs=in_specs, out_specs=out_specs, check_vma=False)
```

```python
import jax
import jax.numpy as jnp
from jax import lax
from jax.sharding import Mesh, PartitionSpec as P

inv_temp = 50.0
YL, CORES, X = 2, 2, 4
LANES = 128
CHIPS = ("yl", "z")
f32, bf16 = jnp.float32, jnp.bfloat16


def swap_cores(value):
    return lax.ppermute(value, "core", [(0, 1), (1, 0)])


def shift(value, axis, by):
    if by == 0:
        return value
    size = lax.axis_size(axis)
    return lax.ppermute(value, axis, [(i, (i + by) % size) for i in range(size)])


def column_slice(value, axis, which, count):
    width = value.shape[axis] // count
    return lax.dynamic_slice_in_dim(value, which % count * width, width, axis)


def per_device(queries, passages, teacher, teacher_rows, positives):
    own_rows, depth = queries.shape[1:]
    block_rows = passages.shape[0]
    chips = lax.axis_size("yl") * lax.axis_size("z")
    x_size, yh_size = lax.axis_size("x"), lax.axis_size("yh")
    rows = chips * own_rows
    chip = lax.axis_index("yl") * lax.axis_size("z") + lax.axis_index("z")
    core, x, yh = lax.axis_index("core"), lax.axis_index("x"), lax.axis_index("yh")

    indices = jnp.stack(
        [teacher_rows[0], positives[0] // 256, positives[0] % 256], axis=1
    ).astype(bf16)
    sent = jnp.concatenate(
        [queries[0], jnp.pad(indices, ((0, 0), (0, LANES - indices.shape[1])))], axis=1
    )
    passages_other = swap_cores(passages)
    teacher_other = swap_cores(teacher[0])
    gathered = lax.all_to_all(
        jnp.broadcast_to(sent[None], (chips,) + sent.shape), CHIPS, 0, 0, tiled=True
    ).reshape(rows, depth + LANES)
    query = gathered[:, :depth]
    queries_x = [column_slice(query, 1, x + d, x_size) for d in range(x_size)]
    queries_x = [shift(v, "x", d) for d, v in enumerate(queries_x)]
    codes = gathered[:, depth : depth + LANES].astype(f32).T
    row_index = codes[0:1].astype(jnp.int32)
    positive = codes[1:2].astype(jnp.int32) * 256 + codes[2:3].astype(jnp.int32)

    pick = (lax.broadcasted_iota(jnp.int32, (teacher.shape[1], rows), 0) == row_index).astype(f32)

    def columns(block, logits, which):
        scores = inv_temp * lax.dot_general(
            block, query, (((1,), (1,)), ((), ())), preferred_element_type=f32
        )
        picked = lax.dot_general(
            logits, pick, (((0,), (0,)), ((), ())),
            precision=lax.Precision.HIGHEST, preferred_element_type=f32,
        )
        place = (chip * CORES + which) * block_rows
        onehot = lax.broadcasted_iota(jnp.int32, (block_rows, rows), 0) + place == positive
        return scores, picked, onehot

    parts = [columns(passages, teacher[0], core), columns(passages_other, teacher_other, 1 - core)]
    top_student = jnp.maximum(*[jnp.max(s, axis=0, keepdims=True) for s, _, _ in parts])
    top_teacher = jnp.maximum(*[jnp.max(t, axis=0, keepdims=True) for _, t, _ in parts])
    sums = []
    for s, t, hot in parts:
        below_s, below_t = s - top_student, t - top_teacher
        weight = jnp.exp(below_t)
        sums.append(
            [
                jnp.sum(v, axis=0, keepdims=True)
                for v in (jnp.exp(below_s), weight, weight * (below_t - below_s), jnp.where(hot, s, 0.0))
            ]
        )
    sums = [a + b for a, b in zip(*sums)]
    stats = jnp.concatenate([top_student, top_teacher] + sums + [jnp.zeros((2, rows), f32)], axis=0)
    stats = lax.all_to_all(
        jnp.broadcast_to(stats[None], (chips,) + stats.shape), CHIPS, 0, 0, tiled=True
    )
    tops_s, tops_t, sums_s, sums_t, cross, hits = (stats[:, i] for i in range(6))
    top_s, top_t = jnp.max(tops_s, axis=0, keepdims=True), jnp.max(tops_t, axis=0, keepdims=True)
    lower_s, lower_t = tops_s - top_s, tops_t - top_t
    total_s = jnp.sum(jnp.exp(lower_s) * sums_s, axis=0, keepdims=True)
    weight_t = jnp.exp(lower_t)
    total_t = jnp.sum(weight_t * sums_t, axis=0, keepdims=True)
    cross = jnp.sum(weight_t * (cross + (lower_t - lower_s) * sums_t), axis=0, keepdims=True)
    hit = jnp.sum(hits, axis=0, keepdims=True)
    log_s = jnp.log(total_s)
    losses = cross / total_t - jnp.log(total_t) + log_s - (hit - top_s - log_s)
    loss = lax.dynamic_slice_in_dim(losses[0], chip * own_rows, own_rows)

    scale_s, scale_t = 2.0 * inv_temp / total_s, inv_temp / total_t
    grads, grads_other = (
        (jnp.exp(s - top_s) * scale_s - jnp.exp(t - top_t) * scale_t - jnp.where(hot, inv_temp, 0.0)).astype(bf16)
        for s, t, hot in parts
    )
    grads_x = [shift(jnp.concatenate([grads, grads_other]), "x", d) for d in range(x_size)]

    query_part = sum(
        lax.dot_general(a, b, (((0,), (0,)), ((), ())), preferred_element_type=f32)
        for a, b in ((grads, passages), (grads_other, passages_other))
    )
    query_parts = lax.all_to_all(
        query_part.astype(bf16).reshape(chips, own_rows, depth), CHIPS, 0, 0, tiled=True
    )
    query_total = jnp.sum(query_parts.astype(f32), axis=0)

    grads_x, queries_x = jnp.concatenate(grads_x, axis=1), jnp.concatenate(queries_x)
    part_other = jnp.dot(grads_x[block_rows:], queries_x, preferred_element_type=f32).astype(bf16)
    part = jnp.dot(grads_x[:block_rows], queries_x, preferred_element_type=f32)
    part = (part + swap_cores(part_other).astype(f32)).astype(bf16)
    parts = [shift(column_slice(part, 1, yh + d, yh_size), "yh", d) for d in range(yh_size)]
    passage_total = sum(v.astype(f32) for v in parts)
    return loss[None], query_total.astype(bf16)[None], passage_total.astype(bf16)


def solution(mesh):
    blk, qgroup = mesh.devices.shape
    split = Mesh(
        mesh.devices.reshape(YL, blk // (YL * CORES), CORES, X, qgroup // X),
        ("yl", "z", "core", "x", "yh"),
    )
    blk, qgroup = ("yl", "z", "core"), ("x", "yh")
    in_specs = (
        P(qgroup, blk, None),
        P(blk, None),
        P(qgroup, None, blk),
        P(qgroup, blk),
        P(qgroup, blk),
    )
    out_specs = (P(qgroup, blk), P(qgroup, blk, None), P(blk, qgroup))
    return jax.shard_map(per_device, mesh=split, in_specs=in_specs, out_specs=out_specs, check_vma=False)
```

```python
import jax
import jax.numpy as jnp
from jax import lax
from jax.experimental import pallas as pl
from jax.experimental.pallas import tpu as pltpu
from jax.sharding import Mesh, PartitionSpec as P

inv_temp = 50.0
YL, CORES, X = 2, 2, 4
LANES = 128
STATS = 8
CHIPS = ("yl", "z")
f32, bf16, i32 = jnp.float32, jnp.bfloat16, jnp.int32
VMEM = pl.BlockSpec(memory_space=pltpu.VMEM)
SMEM = pl.BlockSpec(memory_space=pltpu.SMEM)
PARAMS = pltpu.CompilerParams(vmem_limit_bytes=40 * 1024 * 1024)


def shift(value, axis, by):
    if by == 0:
        return value
    size = lax.axis_size(axis)
    return lax.ppermute(value, axis, [(i, (i + by) % size) for i in range(size)])


def column_slice(value, which, count):
    width = value.shape[1] // count
    return lax.dynamic_slice_in_dim(value, which % count * width, width, 1)


def in_core_order(own, other, axis):
    first, second = jnp.concatenate([own, other], axis), jnp.concatenate([other, own], axis)
    return jnp.where(lax.axis_index("core") == 0, first, second)


def hits(positive, place, shape):
    return lax.broadcasted_iota(i32, shape, 0) + place == positive


def score_kernel(place, query, passages, teacher, scores, logits, positives, stats):
    depth = passages.shape[1]
    rows = query.shape[0]
    codes = query[:, depth:].astype(f32).T
    row_index = codes[0:1].astype(i32)
    positive = codes[1:2].astype(i32) * 256 + codes[2:3].astype(i32)
    positives[...] = positive
    s = inv_temp * lax.dot_general(
        passages[...], query[:, :depth], (((1,), (1,)), ((), ())), preferred_element_type=f32
    )
    pick = (lax.broadcasted_iota(i32, (teacher.shape[0], rows), 0) == row_index).astype(f32)
    t = lax.dot_general(
        teacher[...], pick, (((0,), (0,)), ((), ())),
        precision=lax.Precision.HIGHEST, preferred_element_type=f32,
    )
    scores[...] = s
    logits[...] = t
    top_s, top_t = jnp.max(s, axis=0, keepdims=True), jnp.max(t, axis=0, keepdims=True)
    below_s, below_t = s - top_s, t - top_t
    weight = jnp.exp(below_t)
    hot = hits(positive, place[0], s.shape)
    sums = [
        jnp.sum(v, axis=0, keepdims=True)
        for v in (jnp.exp(below_s), weight, weight * (below_t - below_s), jnp.where(hot, s, 0.0))
    ]
    whole = jnp.concatenate([top_s, top_t] + sums + [jnp.zeros((STATS - 6, rows), f32)], axis=0)
    stats[...] = jnp.broadcast_to(whole[None], stats.shape)


def grad_kernel(place, scores, logits, positives, stats, grads, sent, losses):
    tops_s, tops_t, sums_s, sums_t, cross, hit = (stats[:, i, :] for i in range(6))
    top_s, top_t = jnp.max(tops_s, axis=0, keepdims=True), jnp.max(tops_t, axis=0, keepdims=True)
    lower_s, lower_t = tops_s - top_s, tops_t - top_t
    total_s = jnp.sum(jnp.exp(lower_s) * sums_s, axis=0, keepdims=True)
    weight_t = jnp.exp(lower_t)
    total_t = jnp.sum(weight_t * sums_t, axis=0, keepdims=True)
    cross = jnp.sum(weight_t * (cross + (lower_t - lower_s) * sums_t), axis=0, keepdims=True)
    log_s = jnp.log(total_s)
    own = jnp.sum(hit, axis=0, keepdims=True)
    losses[...] = cross / total_t - jnp.log(total_t) + log_s - (own - top_s - log_s)
    s, t = scores[...], logits[...]
    hot = hits(positives[...], place[0], s.shape)
    values = (
        jnp.exp(s - top_s) * (2.0 * inv_temp / total_s)
        - jnp.exp(t - top_t) * (inv_temp / total_t)
        - jnp.where(hot, inv_temp, 0.0)
    ).astype(bf16)
    grads[...] = values
    half = values.shape[0] // CORES
    for slot in range(sent.shape[0]):
        sent[slot] = values[slot % CORES * half : (slot % CORES + 1) * half]


def passage_kernel(position, grads, query, query_other, out):
    x, core = position[0], position[1]
    groups = query.shape[0]
    total = jnp.zeros(out.shape[1:], f32)
    for d in range(groups):
        group = lax.rem(x + groups - d, groups) * CORES
        for which, columns in ((core, query), (1 - core, query_other)):
            total += jnp.dot(grads[group + which], columns[d], preferred_element_type=f32)
    out[0] = total.astype(bf16)


def per_device(queries, passages, teacher, teacher_rows, positives):
    own_rows, depth = queries.shape[1:]
    block_rows = passages.shape[0]
    chips = lax.axis_size("yl") * lax.axis_size("z")
    x_size, yh_size = lax.axis_size("x"), lax.axis_size("yh")
    rows, wide = chips * own_rows, CORES * block_rows
    chip = lax.axis_index("yl") * lax.axis_size("z") + lax.axis_index("z")
    core, x, yh = lax.axis_index("core"), lax.axis_index("x"), lax.axis_index("yh")
    place = (chip * wide).astype(i32)[None]

    indices = jnp.stack(
        [teacher_rows[0], positives[0] // 256, positives[0] % 256], axis=1
    ).astype(bf16)
    sent = jnp.concatenate(
        [queries[0], jnp.pad(indices, ((0, 0), (0, LANES - indices.shape[1])))], axis=1
    )
    passages = in_core_order(passages, shift(passages, "core", 1), 0)
    teacher = in_core_order(teacher[0], shift(teacher[0], "core", 1), 1)
    query = lax.all_to_all(
        jnp.broadcast_to(sent[None], (chips,) + sent.shape), CHIPS, 0, 0, tiled=True
    ).reshape(rows, depth + LANES)

    scores, logits, positive, stats = pl.pallas_call(
        score_kernel,
        out_shape=(
            jax.ShapeDtypeStruct((wide, rows), f32),
            jax.ShapeDtypeStruct((wide, rows), f32),
            jax.ShapeDtypeStruct((1, rows), i32),
            jax.ShapeDtypeStruct((chips, STATS, rows), f32),
        ),
        in_specs=[SMEM] + [VMEM] * 3,
        out_specs=(VMEM,) * 4,
        compiler_params=PARAMS,
    )(place, query, passages, teacher)
    columns = [shift(column_slice(query[:, :depth], x + d, x_size), "x", d) for d in range(x_size)]
    stats = lax.all_to_all(stats, CHIPS, 0, 0, tiled=True)
    stats, columns = lax.optimization_barrier((stats, columns))
    columns = jnp.stack(columns)
    columns_other = shift(columns, "core", 1)

    grads, sent, losses = pl.pallas_call(
        grad_kernel,
        out_shape=(
            jax.ShapeDtypeStruct((wide, rows), bf16),
            jax.ShapeDtypeStruct((x_size * CORES, block_rows, rows), bf16),
            jax.ShapeDtypeStruct((1, rows), f32),
        ),
        in_specs=[SMEM] + [VMEM] * 4,
        out_specs=(VMEM,) * 3,
        compiler_params=PARAMS,
    )(place, scores, logits, positive, stats)
    loss = lax.dynamic_slice_in_dim(losses[0], chip * own_rows, own_rows)
    grads_x = lax.all_to_all(sent, ("x", "core"), 0, 0, tiled=True)

    query_part = lax.dot_general(
        grads, passages, (((0,), (0,)), ((), ())), preferred_element_type=f32
    ).astype(bf16)
    grads_x, query_part = lax.optimization_barrier((grads_x, query_part))
    query_parts = lax.all_to_all(query_part.reshape(chips, own_rows, depth), CHIPS, 0, 0, tiled=True)
    query_total = jnp.sum(query_parts.astype(f32), axis=0)

    width = depth // (x_size * yh_size)
    part = pl.pallas_call(
        passage_kernel,
        grid=(yh_size,),
        out_shape=jax.ShapeDtypeStruct((yh_size, block_rows, width), bf16),
        in_specs=[
            SMEM,
            pl.BlockSpec((x_size * CORES, block_rows, rows), lambda i: (0, 0, 0)),
            pl.BlockSpec((x_size, rows, width), lambda i: (0, 0, i)),
            pl.BlockSpec((x_size, rows, width), lambda i: (0, 0, i)),
        ],
        out_specs=pl.BlockSpec((1, block_rows, width), lambda i: (i, 0, 0)),
        compiler_params=PARAMS,
    )(jnp.stack([x, core]).astype(i32), grads_x, columns, columns_other)
    parts = [
        shift(lax.dynamic_index_in_dim(part, (yh + d) % yh_size, 0, False), "yh", d) for d in range(yh_size)
    ]
    passage_total = sum(v.astype(f32) for v in parts)
    return loss[None], query_total.astype(bf16)[None], passage_total.astype(bf16)


def solution(mesh):
    blk, qgroup = mesh.devices.shape
    split = Mesh(
        mesh.devices.reshape(YL, blk // (YL * CORES), CORES, X, qgroup // X),
        ("yl", "z", "core", "x", "yh"),
    )
    blk, qgroup = ("yl", "z", "core"), ("x", "yh")
    in_specs = (
        P(qgroup, blk, None),
        P(blk, None),
        P(qgroup, None, blk),
        P(qgroup, blk),
        P(qgroup, blk),
    )
    out_specs = (P(qgroup, blk), P(qgroup, blk, None), P(blk, qgroup))
    return jax.shard_map(per_device, mesh=split, in_specs=in_specs, out_specs=out_specs, check_vma=False)
```

```python
import functools

import jax
import jax.numpy as jnp
from jax import lax
from jax.experimental import pallas as pl
from jax.experimental.pallas import tpu as pltpu
from jax.sharding import Mesh, PartitionSpec as P

inv_temp = 50.0
YL, CORES, X = 2, 2, 4
LANES = 128
STATS = 8
CHIPS = ("yl", "z")
f32, bf16, i32 = jnp.float32, jnp.bfloat16, jnp.int32
VMEM = pl.BlockSpec(memory_space=pltpu.VMEM)
SMEM = pl.BlockSpec(memory_space=pltpu.SMEM)
PARAMS = pltpu.CompilerParams(vmem_limit_bytes=16 * 1024 * 1024)


def shift(value, axis, by):
    if by == 0:
        return value
    size = lax.axis_size(axis)
    return lax.ppermute(value, axis, [(i, (i + by) % size) for i in range(size)])


def column_slice(value, which, count):
    width = value.shape[1] // count
    return lax.dynamic_slice_in_dim(value, which % count * width, width, 1)


def hits(positive, place, shape):
    return lax.broadcasted_iota(i32, shape, 0) + place == positive


def send_kernel(teacher_rows, positives, queries, out):
    own_rows, depth = queries.shape
    shape = (own_rows, out.shape[2] - depth)
    row, column = lax.broadcasted_iota(i32, shape, 0), lax.broadcasted_iota(i32, shape, 1)
    codes = jnp.zeros(shape, i32)
    for r in range(own_rows):
        positive = positives[0, r]
        for c, code in enumerate((teacher_rows[0, r], lax.shift_right_logical(positive, 8), positive & 255)):
            codes = jnp.where((row == r) & (column == c), code, codes)
    codes = codes.astype(f32).astype(bf16)
    for chip in range(out.shape[0]):
        out[chip, :, :depth] = queries[...]
        out[chip, :, depth:] = codes


def score_kernel(places, query, passages, passages_other, teacher, teacher_other, scores, logits, positives, stats):
    depth = passages.shape[1]
    rows = query.shape[0]
    codes = query[:, depth:].astype(f32).T
    row_index = codes[0:1].astype(i32)
    positive = codes[1:2].astype(i32) * 256 + codes[2:3].astype(i32)
    positives[...] = positive
    pick = (lax.broadcasted_iota(i32, (teacher.shape[0], rows), 0) == row_index).astype(f32)
    parts = []
    for half, (block, table) in enumerate(((passages, teacher), (passages_other, teacher_other))):
        s = inv_temp * lax.dot_general(
            block[...], query[:, :depth], (((1,), (1,)), ((), ())), preferred_element_type=f32
        )
        t = lax.dot_general(
            table[...], pick, (((0,), (0,)), ((), ())),
            precision=lax.Precision.HIGHEST, preferred_element_type=f32,
        )
        scores[half] = s
        logits[half] = t
        parts.append((s, t, hits(positive, places[half], s.shape)))
    top_s, top_t = (jnp.maximum(*[jnp.max(p[i], axis=0, keepdims=True) for p in parts]) for i in (0, 1))
    sums = []
    for s, t, hot in parts:
        below_s, below_t = s - top_s, t - top_t
        weight = jnp.exp(below_t)
        values = (jnp.exp(below_s), weight, weight * (below_t - below_s), jnp.where(hot, s, 0.0))
        sums.append([jnp.sum(v, axis=0, keepdims=True) for v in values])
    sums = [a + b for a, b in zip(*sums)]
    whole = jnp.concatenate([top_s, top_t] + sums + [jnp.zeros((STATS - 6, rows), f32)], axis=0)
    stats[...] = jnp.broadcast_to(whole[None], stats.shape)


def grad_kernel(places, scores, logits, positives, stats, grads, grads_other, losses):
    tops_s, tops_t, sums_s, sums_t, cross, hit = (stats[:, i, :] for i in range(6))
    top_s, top_t = jnp.max(tops_s, axis=0, keepdims=True), jnp.max(tops_t, axis=0, keepdims=True)
    lower_s, lower_t = tops_s - top_s, tops_t - top_t
    total_s = jnp.sum(jnp.exp(lower_s) * sums_s, axis=0, keepdims=True)
    weight_t = jnp.exp(lower_t)
    total_t = jnp.sum(weight_t * sums_t, axis=0, keepdims=True)
    cross = jnp.sum(weight_t * (cross + (lower_t - lower_s) * sums_t), axis=0, keepdims=True)
    log_s = jnp.log(total_s)
    own = jnp.sum(hit, axis=0, keepdims=True)
    losses[...] = cross / total_t - jnp.log(total_t) + log_s - (own - top_s - log_s)
    scale_s, scale_t = 2.0 * inv_temp / total_s, inv_temp / total_t
    for half, out in enumerate((grads, grads_other)):
        hot = hits(positives[...], places[half], out.shape)
        out[...] = (
            jnp.exp(scores[half] - top_s) * scale_s
            - jnp.exp(logits[half] - top_t) * scale_t
            - jnp.where(hot, inv_temp, 0.0)
        ).astype(bf16)


def query_kernel(grads, grads_other, passages, passages_other, out):
    total = 0.0
    for g, p in ((grads, passages), (grads_other, passages_other)):
        total += lax.dot_general(g[...], p[...], (((0,), (0,)), ((), ())), preferred_element_type=f32)
    out[...] = total.astype(bf16)


def passage_kernel(groups, yh, *refs):
    grads, query, query_other = (refs[k * groups : (k + 1) * groups] for k in range(3))
    outs = refs[3 * groups :]
    width = outs[0].shape[1]
    for i, out in enumerate(outs):
        columns = pl.ds(pl.multiple_of(lax.rem(yh[0] + i, len(outs)) * width, width), width)
        total = jnp.zeros(out.shape, f32)
        for g, own, other in zip(grads, query, query_other):
            total += jnp.dot(g[0], own[:, columns], preferred_element_type=f32)
            total += jnp.dot(g[1], other[:, columns], preferred_element_type=f32)
        out[...] = total.astype(bf16)


def per_device(queries, passages, teacher, teacher_rows, positives):
    own_rows, depth = queries.shape[1:]
    block_rows = passages.shape[0]
    chips = lax.axis_size("yl") * lax.axis_size("z")
    x_size, yh_size = lax.axis_size("x"), lax.axis_size("yh")
    rows = chips * own_rows
    chip = lax.axis_index("yl") * lax.axis_size("z") + lax.axis_index("z")
    core, x, yh = lax.axis_index("core"), lax.axis_index("x"), lax.axis_index("yh")
    places = ((chip * CORES + jnp.stack([core, 1 - core])) * block_rows).astype(i32)

    sent = pl.pallas_call(
        send_kernel,
        out_shape=jax.ShapeDtypeStruct((chips, own_rows, depth + LANES), bf16),
        in_specs=[SMEM, SMEM, VMEM],
        out_specs=VMEM,
        compiler_params=PARAMS,
    )(teacher_rows, positives, queries[0])
    passages_other, teacher_other = shift(passages, "core", 1), shift(teacher[0], "core", 1)
    query = lax.all_to_all(sent, CHIPS, 0, 0, tiled=True).reshape(rows, depth + LANES)

    scores, logits, positive, stats = pl.pallas_call(
        score_kernel,
        out_shape=(
            jax.ShapeDtypeStruct((CORES, block_rows, rows), f32),
            jax.ShapeDtypeStruct((CORES, block_rows, rows), f32),
            jax.ShapeDtypeStruct((1, rows), i32),
            jax.ShapeDtypeStruct((chips, STATS, rows), f32),
        ),
        in_specs=[SMEM] + [VMEM] * 5,
        out_specs=(VMEM,) * 4,
        compiler_params=PARAMS,
    )(places, query, passages, passages_other, teacher[0], teacher_other)
    query, stats = lax.optimization_barrier((query, stats))
    columns = [shift(column_slice(query[:, :depth], x + d, x_size), "x", d) for d in range(x_size)]
    stats = lax.all_to_all(stats, CHIPS, 0, 0, tiled=True)
    stats, columns = lax.optimization_barrier((stats, columns))

    grads, grads_other, losses = pl.pallas_call(
        grad_kernel,
        out_shape=(
            jax.ShapeDtypeStruct((block_rows, rows), bf16),
            jax.ShapeDtypeStruct((block_rows, rows), bf16),
            jax.ShapeDtypeStruct((1, rows), f32),
        ),
        in_specs=[SMEM] + [VMEM] * 4,
        out_specs=(VMEM,) * 3,
        compiler_params=PARAMS,
    )(places, scores, logits, positive, stats)
    loss = lax.dynamic_slice_in_dim(losses[0], chip * own_rows, own_rows)

    grads_back = shift(grads_other, "core", 1)
    columns_other = shift(jnp.stack(columns), "core", 1)
    query_part = pl.pallas_call(
        query_kernel,
        out_shape=jax.ShapeDtypeStruct((rows, depth), bf16),
        in_specs=[VMEM] * 4,
        out_specs=VMEM,
        compiler_params=PARAMS,
    )(grads, grads_other, passages, passages_other)
    query_parts = lax.all_to_all(query_part.reshape(chips, own_rows, depth), CHIPS, 0, 0, tiled=True)
    query_total = jnp.sum(query_parts.astype(f32), axis=0)

    block_grads = jnp.stack([grads, grads_back])
    block_grads = [shift(block_grads, "x", d) for d in range(x_size)]
    width = depth // (x_size * yh_size)
    parts = pl.pallas_call(
        functools.partial(passage_kernel, x_size),
        out_shape=(jax.ShapeDtypeStruct((block_rows, width), bf16),) * yh_size,
        in_specs=[SMEM] + [VMEM] * (3 * x_size),
        out_specs=(VMEM,) * yh_size,
        compiler_params=PARAMS,
    )(yh.astype(i32)[None], *block_grads, *columns, *columns_other)
    parts = [shift(part, "yh", d) for d, part in enumerate(parts)]
    passage_total = sum(v.astype(f32) for v in parts)
    return loss[None], query_total.astype(bf16)[None], passage_total.astype(bf16)


def solution(mesh):
    blk, qgroup = mesh.devices.shape
    split = Mesh(
        mesh.devices.reshape(YL, blk // (YL * CORES), CORES, X, qgroup // X),
        ("yl", "z", "core", "x", "yh"),
    )
    blk, qgroup = ("yl", "z", "core"), ("x", "yh")
    in_specs = (
        P(qgroup, blk, None),
        P(blk, None),
        P(qgroup, None, blk),
        P(qgroup, blk),
        P(qgroup, blk),
    )
    out_specs = (P(qgroup, blk), P(qgroup, blk, None), P(blk, qgroup))
    return jax.shard_map(per_device, mesh=split, in_specs=in_specs, out_specs=out_specs, check_vma=False)
```

```python
import functools

import jax
import jax.numpy as jnp
from jax import lax
from jax.experimental import pallas as pl
from jax.experimental.pallas import tpu as pltpu
from jax.sharding import Mesh, PartitionSpec as P

inv_temp = 50.0
YL, CORES, X = 2, 2, 4
LANES = 128
STATS = 8
CHIPS = ("yl", "z")
f32, bf16, i32 = jnp.float32, jnp.bfloat16, jnp.int32
VMEM = pl.BlockSpec(memory_space=pltpu.VMEM)
ANY = pl.BlockSpec(memory_space=pl.ANY)
SMEM = pl.BlockSpec(memory_space=pltpu.SMEM)
PARAMS = pltpu.CompilerParams(vmem_limit_bytes=16 * 1024 * 1024)


def shift(value, axis, by):
    if by == 0:
        return value
    size = lax.axis_size(axis)
    return lax.ppermute(value, axis, [(i, (i + by) % size) for i in range(size)])


def column_slice(value, which, count):
    width = value.shape[1] // count
    return lax.dynamic_slice_in_dim(value, which % count * width, width, 1)


def hits(positive, place, shape):
    return lax.broadcasted_iota(i32, shape, 0) + place == positive


def send_kernel(teacher_rows, positives, queries, out, rows_smem, positives_smem, buffer, sems):
    own_rows, depth = queries.shape
    shape = (own_rows, out.shape[2] - depth)
    loads = [
        pltpu.make_async_copy(teacher_rows, rows_smem, sems.at[0]),
        pltpu.make_async_copy(positives, positives_smem, sems.at[1]),
        pltpu.make_async_copy(queries, buffer.at[:, pl.ds(0, depth)], sems.at[2]),
    ]
    for load in loads:
        load.start()
    for load in loads:
        load.wait()
    row, column = lax.broadcasted_iota(i32, shape, 0), lax.broadcasted_iota(i32, shape, 1)
    codes = jnp.zeros(shape, i32)
    for r in range(own_rows):
        positive = positives_smem[0, r]
        for c, code in enumerate((rows_smem[0, r], lax.shift_right_logical(positive, 8), positive & 255)):
            codes = jnp.where((row == r) & (column == c), code, codes)
    buffer[:, depth:] = codes.astype(f32).astype(bf16)
    stores = [pltpu.make_async_copy(buffer, out.at[chip], sems.at[3 + chip]) for chip in range(out.shape[0])]
    for store in stores:
        store.start()
    for store in stores:
        store.wait()


def score_kernel(places, query, passages, passages_other, teacher, teacher_other, scores, logits, positives, stats):
    depth = passages.shape[1]
    rows = query.shape[0]
    codes = query[:, depth:].astype(f32).T
    row_index = codes[0:1].astype(i32)
    positive = codes[1:2].astype(i32) * 256 + codes[2:3].astype(i32)
    positives[...] = positive
    pick = (lax.broadcasted_iota(i32, (teacher.shape[0], rows), 0) == row_index).astype(f32)
    parts = []
    for half, (block, table) in enumerate(((passages, teacher), (passages_other, teacher_other))):
        s = inv_temp * lax.dot_general(
            block[...], query[:, :depth], (((1,), (1,)), ((), ())), preferred_element_type=f32
        )
        t = lax.dot_general(
            table[...], pick, (((0,), (0,)), ((), ())),
            precision=lax.Precision.HIGHEST, preferred_element_type=f32,
        )
        scores[half] = s
        logits[half] = t
        parts.append((s, t, hits(positive, places[half], s.shape)))
    top_s, top_t = (jnp.maximum(*[jnp.max(p[i], axis=0, keepdims=True) for p in parts]) for i in (0, 1))
    sums = []
    for s, t, hot in parts:
        below_s, below_t = s - top_s, t - top_t
        weight = jnp.exp(below_t)
        values = (jnp.exp(below_s), weight, weight * (below_t - below_s), jnp.where(hot, s, 0.0))
        sums.append([jnp.sum(v, axis=0, keepdims=True) for v in values])
    sums = [a + b for a, b in zip(*sums)]
    whole = jnp.concatenate([top_s, top_t] + sums + [jnp.zeros((STATS - 6, rows), f32)], axis=0)
    stats[...] = jnp.broadcast_to(whole[None], stats.shape)


def grad_kernel(places, scores, logits, positives, stats, grads, grads_other, sent, losses):
    tops_s, tops_t, sums_s, sums_t, cross, hit = (stats[:, i, :] for i in range(6))
    top_s, top_t = jnp.max(tops_s, axis=0, keepdims=True), jnp.max(tops_t, axis=0, keepdims=True)
    lower_s, lower_t = tops_s - top_s, tops_t - top_t
    total_s = jnp.sum(jnp.exp(lower_s) * sums_s, axis=0, keepdims=True)
    weight_t = jnp.exp(lower_t)
    total_t = jnp.sum(weight_t * sums_t, axis=0, keepdims=True)
    cross = jnp.sum(weight_t * (cross + (lower_t - lower_s) * sums_t), axis=0, keepdims=True)
    log_s = jnp.log(total_s)
    own = jnp.sum(hit, axis=0, keepdims=True)
    losses[...] = cross / total_t - jnp.log(total_t) + log_s - (own - top_s - log_s)
    scale_s, scale_t = 2.0 * inv_temp / total_s, inv_temp / total_t
    for half, out in enumerate((grads, grads_other)):
        hot = hits(positives[...], places[half], out.shape)
        values = (
            jnp.exp(scores[half] - top_s) * scale_s
            - jnp.exp(logits[half] - top_t) * scale_t
            - jnp.where(hot, inv_temp, 0.0)
        ).astype(bf16)
        out[...] = values
        which = places[CORES + half]
        for group in range(sent.shape[0] // CORES):
            sent[group * CORES + which] = values


def query_kernel(grads, grads_other, passages, passages_other, out):
    total = 0.0
    for g, p in ((grads, passages), (grads_other, passages_other)):
        total += lax.dot_general(g[...], p[...], (((0,), (0,)), ((), ())), preferred_element_type=f32)
    out[...] = total.astype(bf16)


def passage_kernel(groups, position, grads, *refs):
    x, core, yh = position[0], position[1], position[2]
    query, query_other, outs = refs[:groups], refs[groups], refs[groups + 1 :]
    width = outs[0].shape[1]
    for i, out in enumerate(outs):
        columns = pl.ds(pl.multiple_of(lax.rem(yh + i, len(outs)) * width, width), width)
        total = jnp.zeros(out.shape, f32)
        for d in range(groups):
            group = lax.rem(x + groups - d, groups) * CORES
            total += jnp.dot(grads[group + core], query[d][:, columns], preferred_element_type=f32)
            total += jnp.dot(grads[group + 1 - core], query_other[d, :, columns], preferred_element_type=f32)
        out[...] = total.astype(bf16)


def sum_kernel(parts, out):
    total = parts[0].astype(f32)
    for i in range(1, parts.shape[0]):
        total += parts[i].astype(f32)
    out[...] = total.astype(bf16)


def per_device(queries, passages, teacher, teacher_rows, positives):
    own_rows, depth = queries.shape[1:]
    block_rows = passages.shape[0]
    chips = lax.axis_size("yl") * lax.axis_size("z")
    x_size, yh_size = lax.axis_size("x"), lax.axis_size("yh")
    rows = chips * own_rows
    chip = lax.axis_index("yl") * lax.axis_size("z") + lax.axis_index("z")
    core, x, yh = lax.axis_index("core"), lax.axis_index("x"), lax.axis_index("yh")
    cores = jnp.stack([core, 1 - core])
    places = jnp.concatenate([(chip * CORES + cores) * block_rows, cores]).astype(i32)

    sent = pl.pallas_call(
        send_kernel,
        out_shape=jax.ShapeDtypeStruct((chips, own_rows, depth + LANES), bf16),
        in_specs=[ANY] * 3,
        out_specs=ANY,
        scratch_shapes=[
            pltpu.SMEM((1, own_rows), i32),
            pltpu.SMEM((1, own_rows), i32),
            pltpu.VMEM((own_rows, depth + LANES), bf16),
            pltpu.SemaphoreType.DMA((3 + chips,)),
        ],
        compiler_params=PARAMS,
    )(teacher_rows, positives, queries[0])
    sent, passages, teacher = lax.optimization_barrier((sent, passages, teacher))
    passages_other, teacher_other = shift(passages, "core", 1), shift(teacher[0], "core", 1)
    query = lax.all_to_all(sent, CHIPS, 0, 0, tiled=True).reshape(rows, depth + LANES)

    scores, logits, positive, stats = pl.pallas_call(
        score_kernel,
        out_shape=(
            jax.ShapeDtypeStruct((CORES, block_rows, rows), f32),
            jax.ShapeDtypeStruct((CORES, block_rows, rows), f32),
            jax.ShapeDtypeStruct((1, rows), i32),
            jax.ShapeDtypeStruct((chips, STATS, rows), f32),
        ),
        in_specs=[SMEM] + [VMEM] * 5,
        out_specs=(VMEM,) * 4,
        compiler_params=PARAMS,
    )(places, query, passages, passages_other, teacher[0], teacher_other)
    query, stats = lax.optimization_barrier((query, stats))
    columns = [shift(column_slice(query[:, :depth], x + d, x_size), "x", d) for d in range(x_size)]
    stats = lax.all_to_all(stats, CHIPS, 0, 0, tiled=True)
    columns_other = shift(jnp.stack(columns), "core", 1)
    stats, columns, columns_other = lax.optimization_barrier((stats, columns, columns_other))

    grads, grads_other, sent, losses = pl.pallas_call(
        grad_kernel,
        out_shape=(
            jax.ShapeDtypeStruct((block_rows, rows), bf16),
            jax.ShapeDtypeStruct((block_rows, rows), bf16),
            jax.ShapeDtypeStruct((x_size * CORES, block_rows, rows), bf16),
            jax.ShapeDtypeStruct((1, rows), f32),
        ),
        in_specs=[SMEM] + [VMEM] * 4,
        out_specs=(VMEM,) * 4,
        compiler_params=PARAMS,
    )(places, scores, logits, positive, stats)
    loss = lax.dynamic_slice_in_dim(losses[0], chip * own_rows, own_rows)

    block_grads = lax.all_to_all(sent, ("x", "core"), 0, 0, tiled=True)
    width = depth // x_size
    query_part = pl.pallas_call(
        query_kernel,
        grid=(x_size,),
        out_shape=jax.ShapeDtypeStruct((rows, depth), bf16),
        in_specs=[pl.BlockSpec((block_rows, rows), lambda i: (0, 0))] * 2
        + [pl.BlockSpec((block_rows, width), lambda i: (0, i))] * 2,
        out_specs=pl.BlockSpec((rows, width), lambda i: (0, i)),
        compiler_params=PARAMS,
    )(grads, grads_other, passages, passages_other)
    query_part, block_grads = lax.optimization_barrier((query_part, block_grads))
    query_parts = lax.all_to_all(query_part.reshape(chips, own_rows, depth), CHIPS, 0, 0, tiled=True)
    query_total = pl.pallas_call(
        sum_kernel,
        out_shape=jax.ShapeDtypeStruct((own_rows, depth), bf16),
        in_specs=[VMEM],
        out_specs=VMEM,
        compiler_params=PARAMS,
    )(query_parts)

    parts = pl.pallas_call(
        functools.partial(passage_kernel, x_size),
        out_shape=(jax.ShapeDtypeStruct((block_rows, width // yh_size), bf16),) * yh_size,
        in_specs=[SMEM] + [VMEM] * (2 + x_size),
        out_specs=(VMEM,) * yh_size,
        compiler_params=PARAMS,
    )(jnp.stack([x, core, yh]).astype(i32), block_grads, *columns, columns_other)
    parts = [shift(part, "yh", d) for d, part in enumerate(parts)]
    passage_total = sum(v.astype(f32) for v in parts)
    return loss[None], query_total[None], passage_total.astype(bf16)


def solution(mesh):
    blk, qgroup = mesh.devices.shape
    split = Mesh(
        mesh.devices.reshape(YL, blk // (YL * CORES), CORES, X, qgroup // X),
        ("yl", "z", "core", "x", "yh"),
    )
    blk, qgroup = ("yl", "z", "core"), ("x", "yh")
    in_specs = (
        P(qgroup, blk, None),
        P(blk, None),
        P(qgroup, None, blk),
        P(qgroup, blk),
        P(qgroup, blk),
    )
    out_specs = (P(qgroup, blk), P(qgroup, blk, None), P(blk, qgroup))
    return jax.shard_map(per_device, mesh=split, in_specs=in_specs, out_specs=out_specs, check_vma=False)
```

```python
import functools

import jax
import jax.numpy as jnp
from jax import lax
from jax.experimental import pallas as pl
from jax.experimental.pallas import tpu as pltpu
from jax.sharding import Mesh, PartitionSpec as P

inv_temp = 50.0
YL, CORES, X = 2, 2, 4
LANES = 128
STATS = 24
CHIPS = ("yl", "z")
f32, bf16, i32 = jnp.float32, jnp.bfloat16, jnp.int32
VMEM = pl.BlockSpec(memory_space=pltpu.VMEM)
ANY = pl.BlockSpec(memory_space=pl.ANY)
HBM = pl.BlockSpec(memory_space=pltpu.HBM)
SMEM = pl.BlockSpec(memory_space=pltpu.SMEM)
PARAMS = pltpu.CompilerParams(vmem_limit_bytes=16 * 1024 * 1024)


def shift(value, axis, by):
    if by == 0:
        return value
    size = lax.axis_size(axis)
    return lax.ppermute(value, axis, [(i, (i + by) % size) for i in range(size)])


def hits(positive, place, shape):
    return lax.broadcasted_iota(i32, shape, 0) + place == positive


def send_kernel(indices, queries, out, numbers, buffer, sems):
    own_rows, depth = queries.shape
    shape = (own_rows, out.shape[2] - depth)
    loads = [
        pltpu.make_async_copy(indices, numbers, sems.at[0]),
        pltpu.make_async_copy(queries, buffer.at[:, pl.ds(0, depth)], sems.at[1]),
    ]
    for load in loads:
        load.start()
    for load in loads:
        load.wait()
    row, column = lax.broadcasted_iota(i32, shape, 0), lax.broadcasted_iota(i32, shape, 1)
    codes = jnp.zeros(shape, i32)
    for r in range(own_rows):
        for c in range(3):
            code = lax.shift_right_logical(numbers[0, r], 8 * c) & 255
            codes = jnp.where((row == r) & (column == c), code, codes)
    buffer[:, depth:] = codes.astype(f32).astype(bf16)
    stores = [pltpu.make_async_copy(buffer, out.at[chip], sems.at[2 + chip]) for chip in range(out.shape[0])]
    for store in stores:
        store.start()
    for store in stores:
        store.wait()


def score_kernel(
    places, query, passages, teacher, teacher_other, passages_other, values, positives, stats, block, sem
):
    fetch = pltpu.make_async_copy(passages_other, block, sem)
    fetch.start()
    depth = passages.shape[1]
    rows = query.shape[0]
    codes = query[:, depth:].astype(f32).T
    row_index = codes[0:1].astype(i32)
    positive = codes[1:2].astype(i32) + 256 * codes[2:3].astype(i32)
    positives[...] = positive
    pick = (lax.broadcasted_iota(i32, (teacher.shape[0], rows), 0) == row_index).astype(f32)
    parts = []
    for half, table in enumerate((teacher, teacher_other)):
        if half:
            fetch.wait()
        s = inv_temp * lax.dot_general(
            (block if half else passages)[...], query[:, :depth], (((1,), (1,)), ((), ())), preferred_element_type=f32
        )
        t = lax.dot_general(
            table[...], pick, (((0,), (0,)), ((), ())),
            precision=lax.Precision.HIGHEST, preferred_element_type=f32,
        )
        values[half] = s
        values[CORES + half] = t
        parts.append((s, t, hits(positive, places[half], s.shape)))
    top_s, top_t = (jnp.maximum(*[jnp.max(p[i], axis=0, keepdims=True) for p in parts]) for i in (0, 1))
    sums = []
    for s, t, hot in parts:
        below_s, below_t = s - top_s, t - top_t
        weight = jnp.exp(below_t)
        terms = (jnp.exp(below_s), weight, weight * (below_t - below_s), jnp.where(hot, s, 0.0))
        sums.append([jnp.sum(v, axis=0, keepdims=True) for v in terms])
    sums = [a + b for a, b in zip(*sums)]
    whole = jnp.concatenate([top_s, top_t] + sums + [jnp.zeros((STATS - 6, rows), f32)], axis=0)
    stats[...] = jnp.broadcast_to(whole[None], stats.shape)


def slice_kernel(x, query, after, *outs):
    del after
    width = outs[0].shape[1]
    for d, out in enumerate(outs):
        out[...] = query[:, pl.ds(pl.multiple_of(lax.rem(x[0] + d, len(outs)) * width, width), width)]


def grad_kernel(places, logits, positives, stats, grads, sent, losses, buffer, sems):
    tops_s, tops_t, sums_s, sums_t, cross, hit = (stats[:, i, :] for i in range(6))
    top_s, top_t = jnp.max(tops_s, axis=0, keepdims=True), jnp.max(tops_t, axis=0, keepdims=True)
    lower_s, lower_t = tops_s - top_s, tops_t - top_t
    total_s = jnp.sum(jnp.exp(lower_s) * sums_s, axis=0, keepdims=True)
    weight_t = jnp.exp(lower_t)
    total_t = jnp.sum(weight_t * sums_t, axis=0, keepdims=True)
    cross = jnp.sum(weight_t * (cross + (lower_t - lower_s) * sums_t), axis=0, keepdims=True)
    log_s = jnp.log(total_s)
    own = jnp.sum(hit, axis=0, keepdims=True)
    losses[...] = cross / total_t - jnp.log(total_t) + log_s - (own - top_s - log_s)
    scale_s, scale_t = 2.0 * inv_temp / total_s, inv_temp / total_t
    for half in range(CORES):
        hot = hits(positives[...], places[half], logits.shape[1:])
        values = (
            jnp.exp(logits[half] - top_s) * scale_s
            - jnp.exp(logits[CORES + half] - top_t) * scale_t
            - jnp.where(hot, inv_temp, 0.0)
        )
        grads[half] = values.T.astype(bf16)
        buffer[places[CORES + half]] = values.astype(bf16)
    stores = [
        pltpu.make_async_copy(buffer, sent.at[pl.ds(group * CORES, CORES)], sems.at[group])
        for group in range(sent.shape[0] // CORES)
    ]
    for store in stores:
        store.start()
    for store in stores:
        store.wait()


def query_kernel(grads, passages, passages_other, out):
    total = jnp.dot(grads[0], passages[...], preferred_element_type=f32)
    total += jnp.dot(grads[1], passages_other[...], preferred_element_type=f32)
    out[...] = total.astype(bf16)


def passage_kernel(groups, position, grads, *refs):
    x, core, yh = position[0], position[1], position[2]
    query, query_other, outs = refs[:groups], refs[groups], refs[groups + 1 :]
    width = outs[0].shape[1]
    for i, out in enumerate(outs):
        columns = pl.ds(pl.multiple_of(lax.rem(yh + i, len(outs)) * width, width), width)
        total = jnp.zeros(out.shape, f32)
        for d in range(groups):
            group = lax.rem(x + groups - d, groups) * CORES
            total += jnp.dot(grads[group + core], query[d][:, columns], preferred_element_type=f32)
            total += jnp.dot(grads[group + 1 - core], query_other[d, :, columns], preferred_element_type=f32)
        out[...] = total.astype(bf16)


def sum_kernel(parts, out):
    total = parts[0].astype(f32)
    for i in range(1, parts.shape[0]):
        total += parts[i].astype(f32)
    out[...] = total.astype(bf16)


def per_device(queries, passages, teacher, teacher_rows, positives):
    own_rows, depth = queries.shape[1:]
    block_rows = passages.shape[0]
    chips = lax.axis_size("yl") * lax.axis_size("z")
    x_size, yh_size = lax.axis_size("x"), lax.axis_size("yh")
    rows = chips * own_rows
    chip = lax.axis_index("yl") * lax.axis_size("z") + lax.axis_index("z")
    core, x, yh = lax.axis_index("core"), lax.axis_index("x"), lax.axis_index("yh")
    cores = jnp.stack([core, 1 - core])
    places = jnp.concatenate([(chip * CORES + cores) * block_rows, cores]).astype(i32)

    sent = pl.pallas_call(
        send_kernel,
        out_shape=jax.ShapeDtypeStruct((chips, own_rows, depth + LANES), bf16),
        in_specs=[HBM] * 2,
        out_specs=HBM,
        scratch_shapes=[
            pltpu.SMEM((1, own_rows), i32),
            pltpu.VMEM((own_rows, depth + LANES), bf16),
            pltpu.SemaphoreType.DMA((2 + chips,)),
        ],
        compiler_params=PARAMS,
    )(teacher_rows + 256 * positives, queries[0])
    passages_other, teacher_other = shift(passages, "core", 1), shift(teacher[0], "core", 1)
    query = lax.all_to_all(sent, CHIPS, 0, 0, tiled=True).reshape(rows, depth + LANES)

    logits, positive, stats = pl.pallas_call(
        score_kernel,
        out_shape=(
            jax.ShapeDtypeStruct((2 * CORES, block_rows, rows), f32),
            jax.ShapeDtypeStruct((1, rows), i32),
            jax.ShapeDtypeStruct((chips, STATS, rows), f32),
        ),
        in_specs=[SMEM] + [VMEM] * 4 + [ANY],
        out_specs=(VMEM,) * 3,
        scratch_shapes=[pltpu.VMEM((block_rows, depth), bf16), pltpu.SemaphoreType.DMA],
        compiler_params=PARAMS,
    )(places, query, passages, teacher[0], teacher_other, passages_other)
    slices = pl.pallas_call(
        slice_kernel,
        out_shape=(jax.ShapeDtypeStruct((rows, depth // x_size), bf16),) * x_size,
        in_specs=[SMEM, VMEM, VMEM],
        out_specs=(VMEM,) * x_size,
        compiler_params=PARAMS,
    )(x.astype(i32)[None], query, positive)
    columns = [shift(value, "x", d) for d, value in enumerate(slices)]
    stats = lax.all_to_all(stats, CHIPS, 0, 0, tiled=True)
    stats, columns = lax.optimization_barrier((stats, columns))
    columns_other = shift(jnp.stack(columns), "core", 1)

    grads, sent, losses = pl.pallas_call(
        grad_kernel,
        out_shape=(
            jax.ShapeDtypeStruct((CORES, rows, block_rows), bf16),
            jax.ShapeDtypeStruct((x_size * CORES, block_rows, rows), bf16),
            jax.ShapeDtypeStruct((1, rows), f32),
        ),
        in_specs=[SMEM] + [VMEM] * 3,
        out_specs=(VMEM, HBM, VMEM),
        scratch_shapes=[pltpu.VMEM((CORES, block_rows, rows), bf16), pltpu.SemaphoreType.DMA((x_size,))],
        compiler_params=PARAMS,
    )(places, logits, positive, stats)
    loss = lax.dynamic_slice_in_dim(losses[0], chip * own_rows, own_rows)

    block_grads = lax.all_to_all(sent, ("x", "core"), 0, 0, tiled=True)
    width = depth // x_size
    query_part = pl.pallas_call(
        query_kernel,
        grid=(x_size,),
        out_shape=jax.ShapeDtypeStruct((rows, depth), bf16),
        in_specs=[pl.BlockSpec((CORES, rows, block_rows), lambda i: (0, 0, 0))]
        + [pl.BlockSpec((block_rows, width), lambda i: (0, i))] * 2,
        out_specs=pl.BlockSpec((rows, width), lambda i: (0, i)),
        compiler_params=PARAMS,
    )(grads, passages, passages_other)
    query_part, block_grads, columns_other = lax.optimization_barrier((query_part, block_grads, columns_other))
    query_parts = lax.all_to_all(query_part.reshape(chips, own_rows, depth), CHIPS, 0, 0, tiled=True)
    query_total = pl.pallas_call(
        sum_kernel,
        out_shape=jax.ShapeDtypeStruct((own_rows, depth), bf16),
        in_specs=[VMEM],
        out_specs=VMEM,
        compiler_params=PARAMS,
    )(query_parts)

    parts = pl.pallas_call(
        functools.partial(passage_kernel, x_size),
        out_shape=(jax.ShapeDtypeStruct((block_rows, width // yh_size), bf16),) * yh_size,
        in_specs=[SMEM] + [VMEM] * (2 + x_size),
        out_specs=(VMEM,) * yh_size,
        compiler_params=PARAMS,
    )(jnp.stack([x, core, yh]).astype(i32), block_grads, *columns, columns_other)
    parts = [shift(part, "yh", d) for d, part in enumerate(parts)]
    passage_total = sum(v.astype(f32) for v in parts)
    return loss[None], query_total[None], passage_total.astype(bf16)


def solution(mesh):
    blk, qgroup = mesh.devices.shape
    split = Mesh(
        mesh.devices.reshape(YL, blk // (YL * CORES), CORES, X, qgroup // X),
        ("yl", "z", "core", "x", "yh"),
    )
    blk, qgroup = ("yl", "z", "core"), ("x", "yh")
    in_specs = (
        P(qgroup, blk, None),
        P(blk, None),
        P(qgroup, None, blk),
        P(qgroup, blk),
        P(qgroup, blk),
    )
    out_specs = (P(qgroup, blk), P(qgroup, blk, None), P(blk, qgroup))
    return jax.shard_map(per_device, mesh=split, in_specs=in_specs, out_specs=out_specs, check_vma=False)
```

```python
import functools

import jax
import jax.numpy as jnp
from jax import lax
from jax.experimental import pallas as pl
from jax.experimental.pallas import tpu as pltpu
from jax.sharding import Mesh, PartitionSpec as P

inv_temp = 50.0
YL, CORES, X = 2, 2, 4
LANES = 128
STATS = 8
CHIPS = ("yl", "z")
f32, bf16, i32 = jnp.float32, jnp.bfloat16, jnp.int32
VMEM = pl.BlockSpec(memory_space=pltpu.VMEM)
ANY = pl.BlockSpec(memory_space=pl.ANY)
SMEM = pl.BlockSpec(memory_space=pltpu.SMEM)
PARAMS = pltpu.CompilerParams(vmem_limit_bytes=16 * 1024 * 1024)


def shift(value, axis, by):
    if by == 0:
        return value
    size = lax.axis_size(axis)
    return lax.ppermute(value, axis, [(i, (i + by) % size) for i in range(size)])


def hits(positive, place, shape):
    return lax.broadcasted_iota(i32, shape, 0) + place == positive


def score_kernel(places, query, passages, passages_other, teacher, teacher_other, values, positives, stats):
    depth = passages.shape[1]
    rows = query.shape[0]
    codes = query[:, depth:].astype(f32).T
    row_index = codes[0:1].astype(i32)
    positive = codes[1:2].astype(i32) + 256 * codes[2:3].astype(i32)
    positives[...] = positive
    pick = (lax.broadcasted_iota(i32, (teacher.shape[0], rows), 0) == row_index).astype(f32)
    parts = []
    for half, (block, table) in enumerate(((passages, teacher), (passages_other, teacher_other))):
        s = inv_temp * lax.dot_general(
            block[...], query[:, :depth], (((1,), (1,)), ((), ())), preferred_element_type=f32
        )
        t = lax.dot_general(
            table[...], pick, (((0,), (0,)), ((), ())),
            precision=lax.Precision.HIGHEST, preferred_element_type=f32,
        )
        values[half] = s
        values[CORES + half] = t
        parts.append((s, t, hits(positive, places[half], s.shape)))
    top_s, top_t = (jnp.maximum(*[jnp.max(p[i], axis=0, keepdims=True) for p in parts]) for i in (0, 1))
    sums = []
    for s, t, hot in parts:
        below_s, below_t = s - top_s, t - top_t
        weight = jnp.exp(below_t)
        terms = (jnp.exp(below_s), weight, weight * (below_t - below_s), jnp.where(hot, s, 0.0))
        sums.append([jnp.sum(v, axis=0, keepdims=True) for v in terms])
    sums = [a + b for a, b in zip(*sums)]
    whole = jnp.concatenate([top_s, top_t] + sums + [jnp.zeros((STATS - 6, rows), f32)], axis=0)
    stats[...] = jnp.broadcast_to(whole[None], stats.shape)


def slice_kernel(x, query, after, *outs):
    del after
    width = outs[0].shape[1]
    for d, out in enumerate(outs):
        out[...] = query[:, pl.ds(pl.multiple_of(lax.rem(x[0] + d, len(outs)) * width, width), width)]


def grad_kernel(places, logits, positives, stats, rows_first, grads, grads_other, losses):
    tops_s, tops_t, sums_s, sums_t, cross, hit = (stats[:, i, :] for i in range(6))
    top_s, top_t = jnp.max(tops_s, axis=0, keepdims=True), jnp.max(tops_t, axis=0, keepdims=True)
    lower_s, lower_t = tops_s - top_s, tops_t - top_t
    total_s = jnp.sum(jnp.exp(lower_s) * sums_s, axis=0, keepdims=True)
    weight_t = jnp.exp(lower_t)
    total_t = jnp.sum(weight_t * sums_t, axis=0, keepdims=True)
    cross = jnp.sum(weight_t * (cross + (lower_t - lower_s) * sums_t), axis=0, keepdims=True)
    log_s = jnp.log(total_s)
    own = jnp.sum(hit, axis=0, keepdims=True)
    losses[...] = cross / total_t - jnp.log(total_t) + log_s - (own - top_s - log_s)
    scale_s, scale_t = 2.0 * inv_temp / total_s, inv_temp / total_t
    for half, out in enumerate((grads, grads_other)):
        hot = hits(positives[...], places[half], out.shape)
        values = (
            jnp.exp(logits[half] - top_s) * scale_s
            - jnp.exp(logits[CORES + half] - top_t) * scale_t
            - jnp.where(hot, inv_temp, 0.0)
        )
        rows_first[half] = values.T.astype(bf16)
        out[...] = values.astype(bf16)


def query_kernel(grads, passages, passages_other, out):
    total = jnp.dot(grads[0], passages[...], preferred_element_type=f32)
    total += jnp.dot(grads[1], passages_other[...], preferred_element_type=f32)
    out[...] = total.astype(bf16)


def passage_kernel(groups, *refs):
    grads, query, query_other, out = refs[:groups], refs[groups : 2 * groups], refs[2 * groups], refs[-1]
    width = out.shape[2]
    for yh in range(out.shape[0]):
        columns = slice(yh * width, (yh + 1) * width)
        total = jnp.zeros(out.shape[1:], f32)
        for d in range(groups):
            total += jnp.dot(grads[d][0], query[d][:, columns], preferred_element_type=f32)
            total += jnp.dot(grads[d][1], query_other[d, :, columns], preferred_element_type=f32)
        out[yh] = total.astype(bf16)


def sum_kernel(parts, out):
    total = parts[0].astype(f32)
    for i in range(1, parts.shape[0]):
        total += parts[i].astype(f32)
    out[...] = total.astype(bf16)


def per_device(queries, passages, teacher, teacher_rows, positives):
    own_rows, depth = queries.shape[1:]
    block_rows = passages.shape[0]
    chips = lax.axis_size("yl") * lax.axis_size("z")
    x_size, yh_size = lax.axis_size("x"), lax.axis_size("yh")
    rows = chips * own_rows
    chip = lax.axis_index("yl") * lax.axis_size("z") + lax.axis_index("z")
    core, x, yh = lax.axis_index("core"), lax.axis_index("x"), lax.axis_index("yh")
    cores = jnp.stack([core, 1 - core])
    places = jnp.concatenate([(chip * CORES + cores) * block_rows, cores]).astype(i32)

    indices = jnp.stack(
        [teacher_rows[0], positives[0] % 256, positives[0] // 256], axis=1
    ).astype(bf16)
    sent = jnp.concatenate(
        [queries[0], jnp.pad(indices, ((0, 0), (0, LANES - indices.shape[1])))], axis=1
    )
    passages_other, teacher_other = shift(passages, "core", 1), shift(teacher[0], "core", 1)
    query = lax.all_to_all(
        jnp.broadcast_to(sent[None], (chips,) + sent.shape), CHIPS, 0, 0, tiled=True
    ).reshape(rows, depth + LANES)

    logits, positive, stats = pl.pallas_call(
        score_kernel,
        out_shape=(
            jax.ShapeDtypeStruct((2 * CORES, block_rows, rows), f32),
            jax.ShapeDtypeStruct((1, rows), i32),
            jax.ShapeDtypeStruct((chips, STATS, rows), f32),
        ),
        in_specs=[SMEM] + [VMEM] * 5,
        out_specs=(VMEM,) * 3,
        compiler_params=PARAMS,
    )(places, query, passages, passages_other, teacher[0], teacher_other)
    stats = lax.all_to_all(stats, CHIPS, 0, 0, tiled=True)
    rows_first, grads, grads_other, losses = pl.pallas_call(
        grad_kernel,
        out_shape=(
            jax.ShapeDtypeStruct((CORES, rows, block_rows), bf16),
            jax.ShapeDtypeStruct((block_rows, rows), bf16),
            jax.ShapeDtypeStruct((block_rows, rows), bf16),
            jax.ShapeDtypeStruct((1, rows), f32),
        ),
        in_specs=[SMEM] + [VMEM] * 3,
        out_specs=(VMEM,) * 4,
        compiler_params=PARAMS,
    )(places, logits, positive, stats)
    loss = lax.dynamic_slice_in_dim(losses[0], chip * own_rows, own_rows)

    width = depth // x_size
    query_part = pl.pallas_call(
        query_kernel,
        grid=(x_size,),
        out_shape=jax.ShapeDtypeStruct((rows, depth), bf16),
        in_specs=[pl.BlockSpec((CORES, rows, block_rows), lambda i: (0, 0, 0))]
        + [pl.BlockSpec((block_rows, width), lambda i: (0, i))] * 2,
        out_specs=pl.BlockSpec((rows, width), lambda i: (0, i)),
        compiler_params=PARAMS,
    )(rows_first, passages, passages_other)
    query_part, grads_back = lax.optimization_barrier((query_part, shift(grads_other, "core", 1)))
    query_parts = lax.all_to_all(query_part.reshape(chips, own_rows, depth), CHIPS, 0, 0, tiled=True)

    slices = pl.pallas_call(
        slice_kernel,
        out_shape=(jax.ShapeDtypeStruct((rows, width), bf16),) * x_size,
        in_specs=[SMEM, VMEM, ANY],
        out_specs=(VMEM,) * x_size,
        compiler_params=PARAMS,
    )(x.astype(i32)[None], query, query_part)
    columns = [shift(value, "x", d) for d, value in enumerate(slices)]
    block_grads = jnp.stack([grads, grads_back])
    block_grads = [shift(block_grads, "x", d) for d in range(x_size)]
    columns, block_grads = lax.optimization_barrier((columns, block_grads))
    columns_other = shift(jnp.stack(columns), "core", 1)
    part = pl.pallas_call(
        functools.partial(passage_kernel, x_size),
        out_shape=jax.ShapeDtypeStruct((yh_size, block_rows, width // yh_size), bf16),
        in_specs=[VMEM] * (2 * x_size + 1),
        out_specs=VMEM,
        compiler_params=PARAMS,
    )(*block_grads, *columns, columns_other)
    query_parts, part = lax.optimization_barrier((query_parts, part))
    part = lax.all_to_all(part, "yh", 0, 0, tiled=True)
    query_total, passage_total = (
        pl.pallas_call(
            sum_kernel,
            out_shape=jax.ShapeDtypeStruct(value.shape[1:], bf16),
            in_specs=[VMEM],
            out_specs=VMEM,
            compiler_params=PARAMS,
        )(value)
        for value in (query_parts, part)
    )
    return loss[None], query_total[None], passage_total


def solution(mesh):
    blk, qgroup = mesh.devices.shape
    split = Mesh(
        mesh.devices.reshape(YL, blk // (YL * CORES), CORES, X, qgroup // X),
        ("yl", "z", "core", "x", "yh"),
    )
    blk, qgroup = ("yl", "z", "core"), ("x", "yh")
    in_specs = (
        P(qgroup, blk, None),
        P(blk, None),
        P(qgroup, None, blk),
        P(qgroup, blk),
        P(qgroup, blk),
    )
    out_specs = (P(qgroup, blk), P(qgroup, blk, None), P(blk, qgroup))
    return jax.shard_map(per_device, mesh=split, in_specs=in_specs, out_specs=out_specs, check_vma=False)
```

```python
import functools

import jax
import jax.numpy as jnp
from jax import lax
from jax.experimental import pallas as pl
from jax.experimental.pallas import tpu as pltpu
from jax.sharding import Mesh, PartitionSpec as P

inv_temp = 50.0
YL, CORES, X = 2, 2, 4
LANES = 128
STATS = 8
CHIPS = ("yl", "z")
f32, bf16, i32 = jnp.float32, jnp.bfloat16, jnp.int32
VMEM = pl.BlockSpec(memory_space=pltpu.VMEM)
ANY = pl.BlockSpec(memory_space=pl.ANY)
SMEM = pl.BlockSpec(memory_space=pltpu.SMEM)
PARAMS = pltpu.CompilerParams(vmem_limit_bytes=16 * 1024 * 1024)


def shift(value, axis, by):
    if by == 0:
        return value
    size = lax.axis_size(axis)
    return lax.ppermute(value, axis, [(i, (i + by) % size) for i in range(size)])


def hits(positive, place, shape):
    return lax.broadcasted_iota(i32, shape, 0) + place == positive


def score_kernel(places, query, passages, passages_other, teacher, teacher_other, values, positives, stats):
    depth = passages.shape[1]
    rows = query.shape[0]
    codes = query[:, depth:].astype(f32).T
    row_index = codes[0:1].astype(i32)
    positive = codes[1:2].astype(i32) + 256 * codes[2:3].astype(i32)
    positives[...] = positive
    pick = (lax.broadcasted_iota(i32, (teacher.shape[0], rows), 0) == row_index).astype(f32)
    parts = []
    for half, (block, table) in enumerate(((passages, teacher), (passages_other, teacher_other))):
        s = inv_temp * lax.dot_general(
            block[...], query[:, :depth], (((1,), (1,)), ((), ())), preferred_element_type=f32
        )
        t = lax.dot_general(
            table[...], pick, (((0,), (0,)), ((), ())),
            precision=lax.Precision.HIGHEST, preferred_element_type=f32,
        )
        values[half] = s
        values[CORES + half] = t
        parts.append((s, t, hits(positive, places[half], s.shape)))
    top_s, top_t = (jnp.maximum(*[jnp.max(p[i], axis=0, keepdims=True) for p in parts]) for i in (0, 1))
    sums = []
    for s, t, hot in parts:
        below_s, below_t = s - top_s, t - top_t
        weight = jnp.exp(below_t)
        terms = (jnp.exp(below_s), weight, weight * (below_t - below_s), jnp.where(hot, s, 0.0))
        sums.append([jnp.sum(v, axis=0, keepdims=True) for v in terms])
    sums = [a + b for a, b in zip(*sums)]
    whole = jnp.concatenate([top_s, top_t] + sums + [jnp.zeros((STATS - 6, rows), f32)], axis=0)
    stats[...] = jnp.broadcast_to(whole[None], stats.shape)


def pack_kernel(x, query, grads, after, *outs):
    del after
    rows = query.shape[0]
    width = outs[0].shape[1]
    tall = outs[0].shape[0] - rows
    for d, out in enumerate(outs):
        out[:rows] = query[:, pl.ds(pl.multiple_of(lax.rem(x[0] + d, len(outs)) * width, width), width)]
        for k in range(width // rows):
            out[rows:, k * rows : (k + 1) * rows] = grads[k * tall : (k + 1) * tall]


def grad_kernel(places, logits, positives, stats, rows_first, grads, losses):
    tops_s, tops_t, sums_s, sums_t, cross, hit = (stats[:, i, :] for i in range(6))
    top_s, top_t = jnp.max(tops_s, axis=0, keepdims=True), jnp.max(tops_t, axis=0, keepdims=True)
    lower_s, lower_t = tops_s - top_s, tops_t - top_t
    total_s = jnp.sum(jnp.exp(lower_s) * sums_s, axis=0, keepdims=True)
    weight_t = jnp.exp(lower_t)
    total_t = jnp.sum(weight_t * sums_t, axis=0, keepdims=True)
    cross = jnp.sum(weight_t * (cross + (lower_t - lower_s) * sums_t), axis=0, keepdims=True)
    log_s = jnp.log(total_s)
    own = jnp.sum(hit, axis=0, keepdims=True)
    losses[...] = cross / total_t - jnp.log(total_t) + log_s - (own - top_s - log_s)
    scale_s, scale_t = 2.0 * inv_temp / total_s, inv_temp / total_t
    block_rows = logits.shape[1]
    for half in range(CORES):
        hot = hits(positives[...], places[half], logits.shape[1:])
        values = (
            jnp.exp(logits[half] - top_s) * scale_s
            - jnp.exp(logits[CORES + half] - top_t) * scale_t
            - jnp.where(hot, inv_temp, 0.0)
        )
        rows_first[half] = values.T.astype(bf16)
        grads[half * block_rows : (half + 1) * block_rows] = values.astype(bf16)


def query_kernel(grads, passages, passages_other, out):
    total = jnp.dot(grads[0], passages[...], preferred_element_type=f32)
    total += jnp.dot(grads[1], passages_other[...], preferred_element_type=f32)
    out[...] = total.astype(bf16)


def products(packed, half, block_rows, rows):
    tall = packed[0].shape[0] - rows
    total = 0.0
    for ref in packed:
        steps = block_rows // tall
        grads = jnp.concatenate(
            [ref[rows:, k * rows : (k + 1) * rows] for k in range(half * steps, (half + 1) * steps)], axis=0
        )
        total += jnp.dot(grads, ref[:rows], preferred_element_type=f32)
    return total


def other_kernel(rows, *refs):
    out = refs[-1]
    out[...] = products(refs[:-1], 1, out.shape[0], rows).astype(bf16)


def own_kernel(rows, *refs):
    back, out = refs[-2], refs[-1]
    width = out.shape[2]
    total = (products(refs[:-2], 0, back.shape[0], rows) + back[...].astype(f32)).astype(bf16)
    for yh in range(out.shape[0]):
        out[yh] = total[:, yh * width : (yh + 1) * width]


def sum_kernel(parts, out):
    total = parts[0].astype(f32)
    for i in range(1, parts.shape[0]):
        total += parts[i].astype(f32)
    out[...] = total.astype(bf16)


def per_device(queries, passages, teacher, teacher_rows, positives):
    own_rows, depth = queries.shape[1:]
    block_rows = passages.shape[0]
    chips = lax.axis_size("yl") * lax.axis_size("z")
    x_size, yh_size = lax.axis_size("x"), lax.axis_size("yh")
    rows, wide = chips * own_rows, CORES * block_rows
    chip = lax.axis_index("yl") * lax.axis_size("z") + lax.axis_index("z")
    core, x, yh = lax.axis_index("core"), lax.axis_index("x"), lax.axis_index("yh")
    cores = jnp.stack([core, 1 - core])
    places = jnp.concatenate([(chip * CORES + cores) * block_rows, cores]).astype(i32)

    indices = jnp.stack(
        [teacher_rows[0], positives[0] % 256, positives[0] // 256], axis=1
    ).astype(bf16)
    sent = jnp.concatenate(
        [queries[0], jnp.pad(indices, ((0, 0), (0, LANES - indices.shape[1])))], axis=1
    )
    passages_other, teacher_other = shift(passages, "core", 1), shift(teacher[0], "core", 1)
    query = lax.all_to_all(
        jnp.broadcast_to(sent[None], (chips,) + sent.shape), CHIPS, 0, 0, tiled=True
    ).reshape(rows, depth + LANES)

    logits, positive, stats = pl.pallas_call(
        score_kernel,
        out_shape=(
            jax.ShapeDtypeStruct((2 * CORES, block_rows, rows), f32),
            jax.ShapeDtypeStruct((1, rows), i32),
            jax.ShapeDtypeStruct((chips, STATS, rows), f32),
        ),
        in_specs=[SMEM] + [VMEM] * 5,
        out_specs=(VMEM,) * 3,
        compiler_params=PARAMS,
    )(places, query, passages, passages_other, teacher[0], teacher_other)
    stats = lax.all_to_all(stats, CHIPS, 0, 0, tiled=True)
    rows_first, grads, losses = pl.pallas_call(
        grad_kernel,
        out_shape=(
            jax.ShapeDtypeStruct((CORES, rows, block_rows), bf16),
            jax.ShapeDtypeStruct((wide, rows), bf16),
            jax.ShapeDtypeStruct((1, rows), f32),
        ),
        in_specs=[SMEM] + [VMEM] * 3,
        out_specs=(VMEM,) * 3,
        compiler_params=PARAMS,
    )(places, logits, positive, stats)
    loss = lax.dynamic_slice_in_dim(losses[0], chip * own_rows, own_rows)

    width = depth // x_size
    query_part = pl.pallas_call(
        query_kernel,
        out_shape=jax.ShapeDtypeStruct((rows, depth), bf16),
        in_specs=[VMEM] * 3,
        out_specs=VMEM,
        compiler_params=PARAMS,
    )(rows_first, passages, passages_other)
    query_parts = lax.all_to_all(query_part.reshape(chips, own_rows, depth), CHIPS, 0, 0, tiled=True)

    packed_shape = jax.ShapeDtypeStruct((rows + wide * rows // width, width), bf16)
    packed = pl.pallas_call(
        pack_kernel,
        out_shape=(packed_shape,) * x_size,
        in_specs=[SMEM, VMEM, VMEM, ANY],
        out_specs=(VMEM,) * x_size,
        compiler_params=PARAMS,
    )(x.astype(i32)[None], query, grads, query_part)
    packed = [shift(value, "x", d) for d, value in enumerate(packed)]
    part_other = pl.pallas_call(
        functools.partial(other_kernel, rows),
        out_shape=jax.ShapeDtypeStruct((block_rows, width), bf16),
        in_specs=[VMEM] * x_size,
        out_specs=VMEM,
        compiler_params=PARAMS,
    )(*packed)
    part = pl.pallas_call(
        functools.partial(own_kernel, rows),
        out_shape=jax.ShapeDtypeStruct((yh_size, block_rows, width // yh_size), bf16),
        in_specs=[VMEM] * (x_size + 1),
        out_specs=VMEM,
        compiler_params=PARAMS,
    )(*packed, shift(part_other, "core", 1))
    query_parts, part = lax.optimization_barrier((query_parts, part))
    part = lax.all_to_all(part, "yh", 0, 0, tiled=True)
    query_total, passage_total = (
        pl.pallas_call(
            sum_kernel,
            out_shape=jax.ShapeDtypeStruct(value.shape[1:], bf16),
            in_specs=[VMEM],
            out_specs=VMEM,
            compiler_params=PARAMS,
        )(value)
        for value in (query_parts, part)
    )
    return loss[None], query_total[None], passage_total


def solution(mesh):
    blk, qgroup = mesh.devices.shape
    split = Mesh(
        mesh.devices.reshape(YL, blk // (YL * CORES), CORES, X, qgroup // X),
        ("yl", "z", "core", "x", "yh"),
    )
    blk, qgroup = ("yl", "z", "core"), ("x", "yh")
    in_specs = (
        P(qgroup, blk, None),
        P(blk, None),
        P(qgroup, None, blk),
        P(qgroup, blk),
        P(qgroup, blk),
    )
    out_specs = (P(qgroup, blk), P(qgroup, blk, None), P(blk, qgroup))
    return jax.shard_map(per_device, mesh=split, in_specs=in_specs, out_specs=out_specs, check_vma=False)
```

```python
import functools

import jax
import jax.numpy as jnp
from jax import lax
from jax.experimental import pallas as pl
from jax.experimental.pallas import tpu as pltpu
from jax.sharding import Mesh, PartitionSpec as P

inv_temp = 50.0
YL, CORES, X = 2, 2, 4
LANES = 128
STATS = 8
PIECES = 3
CHIPS = ("yl", "z")
f32, bf16, i32 = jnp.float32, jnp.bfloat16, jnp.int32
VMEM = pl.BlockSpec(memory_space=pltpu.VMEM)
ANY = pl.BlockSpec(memory_space=pl.ANY)
SMEM = pl.BlockSpec(memory_space=pltpu.SMEM)
PARAMS = pltpu.CompilerParams(vmem_limit_bytes=16 * 1024 * 1024)


def shift(value, axis, by):
    if by == 0:
        return value
    size = lax.axis_size(axis)
    return lax.ppermute(value, axis, [(i, (i + by) % size) for i in range(size)])


def hits(positive, place, shape):
    return lax.broadcasted_iota(i32, shape, 0) + place == positive


def teacher_kernel(teacher, out):
    rest = teacher[...].T
    for i in range(PIECES):
        piece = rest.astype(bf16)
        out[i] = piece
        rest = rest - piece.astype(f32)


def score_kernel(places, query, passages, passages_other, teacher, teacher_other, values, positives, stats):
    depth = passages.shape[1]
    rows = query.shape[0]
    codes = query[:, depth:].astype(f32).T
    row_index = codes[0:1].astype(i32)
    positive = codes[1:2].astype(i32) + 256 * codes[2:3].astype(i32)
    positives[...] = positive
    pick = (lax.broadcasted_iota(i32, (teacher.shape[2], rows), 0) == row_index).astype(f32).astype(bf16)
    parts = []
    for half, (block, table) in enumerate(((passages, teacher), (passages_other, teacher_other))):
        s = inv_temp * lax.dot_general(
            block[...], query[:, :depth], (((1,), (1,)), ((), ())), preferred_element_type=f32
        )
        t = sum(jnp.dot(table[i], pick, preferred_element_type=f32) for i in range(PIECES))
        values[half] = s
        values[CORES + half] = t
        parts.append((s, t, hits(positive, places[half], s.shape)))
    top_s, top_t = (jnp.maximum(*[jnp.max(p[i], axis=0, keepdims=True) for p in parts]) for i in (0, 1))
    sums = []
    for s, t, hot in parts:
        below_s, below_t = s - top_s, t - top_t
        weight = jnp.exp(below_t)
        terms = (jnp.exp(below_s), weight, weight * (below_t - below_s), jnp.where(hot, s, 0.0))
        sums.append([jnp.sum(v, axis=0, keepdims=True) for v in terms])
    sums = [a + b for a, b in zip(*sums)]
    whole = jnp.concatenate([top_s, top_t] + sums + [jnp.zeros((STATS - 6, rows), f32)], axis=0)
    stats[...] = jnp.broadcast_to(whole[None], stats.shape)


def pack_kernel(places, query, grads, *outs):
    rows = query.shape[0]
    width = outs[0].shape[1]
    tall = outs[0].shape[0] - rows
    for d, out in enumerate(outs):
        out[:rows] = query[:, pl.ds(pl.multiple_of(lax.rem(places[2] + d, len(outs)) * width, width), width)]
        for k in range(width // rows):
            out[rows:, k * rows : (k + 1) * rows] = grads[k * tall : (k + 1) * tall]


def grad_kernel(places, logits, positives, stats, rows_first, grads, losses):
    tops_s, tops_t, sums_s, sums_t, cross, hit = (stats[:, i, :] for i in range(6))
    top_s, top_t = jnp.max(tops_s, axis=0, keepdims=True), jnp.max(tops_t, axis=0, keepdims=True)
    lower_s, lower_t = tops_s - top_s, tops_t - top_t
    total_s = jnp.sum(jnp.exp(lower_s) * sums_s, axis=0, keepdims=True)
    weight_t = jnp.exp(lower_t)
    total_t = jnp.sum(weight_t * sums_t, axis=0, keepdims=True)
    cross = jnp.sum(weight_t * (cross + (lower_t - lower_s) * sums_t), axis=0, keepdims=True)
    log_s = jnp.log(total_s)
    own = jnp.sum(hit, axis=0, keepdims=True)
    losses[...] = cross / total_t - jnp.log(total_t) + log_s - (own - top_s - log_s)
    scale_s, scale_t = 2.0 * inv_temp / total_s, inv_temp / total_t
    block_rows = logits.shape[1]
    for half in range(CORES):
        hot = hits(positives[...], places[half], logits.shape[1:])
        values = (
            jnp.exp(logits[half] - top_s) * scale_s
            - jnp.exp(logits[CORES + half] - top_t) * scale_t
            - jnp.where(hot, inv_temp, 0.0)
        )
        rows_first[half] = values.T.astype(bf16)
        grads[half * block_rows : (half + 1) * block_rows] = values.astype(bf16)


def query_kernel(grads, passages, passages_other, after, out):
    del after
    total = jnp.dot(grads[0], passages[...], preferred_element_type=f32)
    total += jnp.dot(grads[1], passages_other[...], preferred_element_type=f32)
    out[...] = total.astype(bf16)


def products(packed, half, block_rows, rows):
    tall = packed[0].shape[0] - rows
    total = 0.0
    for ref in packed:
        steps = block_rows // tall
        grads = jnp.concatenate(
            [ref[rows:, k * rows : (k + 1) * rows] for k in range(half * steps, (half + 1) * steps)], axis=0
        )
        total += jnp.dot(grads, ref[:rows], preferred_element_type=f32)
    return total


def other_kernel(rows, *refs):
    out = refs[-1]
    out[...] = products(refs[:-1], 1, out.shape[0], rows).astype(bf16)


def own_kernel(groups, rows, places, *refs):
    packed, back, outs, total = refs[:groups], refs[groups], refs[groups + 1 : -1], refs[-1]
    width = outs[0].shape[1]
    total[...] = (products(packed, 0, back.shape[0], rows) + back[...].astype(f32)).astype(bf16)
    for d, out in enumerate(outs):
        out[...] = total[:, pl.ds(pl.multiple_of(lax.rem(places[3] + d, len(outs)) * width, width), width)]


def sum_kernel(query_parts, *refs):
    parts, query_total, total = refs[:-2], refs[-2], refs[-1]
    query_total[...] = sum(query_parts[i].astype(f32) for i in range(query_parts.shape[0])).astype(bf16)
    total[...] = sum(part[...].astype(f32) for part in parts).astype(bf16)


def per_device(queries, passages, teacher, teacher_rows, positives):
    own_rows, depth = queries.shape[1:]
    block_rows = passages.shape[0]
    chips = lax.axis_size("yl") * lax.axis_size("z")
    x_size, yh_size = lax.axis_size("x"), lax.axis_size("yh")
    rows, wide = chips * own_rows, CORES * block_rows
    chip = lax.axis_index("yl") * lax.axis_size("z") + lax.axis_index("z")
    core, x, yh = lax.axis_index("core"), lax.axis_index("x"), lax.axis_index("yh")
    places = jnp.stack(
        [(chip * CORES + core) * block_rows, (chip * CORES + 1 - core) * block_rows, x, yh]
    ).astype(i32)

    indices = jnp.stack(
        [teacher_rows[0], positives[0] % 256, positives[0] // 256], axis=1
    ).astype(bf16)
    sent = jnp.concatenate(
        [queries[0], jnp.pad(indices, ((0, 0), (0, LANES - indices.shape[1])))], axis=1
    )
    passages_other = shift(passages, "core", 1)
    query = lax.all_to_all(
        jnp.broadcast_to(sent[None], (chips,) + sent.shape), CHIPS, 0, 0, tiled=True
    ).reshape(rows, depth + LANES)

    table = pl.pallas_call(
        teacher_kernel,
        out_shape=jax.ShapeDtypeStruct((PIECES, block_rows, teacher.shape[1]), bf16),
        in_specs=[VMEM],
        out_specs=VMEM,
        compiler_params=PARAMS,
        cost_estimate=pl.CostEstimate(flops=10**11, bytes_accessed=2**21, transcendentals=0),
    )(teacher[0])
    table_other = shift(table, "core", 1)
    logits, positive, stats = pl.pallas_call(
        score_kernel,
        out_shape=(
            jax.ShapeDtypeStruct((2 * CORES, block_rows, rows), f32),
            jax.ShapeDtypeStruct((1, rows), i32),
            jax.ShapeDtypeStruct((chips, STATS, rows), f32),
        ),
        in_specs=[SMEM] + [VMEM] * 5,
        out_specs=(VMEM,) * 3,
        compiler_params=PARAMS,
    )(places, query, passages, passages_other, table, table_other)
    stats = lax.all_to_all(stats, CHIPS, 0, 0, tiled=True)
    rows_first, grads, losses = pl.pallas_call(
        grad_kernel,
        out_shape=(
            jax.ShapeDtypeStruct((CORES, rows, block_rows), bf16),
            jax.ShapeDtypeStruct((wide, rows), bf16),
            jax.ShapeDtypeStruct((1, rows), f32),
        ),
        in_specs=[SMEM] + [VMEM] * 3,
        out_specs=(VMEM,) * 3,
        compiler_params=PARAMS,
    )(places, logits, positive, stats)
    loss = lax.dynamic_slice_in_dim(losses[0], chip * own_rows, own_rows)

    width = depth // x_size
    packed_shape = jax.ShapeDtypeStruct((rows + wide * rows // width, width), bf16)
    packed = pl.pallas_call(
        pack_kernel,
        out_shape=(packed_shape,) * x_size,
        in_specs=[SMEM, VMEM, VMEM],
        out_specs=(VMEM,) * x_size,
        compiler_params=PARAMS,
    )(places, query, grads)
    query_part = pl.pallas_call(
        query_kernel,
        out_shape=jax.ShapeDtypeStruct((rows, depth), bf16),
        in_specs=[VMEM] * 3 + [ANY],
        out_specs=VMEM,
        compiler_params=PARAMS,
    )(rows_first, passages, passages_other, packed[0])
    query_parts = lax.all_to_all(query_part.reshape(chips, own_rows, depth), CHIPS, 0, 0, tiled=True)
    packed = [shift(value, "x", d) for d, value in enumerate(packed)]
    part_other = pl.pallas_call(
        functools.partial(other_kernel, rows),
        out_shape=jax.ShapeDtypeStruct((block_rows, width), bf16),
        in_specs=[VMEM] * x_size,
        out_specs=VMEM,
        compiler_params=PARAMS,
        cost_estimate=pl.CostEstimate(flops=10**11, bytes_accessed=2**21, transcendentals=0),
    )(*packed)
    parts = pl.pallas_call(
        functools.partial(own_kernel, x_size, rows),
        out_shape=(jax.ShapeDtypeStruct((block_rows, width // yh_size), bf16),) * yh_size,
        in_specs=[SMEM] + [VMEM] * (x_size + 1),
        out_specs=(VMEM,) * yh_size,
        scratch_shapes=[pltpu.VMEM((block_rows, width), bf16)],
        compiler_params=PARAMS,
    )(places, *packed, shift(part_other, "core", 1))
    parts = [shift(part, "yh", d) for d, part in enumerate(parts)]
    query_total, passage_total = pl.pallas_call(
        sum_kernel,
        out_shape=(
            jax.ShapeDtypeStruct((own_rows, depth), bf16),
            jax.ShapeDtypeStruct(parts[0].shape, bf16),
        ),
        in_specs=[VMEM] * (1 + yh_size),
        out_specs=(VMEM,) * 2,
        compiler_params=PARAMS,
    )(query_parts, *parts)
    return loss[None], query_total[None], passage_total


def solution(mesh):
    blk, qgroup = mesh.devices.shape
    split = Mesh(
        mesh.devices.reshape(YL, blk // (YL * CORES), CORES, X, qgroup // X),
        ("yl", "z", "core", "x", "yh"),
    )
    blk, qgroup = ("yl", "z", "core"), ("x", "yh")
    in_specs = (
        P(qgroup, blk, None),
        P(blk, None),
        P(qgroup, None, blk),
        P(qgroup, blk),
        P(qgroup, blk),
    )
    out_specs = (P(qgroup, blk), P(qgroup, blk, None), P(blk, qgroup))
    return jax.shard_map(per_device, mesh=split, in_specs=in_specs, out_specs=out_specs, check_vma=False)
```

```python
import functools

import jax
import jax.numpy as jnp
from jax import lax
from jax.experimental import pallas as pl
from jax.experimental.pallas import tpu as pltpu
from jax.sharding import Mesh, PartitionSpec as P

inv_temp = 50.0
YL, CORES, X = 2, 2, 4
LANES = 128
STATS = 8
PIECES = 3
CHIPS = ("yl", "z")
f32, bf16, i32 = jnp.float32, jnp.bfloat16, jnp.int32
VMEM = pl.BlockSpec(memory_space=pltpu.VMEM)
ANY = pl.BlockSpec(memory_space=pl.ANY)
SMEM = pl.BlockSpec(memory_space=pltpu.SMEM)
PARAMS = pltpu.CompilerParams(vmem_limit_bytes=16 * 1024 * 1024)


def shift(value, axis, by):
    if by == 0:
        return value
    size = lax.axis_size(axis)
    return lax.ppermute(value, axis, [(i, (i + by) % size) for i in range(size)])


def shifts(values, axis):
    size = len(values)
    order = sorted(range(size), key=lambda d: -min(d, size - d))
    moved = {d: shift(values[d], axis, d) for d in order}
    return [moved[d] for d in range(size)]


def hits(positive, place, shape):
    return lax.broadcasted_iota(i32, shape, 0) + place == positive


def teacher_kernel(teacher, out):
    rest = teacher[...].T
    for i in range(PIECES):
        piece = rest.astype(bf16)
        out[i] = piece
        rest = rest - piece.astype(f32)


def indices(codes, own_rows):
    rows, lanes = codes.shape
    first, second = (lax.broadcasted_iota(i32, (lanes, rows), k) for k in (0, 1))
    spread = (lax.rem(second, own_rows) == first).astype(f32).astype(bf16)
    spread = jnp.dot(codes, spread, preferred_element_type=f32)
    first, second = (lax.broadcasted_iota(i32, (rows, rows), k) for k in (0, 1))
    begin = second - lax.rem(second, own_rows)
    return [
        jnp.sum(jnp.where(first == begin + kind, spread, 0.0), axis=0, keepdims=True).astype(i32) for kind in range(3)
    ]


def score_kernel(places, query, passages, passages_other, teacher, teacher_other, values, positives, stats):
    depth = passages.shape[1]
    rows = query.shape[0]
    row_index, low, high = indices(query[:, depth:], rows // stats.shape[0])
    positive = low + 256 * high
    positives[...] = positive
    pick = (lax.broadcasted_iota(i32, (teacher.shape[2], rows), 0) == row_index).astype(f32).astype(bf16)
    parts = []
    for half, (block, table) in enumerate(((passages, teacher), (passages_other, teacher_other))):
        s = inv_temp * lax.dot_general(
            block[...], query[:, :depth], (((1,), (1,)), ((), ())), preferred_element_type=f32
        )
        t = sum(jnp.dot(table[i], pick, preferred_element_type=f32) for i in range(PIECES))
        values[half] = s
        values[CORES + half] = t
        parts.append((s, t, hits(positive, places[half], s.shape)))
    top_s, top_t = (jnp.maximum(*[jnp.max(p[i], axis=0, keepdims=True) for p in parts]) for i in (0, 1))
    sums = []
    for s, t, hot in parts:
        below_s, below_t = s - top_s, t - top_t
        weight = jnp.exp(below_t)
        terms = (jnp.exp(below_s), weight, weight * (below_t - below_s), jnp.where(hot, s, 0.0))
        sums.append([jnp.sum(v, axis=0, keepdims=True) for v in terms])
    sums = [a + b for a, b in zip(*sums)]
    whole = jnp.concatenate([top_s, top_t] + sums + [jnp.zeros((STATS - 6, rows), f32)], axis=0)
    stats[...] = jnp.broadcast_to(whole[None], stats.shape)


def grad_kernel(places, query, logits, positives, stats, rows_first, losses, *packed):
    rows, width = query.shape[0], packed[0].shape[1]
    for d, out in enumerate(packed):
        out[:rows] = query[:, pl.ds(pl.multiple_of(lax.rem(places[2] + d, len(packed)) * width, width), width)]
    tall = packed[0].shape[0] - rows
    tops_s, tops_t, sums_s, sums_t, cross, hit = (stats[:, i, :] for i in range(6))
    top_s, top_t = jnp.max(tops_s, axis=0, keepdims=True), jnp.max(tops_t, axis=0, keepdims=True)
    lower_s, lower_t = tops_s - top_s, tops_t - top_t
    total_s = jnp.sum(jnp.exp(lower_s) * sums_s, axis=0, keepdims=True)
    weight_t = jnp.exp(lower_t)
    total_t = jnp.sum(weight_t * sums_t, axis=0, keepdims=True)
    cross = jnp.sum(weight_t * (cross + (lower_t - lower_s) * sums_t), axis=0, keepdims=True)
    log_s = jnp.log(total_s)
    own = jnp.sum(hit, axis=0, keepdims=True)
    losses[...] = cross / total_t - jnp.log(total_t) + log_s - (own - top_s - log_s)
    scale_s, scale_t = 2.0 * inv_temp / total_s, inv_temp / total_t
    block_rows = logits.shape[1]
    for half in range(CORES):
        hot = hits(positives[...], places[half], logits.shape[1:])
        values = (
            jnp.exp(logits[half] - top_s) * scale_s
            - jnp.exp(logits[CORES + half] - top_t) * scale_t
            - jnp.where(hot, inv_temp, 0.0)
        )
        rows_first[half] = values.T.astype(bf16)
        values = values.astype(bf16)
        steps = block_rows // tall
        for k in range(steps):
            lane = (half * steps + k) * rows
            for out in packed:
                out[rows:, lane : lane + rows] = values[k * tall : (k + 1) * tall]


def query_kernel(grads, passages, passages_other, after, out):
    del after
    total = jnp.dot(grads[0], passages[...], preferred_element_type=f32)
    total += jnp.dot(grads[1], passages_other[...], preferred_element_type=f32)
    out[...] = total.astype(bf16)


def products(packed, half, block_rows, rows):
    tall = packed[0].shape[0] - rows
    total = 0.0
    for ref in packed:
        steps = block_rows // tall
        grads = jnp.concatenate(
            [ref[rows:, k * rows : (k + 1) * rows] for k in range(half * steps, (half + 1) * steps)], axis=0
        )
        total += jnp.dot(grads, ref[:rows], preferred_element_type=f32)
    return total


def other_kernel(rows, *refs):
    out = refs[-1]
    out[...] = products(refs[:-1], 1, out.shape[0], rows).astype(bf16)


def own_kernel(groups, rows, places, *refs):
    packed, back, outs, total = refs[:groups], refs[groups], refs[groups + 1 : -1], refs[-1]
    width = outs[0].shape[1]
    total[...] = (products(packed, 0, back.shape[0], rows) + back[...].astype(f32)).astype(bf16)
    for d, out in enumerate(outs):
        out[...] = total[:, pl.ds(pl.multiple_of(lax.rem(places[3] + d, len(outs)) * width, width), width)]


def sum_kernel(query_parts, *refs):
    parts, query_total, total = refs[:-2], refs[-2], refs[-1]
    query_total[...] = sum(query_parts[i].astype(f32) for i in range(query_parts.shape[0])).astype(bf16)
    total[...] = sum(part[...].astype(f32) for part in parts).astype(bf16)


def per_device(queries, passages, teacher, teacher_rows, positives):
    own_rows, depth = queries.shape[1:]
    block_rows = passages.shape[0]
    chips = lax.axis_size("yl") * lax.axis_size("z")
    x_size, yh_size = lax.axis_size("x"), lax.axis_size("yh")
    rows, wide = chips * own_rows, CORES * block_rows
    chip = lax.axis_index("yl") * lax.axis_size("z") + lax.axis_index("z")
    core, x, yh = lax.axis_index("core"), lax.axis_index("x"), lax.axis_index("yh")
    places = jnp.stack(
        [(chip * CORES + core) * block_rows, (chip * CORES + 1 - core) * block_rows, x, yh]
    ).astype(i32)

    codes = jnp.concatenate([teacher_rows, positives & 255, lax.shift_right_logical(positives, 8)], axis=0)
    codes = jnp.pad(codes, ((0, own_rows - codes.shape[0]), (0, LANES - own_rows)))
    sent = jnp.concatenate([queries[0], codes.astype(bf16)], axis=1)
    passages_other = shift(passages, "core", 1)
    query = lax.all_to_all(
        jnp.broadcast_to(sent[None], (chips,) + sent.shape), CHIPS, 0, 0, tiled=True
    ).reshape(rows, depth + LANES)

    table = pl.pallas_call(
        teacher_kernel,
        out_shape=jax.ShapeDtypeStruct((PIECES, block_rows, teacher.shape[1]), bf16),
        in_specs=[VMEM],
        out_specs=VMEM,
        compiler_params=PARAMS,
        cost_estimate=pl.CostEstimate(flops=10**11, bytes_accessed=2**21, transcendentals=0),
    )(teacher[0])
    table_other = shift(table, "core", 1)
    logits, positive, stats = pl.pallas_call(
        score_kernel,
        out_shape=(
            jax.ShapeDtypeStruct((2 * CORES, block_rows, rows), f32),
            jax.ShapeDtypeStruct((1, rows), i32),
            jax.ShapeDtypeStruct((chips, STATS, rows), f32),
        ),
        in_specs=[SMEM] + [VMEM] * 5,
        out_specs=(VMEM,) * 3,
        compiler_params=PARAMS,
    )(places, query, passages, passages_other, table, table_other)
    stats = lax.all_to_all(stats, CHIPS, 0, 0, tiled=True)
    width = depth // x_size
    rows_first, losses, *packed = pl.pallas_call(
        grad_kernel,
        out_shape=(
            jax.ShapeDtypeStruct((CORES, rows, block_rows), bf16),
            jax.ShapeDtypeStruct((1, rows), f32),
        )
        + (jax.ShapeDtypeStruct((rows + wide * rows // width, width), bf16),) * x_size,
        in_specs=[SMEM] + [VMEM] * 4,
        out_specs=(VMEM,) * (2 + x_size),
        compiler_params=PARAMS,
    )(places, query, logits, positive, stats)
    loss = lax.dynamic_slice_in_dim(losses[0], chip * own_rows, own_rows)

    width = depth // x_size
    query_part = pl.pallas_call(
        query_kernel,
        out_shape=jax.ShapeDtypeStruct((rows, depth), bf16),
        in_specs=[VMEM] * 3 + [ANY],
        out_specs=VMEM,
        compiler_params=PARAMS,
    )(rows_first, passages, passages_other, packed[0])
    query_parts = lax.all_to_all(query_part.reshape(chips, own_rows, depth), CHIPS, 0, 0, tiled=True)
    packed = shifts(packed, "x")
    part_other = pl.pallas_call(
        functools.partial(other_kernel, rows),
        out_shape=jax.ShapeDtypeStruct((block_rows, width), bf16),
        in_specs=[VMEM] * x_size,
        out_specs=VMEM,
        compiler_params=PARAMS,
        cost_estimate=pl.CostEstimate(flops=10**11, bytes_accessed=2**21, transcendentals=0),
    )(*packed)
    parts = pl.pallas_call(
        functools.partial(own_kernel, x_size, rows),
        out_shape=(jax.ShapeDtypeStruct((block_rows, width // yh_size), bf16),) * yh_size,
        in_specs=[SMEM] + [VMEM] * (x_size + 1),
        out_specs=(VMEM,) * yh_size,
        scratch_shapes=[pltpu.VMEM((block_rows, width), bf16)],
        compiler_params=PARAMS,
    )(places, *packed, shift(part_other, "core", 1))
    parts = shifts(parts, "yh")
    query_total, passage_total = pl.pallas_call(
        sum_kernel,
        out_shape=(
            jax.ShapeDtypeStruct((own_rows, depth), bf16),
            jax.ShapeDtypeStruct(parts[0].shape, bf16),
        ),
        in_specs=[VMEM] * (1 + yh_size),
        out_specs=(VMEM,) * 2,
        compiler_params=PARAMS,
    )(query_parts, *parts)
    return loss[None], query_total[None], passage_total


def solution(mesh):
    blk, qgroup = mesh.devices.shape
    split = Mesh(
        mesh.devices.reshape(YL, blk // (YL * CORES), CORES, X, qgroup // X),
        ("yl", "z", "core", "x", "yh"),
    )
    blk, qgroup = ("yl", "z", "core"), ("x", "yh")
    in_specs = (
        P(qgroup, blk, None),
        P(blk, None),
        P(qgroup, None, blk),
        P(qgroup, blk),
        P(qgroup, blk),
    )
    out_specs = (P(qgroup, blk), P(qgroup, blk, None), P(blk, qgroup))
    return jax.shard_map(per_device, mesh=split, in_specs=in_specs, out_specs=out_specs, check_vma=False)
```

```python
import functools

import jax
import jax.numpy as jnp
from jax import lax
from jax.experimental import pallas as pl
from jax.experimental.pallas import tpu as pltpu
from jax.sharding import Mesh, PartitionSpec as P

inv_temp = 50.0
YL, ZL, CORES, X = 2, 2, 2, 4
LANES = 128
STATS = 8
PIECES = 3
NEAR, FAR = ("yl", "zl"), ("zh",)
CHIPS = NEAR + FAR
f32, bf16, i32 = jnp.float32, jnp.bfloat16, jnp.int32
VMEM = pl.BlockSpec(memory_space=pltpu.VMEM)
ANY = pl.BlockSpec(memory_space=pl.ANY)
SMEM = pl.BlockSpec(memory_space=pltpu.SMEM)
PARAMS = pltpu.CompilerParams(vmem_limit_bytes=16 * 1024 * 1024)


def shift(value, axis, by):
    if by == 0:
        return value
    size = lax.axis_size(axis)
    return lax.ppermute(value, axis, [(i, (i + by) % size) for i in range(size)])


def shifts(values, axis):
    size = len(values)
    order = sorted(range(size), key=lambda d: -min(d, size - d))
    moved = {d: shift(values[d], axis, d) for d in order}
    return [moved[d] for d in range(size)]


def spread(value, axes):
    size = 1
    for axis in axes:
        size *= lax.axis_size(axis)
    copies = jnp.broadcast_to(value[None], (size,) + value.shape)
    return lax.all_to_all(copies, axes, 0, 0, tiled=True).reshape(size * value.shape[0], value.shape[1])


def hits(positive, place, shape):
    return lax.broadcasted_iota(i32, shape, 0) + place == positive


def teacher_kernel(teacher, out):
    rest = teacher[...].T
    for i in range(PIECES):
        piece = rest.astype(bf16)
        out[i] = piece
        rest = rest - piece.astype(f32)


def indices(codes, own_rows):
    rows, lanes = codes.shape
    first, second = (lax.broadcasted_iota(i32, (lanes, rows), k) for k in (0, 1))
    spread = (lax.rem(second, own_rows) == first).astype(f32).astype(bf16)
    spread = jnp.dot(codes, spread, preferred_element_type=f32)
    first, second = (lax.broadcasted_iota(i32, (rows, rows), k) for k in (0, 1))
    begin = second - lax.rem(second, own_rows)
    return [
        jnp.sum(jnp.where(first == begin + kind, spread, 0.0), axis=0, keepdims=True).astype(i32) for kind in range(3)
    ]


def score_kernel(places, query, passages, passages_other, teacher, teacher_other, values, positives, stats):
    depth = passages.shape[1]
    rows = query.shape[0]
    row_index, low, high = indices(query[:, depth:], rows // stats.shape[0])
    positive = low + 256 * high
    positives[...] = positive
    pick = (lax.broadcasted_iota(i32, (teacher.shape[2], rows), 0) == row_index).astype(f32).astype(bf16)
    parts = []
    for half, (block, table) in enumerate(((passages, teacher), (passages_other, teacher_other))):
        s = inv_temp * lax.dot_general(
            block[...], query[:, :depth], (((1,), (1,)), ((), ())), preferred_element_type=f32
        )
        t = sum(jnp.dot(table[i], pick, preferred_element_type=f32) for i in range(PIECES))
        values[half] = s
        values[CORES + half] = t
        parts.append((s, t, hits(positive, places[half], s.shape)))
    top_s, top_t = (jnp.maximum(*[jnp.max(p[i], axis=0, keepdims=True) for p in parts]) for i in (0, 1))
    sums = []
    for s, t, hot in parts:
        below_s, below_t = s - top_s, t - top_t
        weight = jnp.exp(below_t)
        terms = (jnp.exp(below_s), weight, weight * (below_t - below_s), jnp.where(hot, s, 0.0))
        sums.append([jnp.sum(v, axis=0, keepdims=True) for v in terms])
    sums = [a + b for a, b in zip(*sums)]
    whole = jnp.concatenate([top_s, top_t] + sums + [jnp.zeros((STATS - 6, rows), f32)], axis=0)
    stats[...] = jnp.broadcast_to(whole[None], stats.shape)


def grad_kernel(places, query, logits, positives, stats, rows_first, losses, *packed):
    rows, width = query.shape[0], packed[0].shape[1]
    for d, out in enumerate(packed):
        out[:rows] = query[:, pl.ds(pl.multiple_of(lax.rem(places[2] + d, len(packed)) * width, width), width)]
    tall = packed[0].shape[0] - rows
    tops_s, tops_t, sums_s, sums_t, cross, hit = (stats[:, i, :] for i in range(6))
    top_s, top_t = jnp.max(tops_s, axis=0, keepdims=True), jnp.max(tops_t, axis=0, keepdims=True)
    lower_s, lower_t = tops_s - top_s, tops_t - top_t
    total_s = jnp.sum(jnp.exp(lower_s) * sums_s, axis=0, keepdims=True)
    weight_t = jnp.exp(lower_t)
    total_t = jnp.sum(weight_t * sums_t, axis=0, keepdims=True)
    cross = jnp.sum(weight_t * (cross + (lower_t - lower_s) * sums_t), axis=0, keepdims=True)
    log_s = jnp.log(total_s)
    own = jnp.sum(hit, axis=0, keepdims=True)
    losses[...] = cross / total_t - jnp.log(total_t) + log_s - (own - top_s - log_s)
    scale_s, scale_t = 2.0 * inv_temp / total_s, inv_temp / total_t
    block_rows = logits.shape[1]
    for half in range(CORES):
        hot = hits(positives[...], places[half], logits.shape[1:])
        values = (
            jnp.exp(logits[half] - top_s) * scale_s
            - jnp.exp(logits[CORES + half] - top_t) * scale_t
            - jnp.where(hot, inv_temp, 0.0)
        )
        rows_first[half] = values.T.astype(bf16)
        values = values.astype(bf16)
        steps = block_rows // tall
        for k in range(steps):
            lane = (half * steps + k) * rows
            for out in packed:
                out[rows:, lane : lane + rows] = values[k * tall : (k + 1) * tall]


def query_kernel(grads, passages, passages_other, after, out):
    del after
    total = jnp.dot(grads[0], passages[...], preferred_element_type=f32)
    total += jnp.dot(grads[1], passages_other[...], preferred_element_type=f32)
    out[...] = total.astype(bf16)


def products(packed, half, block_rows, rows):
    tall = packed[0].shape[0] - rows
    total = 0.0
    for ref in packed:
        steps = block_rows // tall
        grads = jnp.concatenate(
            [ref[rows:, k * rows : (k + 1) * rows] for k in range(half * steps, (half + 1) * steps)], axis=0
        )
        total += jnp.dot(grads, ref[:rows], preferred_element_type=f32)
    return total


def product_kernel(half, rows, *refs):
    out = refs[-1]
    out[...] = products(refs[:-1], half, out.shape[0], rows).astype(out.dtype)


def add_kernel(places, part, back, *outs):
    width = outs[0].shape[1]
    for d, out in enumerate(outs):
        columns = pl.ds(pl.multiple_of(lax.rem(places[3] + d, len(outs)) * width, width), width)
        out[...] = (part[:, columns] + back[:, columns].astype(f32)).astype(bf16)


def sum_kernel(query_parts, *refs):
    parts, query_total, total = refs[:-2], refs[-2], refs[-1]
    query_total[...] = sum(query_parts[i].astype(f32) for i in range(query_parts.shape[0])).astype(bf16)
    total[...] = sum(part[...].astype(f32) for part in parts).astype(bf16)


def per_device(queries, passages, teacher, teacher_rows, positives):
    own_rows, depth = queries.shape[1:]
    block_rows = passages.shape[0]
    yl, zh, zl = (lax.axis_index(axis) for axis in ("yl", "zh", "zl"))
    far, near = lax.axis_size("zh"), lax.axis_size("zl")
    chips = lax.axis_size("yl") * near * far
    x_size, yh_size = lax.axis_size("x"), lax.axis_size("yh")
    rows, wide = chips * own_rows, CORES * block_rows
    chip, block = (yl * near + zl) * far + zh, (yl * far + zh) * near + zl
    core, x, yh = lax.axis_index("core"), lax.axis_index("x"), lax.axis_index("yh")
    places = jnp.stack(
        [(block * CORES + core) * block_rows, (block * CORES + 1 - core) * block_rows, x, yh]
    ).astype(i32)

    codes = jnp.concatenate([teacher_rows, positives & 255, lax.shift_right_logical(positives, 8)], axis=0)
    codes = jnp.pad(codes, ((0, own_rows - codes.shape[0]), (0, LANES - own_rows)))
    sent = jnp.concatenate([queries[0], codes.astype(bf16)], axis=1)
    passages_other = shift(passages, "core", 1)
    query = spread(spread(sent, FAR), NEAR)

    table = pl.pallas_call(
        teacher_kernel,
        out_shape=jax.ShapeDtypeStruct((PIECES, block_rows, teacher.shape[1]), bf16),
        in_specs=[VMEM],
        out_specs=VMEM,
        compiler_params=PARAMS,
        cost_estimate=pl.CostEstimate(flops=10**11, bytes_accessed=2**21, transcendentals=0),
    )(teacher[0])
    table_other = shift(table, "core", 1)
    logits, positive, stats = pl.pallas_call(
        score_kernel,
        out_shape=(
            jax.ShapeDtypeStruct((2 * CORES, block_rows, rows), f32),
            jax.ShapeDtypeStruct((1, rows), i32),
            jax.ShapeDtypeStruct((chips, STATS, rows), f32),
        ),
        in_specs=[SMEM] + [VMEM] * 5,
        out_specs=(VMEM,) * 3,
        compiler_params=PARAMS,
    )(places, query, passages, passages_other, table, table_other)
    stats = lax.all_to_all(stats, CHIPS, 0, 0, tiled=True)
    width = depth // x_size
    rows_first, losses, *packed = pl.pallas_call(
        grad_kernel,
        out_shape=(
            jax.ShapeDtypeStruct((CORES, rows, block_rows), bf16),
            jax.ShapeDtypeStruct((1, rows), f32),
        )
        + (jax.ShapeDtypeStruct((rows + wide * rows // width, width), bf16),) * x_size,
        in_specs=[SMEM] + [VMEM] * 4,
        out_specs=(VMEM,) * (2 + x_size),
        compiler_params=PARAMS,
    )(places, query, logits, positive, stats)
    loss = lax.dynamic_slice_in_dim(losses[0], chip * own_rows, own_rows)

    width = depth // x_size
    query_part = pl.pallas_call(
        query_kernel,
        out_shape=jax.ShapeDtypeStruct((rows, depth), bf16),
        in_specs=[VMEM] * 3 + [ANY],
        out_specs=VMEM,
        compiler_params=PARAMS,
    )(rows_first, passages, passages_other, packed[0])
    query_parts = lax.all_to_all(query_part.reshape(chips, own_rows, depth), CHIPS, 0, 0, tiled=True)
    packed = shifts(packed, "x")
    part, part_other = (
        pl.pallas_call(
            functools.partial(product_kernel, half, rows),
            out_shape=jax.ShapeDtypeStruct((block_rows, width), dtype),
            in_specs=[VMEM] * x_size,
            out_specs=VMEM,
            compiler_params=PARAMS,
            cost_estimate=pl.CostEstimate(flops=10**11, bytes_accessed=2**21, transcendentals=0),
        )(*packed)
        for half, dtype in enumerate((f32, bf16))
    )
    parts = pl.pallas_call(
        add_kernel,
        out_shape=(jax.ShapeDtypeStruct((block_rows, width // yh_size), bf16),) * yh_size,
        in_specs=[SMEM] + [VMEM] * 2,
        out_specs=(VMEM,) * yh_size,
        compiler_params=PARAMS,
    )(places, part, shift(part_other, "core", 1))
    parts = shifts(parts, "yh")
    query_total, passage_total = pl.pallas_call(
        sum_kernel,
        out_shape=(
            jax.ShapeDtypeStruct((own_rows, depth), bf16),
            jax.ShapeDtypeStruct(parts[0].shape, bf16),
        ),
        in_specs=[VMEM] * (1 + yh_size),
        out_specs=(VMEM,) * 2,
        compiler_params=PARAMS,
    )(query_parts, *parts)
    return loss[None], query_total[None], passage_total


def solution(mesh):
    blk, qgroup = mesh.devices.shape
    split = Mesh(
        mesh.devices.reshape(YL, blk // (YL * ZL * CORES), ZL, CORES, X, qgroup // X),
        ("yl", "zh", "zl", "core", "x", "yh"),
    )
    blk, qgroup = ("yl", "zh", "zl", "core"), ("x", "yh")
    in_specs = (
        P(qgroup, blk, None),
        P(blk, None),
        P(qgroup, None, blk),
        P(qgroup, blk),
        P(qgroup, blk),
    )
    out_specs = (P(qgroup, blk), P(qgroup, blk, None), P(blk, qgroup))
    return jax.shard_map(per_device, mesh=split, in_specs=in_specs, out_specs=out_specs, check_vma=False)
```

```python
import functools

import jax
import jax.numpy as jnp
from jax import lax
from jax.experimental import pallas as pl
from jax.experimental.pallas import tpu as pltpu
from jax.sharding import Mesh, PartitionSpec as P

inv_temp = 50.0
YL, CORES, X = 2, 2, 4
LANES = 128
STATS = 8
PIECES = 3
CHIPS = ("yl", "z")
f32, bf16, i32 = jnp.float32, jnp.bfloat16, jnp.int32
VMEM = pl.BlockSpec(memory_space=pltpu.VMEM)
ANY = pl.BlockSpec(memory_space=pl.ANY)
SMEM = pl.BlockSpec(memory_space=pltpu.SMEM)
PARAMS = pltpu.CompilerParams(vmem_limit_bytes=16 * 1024 * 1024)


def shift(value, axis, by):
    if by == 0:
        return value
    size = lax.axis_size(axis)
    return lax.ppermute(value, axis, [(i, (i + by) % size) for i in range(size)])


def shifts(values, axis):
    size = len(values)
    order = sorted(range(size), key=lambda d: -min(d, size - d))
    moved = {d: shift(values[d], axis, d) for d in order}
    return [moved[d] for d in range(size)]


def hits(positive, place, shape):
    return lax.broadcasted_iota(i32, shape, 0) + place == positive


def teacher_kernel(teacher, out):
    rest = teacher[...].T
    for i in range(PIECES):
        piece = rest.astype(bf16)
        out[i] = piece
        rest = rest - piece.astype(f32)


def indices(codes, own_rows):
    rows, lanes = codes.shape
    first, second = (lax.broadcasted_iota(i32, (lanes, rows), k) for k in (0, 1))
    spread = (lax.rem(second, own_rows) == first).astype(f32).astype(bf16)
    spread = jnp.dot(codes, spread, preferred_element_type=f32)
    first, second = (lax.broadcasted_iota(i32, (rows, rows), k) for k in (0, 1))
    begin = second - lax.rem(second, own_rows)
    return [
        jnp.sum(jnp.where(first == begin + kind, spread, 0.0), axis=0, keepdims=True).astype(i32) for kind in range(3)
    ]


def score_kernel(places, query, passages, passages_other, teacher, teacher_other, values, positives, stats):
    depth = passages.shape[1]
    rows = query.shape[0]
    row_index, low, high = indices(query[:, depth:], rows // stats.shape[0])
    positive = low + 256 * high
    positives[...] = positive
    pick = (lax.broadcasted_iota(i32, (teacher.shape[2], rows), 0) == row_index).astype(f32).astype(bf16)
    parts = []
    for half, (block, table) in enumerate(((passages, teacher), (passages_other, teacher_other))):
        s = inv_temp * lax.dot_general(
            block[...], query[:, :depth], (((1,), (1,)), ((), ())), preferred_element_type=f32
        )
        t = sum(jnp.dot(table[i], pick, preferred_element_type=f32) for i in range(PIECES))
        values[half] = s
        values[CORES + half] = t
        parts.append((s, t, hits(positive, places[half], s.shape)))
    top_s, top_t = (jnp.maximum(*[jnp.max(p[i], axis=0, keepdims=True) for p in parts]) for i in (0, 1))
    sums = []
    for s, t, hot in parts:
        below_s, below_t = s - top_s, t - top_t
        weight = jnp.exp(below_t)
        terms = (jnp.exp(below_s), weight, weight * (below_t - below_s), jnp.where(hot, s, 0.0))
        sums.append([jnp.sum(v, axis=0, keepdims=True) for v in terms])
    sums = [a + b for a, b in zip(*sums)]
    whole = jnp.concatenate([top_s, top_t] + sums + [jnp.zeros((STATS - 6, rows), f32)], axis=0)
    stats[...] = jnp.broadcast_to(whole[None], stats.shape)


def slice_kernel(places, query, out):
    width = out.shape[1]
    count = (query.shape[1] - LANES) // width
    out[...] = query[:, pl.ds(pl.multiple_of(lax.rem(places[2] + count // 2, count) * width, width), width)]


def pack_kernel(places, query, grads, after, *outs):
    del after
    rows = query.shape[0]
    tall, width = outs[len(outs) // 2].shape
    for d, out in enumerate(outs):
        if d != len(outs) // 2:
            out[:rows] = query[:, pl.ds(pl.multiple_of(lax.rem(places[2] + d, len(outs)) * width, width), width)]
        for k in range(width // rows):
            out[out.shape[0] - tall :, k * rows : (k + 1) * rows] = grads[k * tall : (k + 1) * tall]


def grad_kernel(places, logits, positives, stats, after, rows_first, grads, losses):
    del after
    tops_s, tops_t, sums_s, sums_t, cross, hit = (stats[:, i, :] for i in range(6))
    top_s, top_t = jnp.max(tops_s, axis=0, keepdims=True), jnp.max(tops_t, axis=0, keepdims=True)
    lower_s, lower_t = tops_s - top_s, tops_t - top_t
    total_s = jnp.sum(jnp.exp(lower_s) * sums_s, axis=0, keepdims=True)
    weight_t = jnp.exp(lower_t)
    total_t = jnp.sum(weight_t * sums_t, axis=0, keepdims=True)
    cross = jnp.sum(weight_t * (cross + (lower_t - lower_s) * sums_t), axis=0, keepdims=True)
    log_s = jnp.log(total_s)
    own = jnp.sum(hit, axis=0, keepdims=True)
    losses[...] = cross / total_t - jnp.log(total_t) + log_s - (own - top_s - log_s)
    scale_s, scale_t = 2.0 * inv_temp / total_s, inv_temp / total_t
    block_rows = logits.shape[1]
    for half in range(CORES):
        hot = hits(positives[...], places[half], logits.shape[1:])
        values = (
            jnp.exp(logits[half] - top_s) * scale_s
            - jnp.exp(logits[CORES + half] - top_t) * scale_t
            - jnp.where(hot, inv_temp, 0.0)
        )
        rows_first[half] = values.T.astype(bf16)
        grads[half * block_rows : (half + 1) * block_rows] = values.astype(bf16)


def query_kernel(grads, passages, passages_other, out):
    total = jnp.dot(grads[0], passages[...], preferred_element_type=f32)
    total += jnp.dot(grads[1], passages_other[...], preferred_element_type=f32)
    out[...] = total.astype(bf16)


def products(packed, columns, half, block_rows, rows):
    tall = packed[len(packed) // 2].shape[0]
    total = 0.0
    for d, ref in enumerate(packed):
        begin = ref.shape[0] - tall
        steps = block_rows // tall
        grads = jnp.concatenate(
            [ref[begin:, k * rows : (k + 1) * rows] for k in range(half * steps, (half + 1) * steps)], axis=0
        )
        total += jnp.dot(grads, ref[:rows] if begin else columns[...], preferred_element_type=f32)
    return total


def other_kernel(rows, *refs):
    *packed, columns, out = refs
    out[...] = products(packed, columns, 1, out.shape[0], rows).astype(bf16)


def own_kernel(groups, rows, places, *refs):
    packed, columns, back, outs, total = refs[:groups], refs[groups], refs[groups + 1], refs[groups + 2 : -1], refs[-1]
    width = outs[0].shape[1]
    total[...] = (products(packed, columns, 0, back.shape[0], rows) + back[...].astype(f32)).astype(bf16)
    for d, out in enumerate(outs):
        out[...] = total[:, pl.ds(pl.multiple_of(lax.rem(places[3] + d, len(outs)) * width, width), width)]


def sum_kernel(query_parts, *refs):
    parts, query_total, total = refs[:-2], refs[-2], refs[-1]
    query_total[...] = sum(query_parts[i].astype(f32) for i in range(query_parts.shape[0])).astype(bf16)
    total[...] = sum(part[...].astype(f32) for part in parts).astype(bf16)


def per_device(queries, passages, teacher, teacher_rows, positives):
    own_rows, depth = queries.shape[1:]
    block_rows = passages.shape[0]
    chips = lax.axis_size("yl") * lax.axis_size("z")
    x_size, yh_size = lax.axis_size("x"), lax.axis_size("yh")
    rows, wide = chips * own_rows, CORES * block_rows
    chip = lax.axis_index("yl") * lax.axis_size("z") + lax.axis_index("z")
    core, x, yh = lax.axis_index("core"), lax.axis_index("x"), lax.axis_index("yh")
    places = jnp.stack(
        [(chip * CORES + core) * block_rows, (chip * CORES + 1 - core) * block_rows, x, yh]
    ).astype(i32)

    codes = jnp.concatenate([teacher_rows, positives & 255, lax.shift_right_logical(positives, 8)], axis=0)
    codes = jnp.pad(codes, ((0, own_rows - codes.shape[0]), (0, LANES - own_rows)))
    sent = jnp.concatenate([queries[0], codes.astype(bf16)], axis=1)
    passages_other = shift(passages, "core", 1)
    query = lax.all_to_all(
        jnp.broadcast_to(sent[None], (chips,) + sent.shape), CHIPS, 0, 0, tiled=True
    ).reshape(rows, depth + LANES)

    table = pl.pallas_call(
        teacher_kernel,
        out_shape=jax.ShapeDtypeStruct((PIECES, block_rows, teacher.shape[1]), bf16),
        in_specs=[VMEM],
        out_specs=VMEM,
        compiler_params=PARAMS,
        cost_estimate=pl.CostEstimate(flops=10**11, bytes_accessed=2**21, transcendentals=0),
    )(teacher[0])
    table_other = shift(table, "core", 1)
    logits, positive, stats = pl.pallas_call(
        score_kernel,
        out_shape=(
            jax.ShapeDtypeStruct((2 * CORES, block_rows, rows), f32),
            jax.ShapeDtypeStruct((1, rows), i32),
            jax.ShapeDtypeStruct((chips, STATS, rows), f32),
        ),
        in_specs=[SMEM] + [VMEM] * 5,
        out_specs=(VMEM,) * 3,
        compiler_params=PARAMS,
    )(places, query, passages, passages_other, table, table_other)
    width = depth // x_size
    columns = pl.pallas_call(
        slice_kernel,
        out_shape=jax.ShapeDtypeStruct((rows, width), bf16),
        in_specs=[SMEM, VMEM],
        out_specs=VMEM,
        compiler_params=PARAMS,
    )(places, query)
    columns = shift(columns, "x", x_size // 2)
    stats = lax.all_to_all(stats, CHIPS, 0, 0, tiled=True)
    rows_first, grads, losses = pl.pallas_call(
        grad_kernel,
        out_shape=(
            jax.ShapeDtypeStruct((CORES, rows, block_rows), bf16),
            jax.ShapeDtypeStruct((wide, rows), bf16),
            jax.ShapeDtypeStruct((1, rows), f32),
        ),
        in_specs=[SMEM] + [VMEM] * 3 + [ANY],
        out_specs=(VMEM,) * 3,
        compiler_params=PARAMS,
    )(places, logits, positive, stats, columns)
    loss = lax.dynamic_slice_in_dim(losses[0], chip * own_rows, own_rows)

    query_part = pl.pallas_call(
        query_kernel,
        out_shape=jax.ShapeDtypeStruct((rows, depth), bf16),
        in_specs=[VMEM] * 3,
        out_specs=VMEM,
        compiler_params=PARAMS,
    )(rows_first, passages, passages_other)
    query_parts = lax.all_to_all(query_part.reshape(chips, own_rows, depth), CHIPS, 0, 0, tiled=True)

    tall = wide * rows // width
    packed = pl.pallas_call(
        pack_kernel,
        out_shape=tuple(
            jax.ShapeDtypeStruct((tall if d == x_size // 2 else rows + tall, width), bf16) for d in range(x_size)
        ),
        in_specs=[SMEM, VMEM, VMEM, ANY],
        out_specs=(VMEM,) * x_size,
        compiler_params=PARAMS,
    )(places, query, grads, query_part)
    packed = shifts(packed, "x")
    part_other = pl.pallas_call(
        functools.partial(other_kernel, rows),
        out_shape=jax.ShapeDtypeStruct((block_rows, width), bf16),
        in_specs=[VMEM] * (x_size + 1),
        out_specs=VMEM,
        compiler_params=PARAMS,
    )(*packed, columns)
    parts = pl.pallas_call(
        functools.partial(own_kernel, x_size, rows),
        out_shape=(jax.ShapeDtypeStruct((block_rows, width // yh_size), bf16),) * yh_size,
        in_specs=[SMEM] + [VMEM] * (x_size + 2),
        out_specs=(VMEM,) * yh_size,
        scratch_shapes=[pltpu.VMEM((block_rows, width), bf16)],
        compiler_params=PARAMS,
    )(places, *packed, columns, shift(part_other, "core", 1))
    parts = shifts(parts, "yh")
    query_total, passage_total = pl.pallas_call(
        sum_kernel,
        out_shape=(
            jax.ShapeDtypeStruct((own_rows, depth), bf16),
            jax.ShapeDtypeStruct(parts[0].shape, bf16),
        ),
        in_specs=[VMEM] * (1 + yh_size),
        out_specs=(VMEM,) * 2,
        compiler_params=PARAMS,
    )(query_parts, *parts)
    return loss[None], query_total[None], passage_total


def solution(mesh):
    blk, qgroup = mesh.devices.shape
    split = Mesh(
        mesh.devices.reshape(YL, blk // (YL * CORES), CORES, X, qgroup // X),
        ("yl", "z", "core", "x", "yh"),
    )
    blk, qgroup = ("yl", "z", "core"), ("x", "yh")
    in_specs = (
        P(qgroup, blk, None),
        P(blk, None),
        P(qgroup, None, blk),
        P(qgroup, blk),
        P(qgroup, blk),
    )
    out_specs = (P(qgroup, blk), P(qgroup, blk, None), P(blk, qgroup))
    return jax.shard_map(per_device, mesh=split, in_specs=in_specs, out_specs=out_specs, check_vma=False)
```

```python
import functools

import jax
import jax.numpy as jnp
from jax import lax
from jax.experimental import pallas as pl
from jax.experimental.pallas import tpu as pltpu
from jax.sharding import Mesh, PartitionSpec as P

inv_temp = 50.0
YL, ZL, CORES, X = 2, 2, 2, 4
LANES = 128
STATS = 8
PIECES = 3
NEAR, FAR = ("yl", "zl"), ("zh",)
CHIPS = NEAR + FAR
f32, bf16, i32 = jnp.float32, jnp.bfloat16, jnp.int32
VMEM = pl.BlockSpec(memory_space=pltpu.VMEM)
ANY = pl.BlockSpec(memory_space=pl.ANY)
SMEM = pl.BlockSpec(memory_space=pltpu.SMEM)
PARAMS = pltpu.CompilerParams(vmem_limit_bytes=16 * 1024 * 1024)


def shift(value, axis, by):
    if by == 0:
        return value
    size = lax.axis_size(axis)
    return lax.ppermute(value, axis, [(i, (i + by) % size) for i in range(size)])


def shifts(values, axis):
    size = len(values)
    order = sorted(range(size), key=lambda d: -min(d, size - d))
    moved = {d: shift(values[d], axis, d) for d in order}
    return [moved[d] for d in range(size)]


def hits(positive, place, shape):
    return lax.broadcasted_iota(i32, shape, 0) + place == positive


def teacher_kernel(teacher, out):
    rest = teacher[...].T
    for i in range(PIECES):
        piece = rest.astype(bf16)
        out[i] = piece
        rest = rest - piece.astype(f32)


def indices(codes, own_rows):
    rows, lanes = codes.shape
    first, second = (lax.broadcasted_iota(i32, (lanes, rows), k) for k in (0, 1))
    spread = (lax.rem(second, own_rows) == first).astype(f32).astype(bf16)
    spread = jnp.dot(codes, spread, preferred_element_type=f32)
    first, second = (lax.broadcasted_iota(i32, (rows, rows), k) for k in (0, 1))
    begin = second - lax.rem(second, own_rows)
    return [
        jnp.sum(jnp.where(first == begin + kind, spread, 0.0), axis=0, keepdims=True).astype(i32) for kind in range(3)
    ]


def score_kernel(places, query, passages, passages_other, teacher, teacher_other, values, positives, stats):
    depth = passages.shape[1]
    rows = query.shape[0]
    row_index, low, high = indices(query[:, depth:], rows // stats.shape[0])
    positive = low + 256 * high
    positives[...] = positive
    pick = (lax.broadcasted_iota(i32, (teacher.shape[2], rows), 0) == row_index).astype(f32).astype(bf16)
    parts = []
    for half, (block, table) in enumerate(((passages, teacher), (passages_other, teacher_other))):
        s = inv_temp * lax.dot_general(
            block[...], query[:, :depth], (((1,), (1,)), ((), ())), preferred_element_type=f32
        )
        t = sum(jnp.dot(table[i], pick, preferred_element_type=f32) for i in range(PIECES))
        values[half] = s
        values[CORES + half] = t
        parts.append((s, t, hits(positive, places[half], s.shape)))
    top_s, top_t = (jnp.maximum(*[jnp.max(p[i], axis=0, keepdims=True) for p in parts]) for i in (0, 1))
    sums = []
    for s, t, hot in parts:
        below_s, below_t = s - top_s, t - top_t
        weight = jnp.exp(below_t)
        terms = (jnp.exp(below_s), weight, weight * (below_t - below_s), jnp.where(hot, s, 0.0))
        sums.append([jnp.sum(v, axis=0, keepdims=True) for v in terms])
    sums = [a + b for a, b in zip(*sums)]
    whole = jnp.concatenate([top_s, top_t] + sums + [jnp.zeros((STATS - 6, rows), f32)], axis=0)
    stats[...] = jnp.broadcast_to(whole[None], stats.shape)


def grad_kernel(places, query, logits, positives, stats, rows_first, losses, packed):
    rows, width = query.shape[0], packed.shape[2]
    for x in range(packed.shape[0]):
        packed[x, :rows] = query[:, x * width : (x + 1) * width]
    tall = packed.shape[1] - rows
    tops_s, tops_t, sums_s, sums_t, cross, hit = (stats[:, i, :] for i in range(6))
    top_s, top_t = jnp.max(tops_s, axis=0, keepdims=True), jnp.max(tops_t, axis=0, keepdims=True)
    lower_s, lower_t = tops_s - top_s, tops_t - top_t
    total_s = jnp.sum(jnp.exp(lower_s) * sums_s, axis=0, keepdims=True)
    weight_t = jnp.exp(lower_t)
    total_t = jnp.sum(weight_t * sums_t, axis=0, keepdims=True)
    cross = jnp.sum(weight_t * (cross + (lower_t - lower_s) * sums_t), axis=0, keepdims=True)
    log_s = jnp.log(total_s)
    own = jnp.sum(hit, axis=0, keepdims=True)
    losses[...] = cross / total_t - jnp.log(total_t) + log_s - (own - top_s - log_s)
    scale_s, scale_t = 2.0 * inv_temp / total_s, inv_temp / total_t
    block_rows = logits.shape[1]
    for half in range(CORES):
        hot = hits(positives[...], places[half], logits.shape[1:])
        values = (
            jnp.exp(logits[half] - top_s) * scale_s
            - jnp.exp(logits[CORES + half] - top_t) * scale_t
            - jnp.where(hot, inv_temp, 0.0)
        )
        rows_first[half] = values.T.astype(bf16)
        values = values.astype(bf16)
        steps = block_rows // tall
        for k in range(steps):
            lane = (half * steps + k) * rows
            for x in range(packed.shape[0]):
                packed[x, rows:, lane : lane + rows] = values[k * tall : (k + 1) * tall]


def query_kernel(places, grads, passages, passages_other, total, *outs):
    result = jnp.dot(grads[0], passages[...], preferred_element_type=f32)
    result += jnp.dot(grads[1], passages_other[...], preferred_element_type=f32)
    total[...] = result.astype(bf16).reshape(total.shape)
    for d, out in enumerate(outs):
        out[...] = total[places[4] ^ d]


def products(packed, half, block_rows, rows):
    tall = packed.shape[1] - rows
    total = 0.0
    for x in range(packed.shape[0]):
        steps = block_rows // tall
        grads = jnp.concatenate(
            [packed[x, rows:, k * rows : (k + 1) * rows] for k in range(half * steps, (half + 1) * steps)], axis=0
        )
        total += jnp.dot(grads, packed[x, :rows], preferred_element_type=f32)
    return total


def other_kernel(rows, packed, out):
    out[...] = products(packed, 1, out.shape[0], rows).astype(bf16)


def own_kernel(rows, places, packed, back, after, *refs):
    del after
    *outs, total = refs
    width = outs[0].shape[1]
    total[...] = (products(packed, 0, back.shape[0], rows) + back[...].astype(f32)).astype(bf16)
    for d, out in enumerate(outs):
        out[...] = total[:, pl.ds(pl.multiple_of(lax.rem(places[3] + d, len(outs)) * width, width), width)]


def near_kernel(*refs):
    *parts, out = refs
    out[...] = sum(part[...].astype(f32) for part in parts).astype(bf16)


def sum_kernel(query_parts, *refs):
    parts, query_total, total = refs[:-2], refs[-2], refs[-1]
    query_total[...] = sum(query_parts[i].astype(f32) for i in range(query_parts.shape[0])).astype(bf16)
    total[...] = sum(part[...].astype(f32) for part in parts).astype(bf16)


def per_device(queries, passages, teacher, teacher_rows, positives):
    own_rows, depth = queries.shape[1:]
    block_rows = passages.shape[0]
    yl, zh, zl = (lax.axis_index(axis) for axis in ("yl", "zh", "zl"))
    far_size, zl_size = lax.axis_size("zh"), lax.axis_size("zl")
    near_size = lax.axis_size("yl") * zl_size
    chips = near_size * far_size
    x_size, yh_size = lax.axis_size("x"), lax.axis_size("yh")
    rows, wide = chips * own_rows, CORES * block_rows
    near = yl * zl_size + zl
    chip, block = near * far_size + zh, (yl * far_size + zh) * zl_size + zl
    core, x, yh = lax.axis_index("core"), lax.axis_index("x"), lax.axis_index("yh")
    places = jnp.stack(
        [(block * CORES + core) * block_rows, (block * CORES + 1 - core) * block_rows, x, yh, near]
    ).astype(i32)

    codes = jnp.concatenate([teacher_rows, positives & 255, lax.shift_right_logical(positives, 8)], axis=0)
    codes = jnp.pad(codes, ((0, own_rows - codes.shape[0]), (0, LANES - own_rows)))
    sent = jnp.concatenate([queries[0], codes.astype(bf16)], axis=1)
    passages_other = shift(passages, "core", 1)
    query = lax.all_to_all(
        jnp.broadcast_to(sent[None], (chips,) + sent.shape), CHIPS, 0, 0, tiled=True
    ).reshape(rows, depth + LANES)

    table = pl.pallas_call(
        teacher_kernel,
        out_shape=jax.ShapeDtypeStruct((PIECES, block_rows, teacher.shape[1]), bf16),
        in_specs=[VMEM],
        out_specs=VMEM,
        compiler_params=PARAMS,
        cost_estimate=pl.CostEstimate(flops=10**11, bytes_accessed=2**21, transcendentals=0),
    )(teacher[0])
    table_other = shift(table, "core", 1)
    logits, positive, stats = pl.pallas_call(
        score_kernel,
        out_shape=(
            jax.ShapeDtypeStruct((2 * CORES, block_rows, rows), f32),
            jax.ShapeDtypeStruct((1, rows), i32),
            jax.ShapeDtypeStruct((chips, STATS, rows), f32),
        ),
        in_specs=[SMEM] + [VMEM] * 5,
        out_specs=(VMEM,) * 3,
        compiler_params=PARAMS,
    )(places, query, passages, passages_other, table, table_other)
    stats = lax.all_to_all(stats, CHIPS, 0, 0, tiled=True)
    width = depth // x_size
    rows_first, losses, packed = pl.pallas_call(
        grad_kernel,
        out_shape=(
            jax.ShapeDtypeStruct((CORES, rows, block_rows), bf16),
            jax.ShapeDtypeStruct((1, rows), f32),
            jax.ShapeDtypeStruct((x_size, rows + wide * rows // width, width), bf16),
        ),
        in_specs=[SMEM] + [VMEM] * 4,
        out_specs=(VMEM,) * 3,
        compiler_params=PARAMS,
    )(places, query, logits, positive, stats)
    loss = lax.dynamic_slice_in_dim(losses[0], chip * own_rows, own_rows)

    width = depth // x_size
    packed = lax.all_to_all(packed, "x", 0, 0, tiled=True)
    _, *query_parts = pl.pallas_call(
        query_kernel,
        out_shape=(jax.ShapeDtypeStruct((near_size, rows // near_size, depth), bf16),)
        + (jax.ShapeDtypeStruct((rows // near_size, depth), bf16),) * near_size,
        in_specs=[SMEM] + [VMEM] * 3,
        out_specs=(VMEM,) * (1 + near_size),
        compiler_params=PARAMS,
    )(places, rows_first, passages, passages_other)
    query_parts = [
        lax.ppermute(part, NEAR, [(i, i ^ d) for i in range(near_size)]) if d else part
        for d, part in enumerate(query_parts)
    ]
    part_other = pl.pallas_call(
        functools.partial(other_kernel, rows),
        out_shape=jax.ShapeDtypeStruct((block_rows, width), bf16),
        in_specs=[VMEM],
        out_specs=VMEM,
        compiler_params=PARAMS,
    )(packed)
    query_part = pl.pallas_call(
        near_kernel,
        out_shape=jax.ShapeDtypeStruct((rows // near_size, depth), bf16),
        in_specs=[VMEM] * near_size,
        out_specs=VMEM,
        compiler_params=PARAMS,
    )(*query_parts)
    query_parts = lax.all_to_all(query_part.reshape(far_size, own_rows, depth), FAR, 0, 0, tiled=True)
    parts = pl.pallas_call(
        functools.partial(own_kernel, rows),
        out_shape=(jax.ShapeDtypeStruct((block_rows, width // yh_size), bf16),) * yh_size,
        in_specs=[SMEM] + [VMEM] * 2 + [ANY],
        out_specs=(VMEM,) * yh_size,
        scratch_shapes=[pltpu.VMEM((block_rows, width), bf16)],
        compiler_params=PARAMS,
    )(places, packed, shift(part_other, "core", 1), query_part)
    parts = shifts(parts, "yh")
    query_total, passage_total = pl.pallas_call(
        sum_kernel,
        out_shape=(
            jax.ShapeDtypeStruct((own_rows, depth), bf16),
            jax.ShapeDtypeStruct(parts[0].shape, bf16),
        ),
        in_specs=[VMEM] * (1 + yh_size),
        out_specs=(VMEM,) * 2,
        compiler_params=PARAMS,
    )(query_parts, *parts)
    return loss[None], query_total[None], passage_total


def solution(mesh):
    blk, qgroup = mesh.devices.shape
    split = Mesh(
        mesh.devices.reshape(YL, blk // (YL * ZL * CORES), ZL, CORES, X, qgroup // X),
        ("yl", "zh", "zl", "core", "x", "yh"),
    )
    blk, qgroup = ("yl", "zh", "zl", "core"), ("x", "yh")
    in_specs = (
        P(qgroup, blk, None),
        P(blk, None),
        P(qgroup, None, blk),
        P(qgroup, blk),
        P(qgroup, blk),
    )
    out_specs = (P(qgroup, blk), P(qgroup, blk, None), P(blk, qgroup))
    return jax.shard_map(per_device, mesh=split, in_specs=in_specs, out_specs=out_specs, check_vma=False)
```

```python
import functools

import jax
import jax.numpy as jnp
from jax import lax
from jax.experimental import pallas as pl
from jax.experimental.pallas import tpu as pltpu
from jax.sharding import Mesh, PartitionSpec as P

inv_temp = 50.0
YL, CORES, X = 2, 2, 4
LANES = 128
STATS = 8
PIECES = 3
CHIPS = ("yl", "z")
f32, bf16, i32 = jnp.float32, jnp.bfloat16, jnp.int32
VMEM = pl.BlockSpec(memory_space=pltpu.VMEM)
ANY = pl.BlockSpec(memory_space=pl.ANY)
SMEM = pl.BlockSpec(memory_space=pltpu.SMEM)
PARAMS = pltpu.CompilerParams(vmem_limit_bytes=16 * 1024 * 1024)


def shift(value, axis, by):
    if by == 0:
        return value
    size = lax.axis_size(axis)
    return lax.ppermute(value, axis, [(i, (i + by) % size) for i in range(size)])


def shifts(values, axis):
    size = len(values)
    order = sorted(range(size), key=lambda d: -min(d, size - d))
    moved = {d: shift(values[d], axis, d) for d in order}
    return [moved[d] for d in range(size)]


def hits(positive, place, shape):
    return lax.broadcasted_iota(i32, shape, 0) + place == positive


def teacher_kernel(teacher, out):
    rest = teacher[...].T
    for i in range(PIECES):
        piece = rest.astype(bf16)
        out[i] = piece
        rest = rest - piece.astype(f32)


def indices(codes, own_rows):
    rows, lanes = codes.shape
    first, second = (lax.broadcasted_iota(i32, (lanes, rows), k) for k in (0, 1))
    spread = (lax.rem(second, own_rows) == first).astype(f32).astype(bf16)
    spread = jnp.dot(codes, spread, preferred_element_type=f32)
    first, second = (lax.broadcasted_iota(i32, (rows, rows), k) for k in (0, 1))
    begin = second - lax.rem(second, own_rows)
    return [
        jnp.sum(jnp.where(first == begin + kind, spread, 0.0), axis=0, keepdims=True).astype(i32) for kind in range(3)
    ]


def score_kernel(places, query, passages, passages_other, teacher, teacher_other, values, positives, stats):
    depth = passages.shape[1]
    rows = query.shape[0]
    row_index, low, high = indices(query[:, depth:], rows // stats.shape[0])
    positive = low + 256 * high
    positives[...] = positive
    pick = (lax.broadcasted_iota(i32, (teacher.shape[2], rows), 0) == row_index).astype(f32).astype(bf16)
    parts = []
    for half, (block, table) in enumerate(((passages, teacher), (passages_other, teacher_other))):
        s = inv_temp * lax.dot_general(
            block[...], query[:, :depth], (((1,), (1,)), ((), ())), preferred_element_type=f32
        )
        t = sum(jnp.dot(table[i], pick, preferred_element_type=f32) for i in range(PIECES))
        values[half] = s
        values[CORES + half] = t
        parts.append((s, t, hits(positive, places[half], s.shape)))
    top_s, top_t = (jnp.maximum(*[jnp.max(p[i], axis=0, keepdims=True) for p in parts]) for i in (0, 1))
    sums = []
    for s, t, hot in parts:
        below_s, below_t = s - top_s, t - top_t
        weight = jnp.exp(below_t)
        terms = (jnp.exp(below_s), weight, weight * (below_t - below_s), jnp.where(hot, s, 0.0))
        sums.append([jnp.sum(v, axis=0, keepdims=True) for v in terms])
    sums = [a + b for a, b in zip(*sums)]
    whole = jnp.concatenate([top_s, top_t] + sums + [jnp.zeros((STATS - 6, rows), f32)], axis=0)
    stats[...] = jnp.broadcast_to(whole[None], stats.shape)


def grad_kernel(places, query, logits, positives, stats, grads, losses, *packed):
    rows, width = query.shape[0], packed[0].shape[1]
    for d, out in enumerate(packed):
        out[:rows] = query[:, pl.ds(pl.multiple_of(lax.rem(places[2] + d, len(packed)) * width, width), width)]
    tall = packed[0].shape[0] - rows
    tops_s, tops_t, sums_s, sums_t, cross, hit = (stats[:, i, :] for i in range(6))
    top_s, top_t = jnp.max(tops_s, axis=0, keepdims=True), jnp.max(tops_t, axis=0, keepdims=True)
    lower_s, lower_t = tops_s - top_s, tops_t - top_t
    total_s = jnp.sum(jnp.exp(lower_s) * sums_s, axis=0, keepdims=True)
    weight_t = jnp.exp(lower_t)
    total_t = jnp.sum(weight_t * sums_t, axis=0, keepdims=True)
    cross = jnp.sum(weight_t * (cross + (lower_t - lower_s) * sums_t), axis=0, keepdims=True)
    log_s = jnp.log(total_s)
    own = jnp.sum(hit, axis=0, keepdims=True)
    losses[...] = cross / total_t - jnp.log(total_t) + log_s - (own - top_s - log_s)
    scale_s, scale_t = 2.0 * inv_temp / total_s, inv_temp / total_t
    block_rows = logits.shape[1]
    for half in range(CORES):
        hot = hits(positives[...], places[half], logits.shape[1:])
        values = (
            jnp.exp(logits[half] - top_s) * scale_s
            - jnp.exp(logits[CORES + half] - top_t) * scale_t
            - jnp.where(hot, inv_temp, 0.0)
        )
        values = values.astype(bf16)
        grads[half] = values
        steps = block_rows // tall
        for k in range(steps):
            lane = (half * steps + k) * rows
            for out in packed:
                out[rows:, lane : lane + rows] = values[k * tall : (k + 1) * tall]


def query_kernel(grads, passages, passages_other, after, out):
    del after
    total = 0.0
    for half, block in enumerate((passages, passages_other)):
        total += lax.dot_general(grads[half], block[...], (((0,), (0,)), ((), ())), preferred_element_type=f32)
    out[...] = total.astype(bf16)


def products(packed, half, block_rows, rows):
    tall = packed[0].shape[0] - rows
    total = 0.0
    for ref in packed:
        steps = block_rows // tall
        grads = jnp.concatenate(
            [ref[rows:, k * rows : (k + 1) * rows] for k in range(half * steps, (half + 1) * steps)], axis=0
        )
        total += jnp.dot(grads, ref[:rows], preferred_element_type=f32)
    return total


def other_kernel(rows, *refs):
    out = refs[-1]
    out[...] = products(refs[:-1], 1, out.shape[0], rows).astype(bf16)


def own_kernel(groups, rows, places, *refs):
    packed, back, outs, total = refs[:groups], refs[groups], refs[groups + 1 : -1], refs[-1]
    width = outs[0].shape[1]
    total[...] = (products(packed, 0, back.shape[0], rows) + back[...].astype(f32)).astype(bf16)
    for d, out in enumerate(outs):
        out[...] = total[:, pl.ds(pl.multiple_of(lax.rem(places[3] + d, len(outs)) * width, width), width)]


def sum_kernel(query_parts, *refs):
    parts, query_total, total = refs[:-2], refs[-2], refs[-1]
    query_total[...] = sum(query_parts[i].astype(f32) for i in range(query_parts.shape[0])).astype(bf16)
    total[...] = sum(part[...].astype(f32) for part in parts).astype(bf16)


def per_device(queries, passages, teacher, teacher_rows, positives):
    own_rows, depth = queries.shape[1:]
    block_rows = passages.shape[0]
    chips = lax.axis_size("yl") * lax.axis_size("z")
    x_size, yh_size = lax.axis_size("x"), lax.axis_size("yh")
    rows, wide = chips * own_rows, CORES * block_rows
    chip = lax.axis_index("yl") * lax.axis_size("z") + lax.axis_index("z")
    core, x, yh = lax.axis_index("core"), lax.axis_index("x"), lax.axis_index("yh")
    places = jnp.stack(
        [(chip * CORES + core) * block_rows, (chip * CORES + 1 - core) * block_rows, x, yh]
    ).astype(i32)

    codes = jnp.concatenate([teacher_rows & 255, positives & 255, lax.shift_right_logical(positives, 8) & 255], axis=0)
    codes = jnp.pad(codes, ((0, own_rows - codes.shape[0]), (0, LANES - own_rows)))
    sent = jnp.concatenate([queries[0], codes.astype(bf16)], axis=1)
    passages_other = shift(passages, "core", 1)
    query = lax.all_to_all(
        jnp.broadcast_to(sent[None], (chips,) + sent.shape), CHIPS, 0, 0, tiled=True
    ).reshape(rows, depth + LANES)

    table = pl.pallas_call(
        teacher_kernel,
        out_shape=jax.ShapeDtypeStruct((PIECES, block_rows, teacher.shape[1]), bf16),
        in_specs=[VMEM],
        out_specs=VMEM,
        compiler_params=PARAMS,
        cost_estimate=pl.CostEstimate(flops=10**11, bytes_accessed=2**21, transcendentals=0),
    )(teacher[0])
    table_other = shift(table, "core", 1)
    logits, positive, stats = pl.pallas_call(
        score_kernel,
        out_shape=(
            jax.ShapeDtypeStruct((2 * CORES, block_rows, rows), f32),
            jax.ShapeDtypeStruct((1, rows), i32),
            jax.ShapeDtypeStruct((chips, STATS, rows), f32),
        ),
        in_specs=[SMEM] + [VMEM] * 5,
        out_specs=(VMEM,) * 3,
        compiler_params=PARAMS,
    )(places, query, passages, passages_other, table, table_other)
    stats = lax.all_to_all(stats, CHIPS, 0, 0, tiled=True)
    width = depth // x_size
    grads, losses, *packed = pl.pallas_call(
        grad_kernel,
        out_shape=(
            jax.ShapeDtypeStruct((CORES, block_rows, rows), bf16),
            jax.ShapeDtypeStruct((1, rows), f32),
        )
        + (jax.ShapeDtypeStruct((rows + wide * rows // width, width), bf16),) * x_size,
        in_specs=[SMEM] + [VMEM] * 4,
        out_specs=(VMEM,) * (2 + x_size),
        compiler_params=PARAMS,
    )(places, query, logits, positive, stats)
    loss = lax.dynamic_slice_in_dim(losses[0], chip * own_rows, own_rows)

    width = depth // x_size
    query_part = pl.pallas_call(
        query_kernel,
        out_shape=jax.ShapeDtypeStruct((rows, depth), bf16),
        in_specs=[VMEM] * 3 + [ANY],
        out_specs=VMEM,
        compiler_params=PARAMS,
    )(grads, passages, passages_other, packed[0])
    query_parts = lax.all_to_all(query_part.reshape(chips, own_rows, depth), CHIPS, 0, 0, tiled=True)
    packed = shifts(packed, "x")
    part_other = pl.pallas_call(
        functools.partial(other_kernel, rows),
        out_shape=jax.ShapeDtypeStruct((block_rows, width), bf16),
        in_specs=[VMEM] * x_size,
        out_specs=VMEM,
        compiler_params=PARAMS,
        cost_estimate=pl.CostEstimate(flops=10**11, bytes_accessed=2**21, transcendentals=0),
    )(*packed)
    parts = pl.pallas_call(
        functools.partial(own_kernel, x_size, rows),
        out_shape=(jax.ShapeDtypeStruct((block_rows, width // yh_size), bf16),) * yh_size,
        in_specs=[SMEM] + [VMEM] * (x_size + 1),
        out_specs=(VMEM,) * yh_size,
        scratch_shapes=[pltpu.VMEM((block_rows, width), bf16)],
        compiler_params=PARAMS,
    )(places, *packed, shift(part_other, "core", 1))
    parts = shifts(parts, "yh")
    query_total, passage_total = pl.pallas_call(
        sum_kernel,
        out_shape=(
            jax.ShapeDtypeStruct((own_rows, depth), bf16),
            jax.ShapeDtypeStruct(parts[0].shape, bf16),
        ),
        in_specs=[VMEM] * (1 + yh_size),
        out_specs=(VMEM,) * 2,
        compiler_params=PARAMS,
    )(query_parts, *parts)
    return loss[None], query_total[None], passage_total


def solution(mesh):
    blk, qgroup = mesh.devices.shape
    split = Mesh(
        mesh.devices.reshape(YL, blk // (YL * CORES), CORES, X, qgroup // X),
        ("yl", "z", "core", "x", "yh"),
    )
    blk, qgroup = ("yl", "z", "core"), ("x", "yh")
    in_specs = (
        P(qgroup, blk, None),
        P(blk, None),
        P(qgroup, None, blk),
        P(qgroup, blk),
        P(qgroup, blk),
    )
    out_specs = (P(qgroup, blk), P(qgroup, blk, None), P(blk, qgroup))
    return jax.shard_map(per_device, mesh=split, in_specs=in_specs, out_specs=out_specs, check_vma=False)
```

```python
import functools

import jax
import jax.numpy as jnp
from jax import lax
from jax.experimental import pallas as pl
from jax.experimental.pallas import tpu as pltpu
from jax.sharding import Mesh, PartitionSpec as P

inv_temp = 50.0
YL, CORES, X = 2, 2, 4
LANES = 128
STATS = 8
PIECES = 3
CHIPS = ("yl", "z")
f32, bf16, i32 = jnp.float32, jnp.bfloat16, jnp.int32
VMEM = pl.BlockSpec(memory_space=pltpu.VMEM)
ANY = pl.BlockSpec(memory_space=pl.ANY)
SMEM = pl.BlockSpec(memory_space=pltpu.SMEM)
PARAMS = pltpu.CompilerParams(vmem_limit_bytes=16 * 1024 * 1024)


def shift(value, axis, by):
    if by == 0:
        return value
    size = lax.axis_size(axis)
    return lax.ppermute(value, axis, [(i, (i + by) % size) for i in range(size)])


def shifts(values, axis):
    size = len(values)
    order = sorted(range(size), key=lambda d: (-min(d, size - d), -d))
    return [shift(values[d], axis, d) for d in order]


def hits(positive, place, shape):
    return lax.broadcasted_iota(i32, shape, 0) + place == positive


def teacher_kernel(teacher, out):
    rest = teacher[...].T
    for i in range(PIECES):
        piece = rest.astype(bf16)
        out[i] = piece
        rest = rest - piece.astype(f32)


def indices(codes, own_rows):
    rows, lanes = codes.shape
    first, second = (lax.broadcasted_iota(i32, (lanes, rows), k) for k in (0, 1))
    spread = (lax.rem(second, own_rows) == first).astype(f32).astype(bf16)
    spread = jnp.dot(codes, spread, preferred_element_type=f32)
    first, second = (lax.broadcasted_iota(i32, (rows, rows), k) for k in (0, 1))
    begin = second - lax.rem(second, own_rows)
    return [
        jnp.sum(jnp.where(first == begin + kind, spread, 0.0), axis=0, keepdims=True).astype(i32) for kind in range(3)
    ]


def score_kernel(places, query, passages, passages_other, teacher, teacher_other, values, positives, stats):
    depth = passages.shape[1]
    rows = query.shape[0]
    row_index, low, high = indices(query[:, depth:], rows // stats.shape[0])
    positive = low + 256 * high
    positives[...] = positive
    pick = (lax.broadcasted_iota(i32, (teacher.shape[2], rows), 0) == row_index).astype(f32).astype(bf16)
    parts = []
    for half, (block, table) in enumerate(((passages, teacher), (passages_other, teacher_other))):
        s = inv_temp * lax.dot_general(
            block[...], query[:, :depth], (((1,), (1,)), ((), ())), preferred_element_type=f32
        )
        t = sum(jnp.dot(table[i], pick, preferred_element_type=f32) for i in range(PIECES))
        values[half] = s
        values[CORES + half] = t
        parts.append((s, t, hits(positive, places[half], s.shape)))
    top_s, top_t = (jnp.maximum(*[jnp.max(p[i], axis=0, keepdims=True) for p in parts]) for i in (0, 1))
    sums = []
    for s, t, hot in parts:
        below_s, below_t = s - top_s, t - top_t
        weight = jnp.exp(below_t)
        terms = (jnp.exp(below_s), weight, weight * (below_t - below_s), jnp.where(hot, s, 0.0))
        sums.append([jnp.sum(v, axis=0, keepdims=True) for v in terms])
    sums = [a + b for a, b in zip(*sums)]
    whole = jnp.concatenate([top_s, top_t] + sums + [jnp.zeros((STATS - 6, rows), f32)], axis=0)
    stats[...] = jnp.broadcast_to(whole[None], stats.shape)


def grad_kernel(places, query, logits, positives, stats, grads, losses, *packed):
    rows, width = query.shape[0], packed[0].shape[1]
    for d, out in enumerate(packed):
        out[:rows] = query[:, pl.ds(pl.multiple_of(lax.rem(places[2] + d, len(packed)) * width, width), width)]
    tall = packed[0].shape[0] - rows
    tops_s, tops_t, sums_s, sums_t, cross, hit = (stats[:, i, :] for i in range(6))
    top_s, top_t = jnp.max(tops_s, axis=0, keepdims=True), jnp.max(tops_t, axis=0, keepdims=True)
    lower_s, lower_t = tops_s - top_s, tops_t - top_t
    total_s = jnp.sum(jnp.exp(lower_s) * sums_s, axis=0, keepdims=True)
    weight_t = jnp.exp(lower_t)
    total_t = jnp.sum(weight_t * sums_t, axis=0, keepdims=True)
    cross = jnp.sum(weight_t * (cross + (lower_t - lower_s) * sums_t), axis=0, keepdims=True)
    log_s = jnp.log(total_s)
    own = jnp.sum(hit, axis=0, keepdims=True)
    losses[...] = cross / total_t - jnp.log(total_t) + log_s - (own - top_s - log_s)
    scale_s, scale_t = 2.0 * inv_temp / total_s, inv_temp / total_t
    block_rows = logits.shape[1]
    for half in range(CORES):
        hot = hits(positives[...], places[half], logits.shape[1:])
        values = (
            jnp.exp(logits[half] - top_s) * scale_s
            - jnp.exp(logits[CORES + half] - top_t) * scale_t
            - jnp.where(hot, inv_temp, 0.0)
        )
        values = values.astype(bf16)
        grads[half] = values
        steps = block_rows // tall
        for k in range(steps):
            lane = (half * steps + k) * rows
            for out in packed:
                out[rows:, lane : lane + rows] = values[k * tall : (k + 1) * tall]


def query_kernel(grads, passages, passages_other, after, out):
    del after
    total = 0.0
    for half, block in enumerate((passages, passages_other)):
        total += lax.dot_general(grads[half], block[...], (((0,), (0,)), ((), ())), preferred_element_type=f32)
    out[...] = total.astype(bf16)


def products(packed, half, block_rows, rows):
    tall = packed[0].shape[0] - rows
    total = 0.0
    for ref in packed:
        steps = block_rows // tall
        grads = jnp.concatenate(
            [ref[rows:, k * rows : (k + 1) * rows] for k in range(half * steps, (half + 1) * steps)], axis=0
        )
        total += jnp.dot(grads, ref[:rows], preferred_element_type=f32)
    return total


def other_kernel(rows, *refs):
    out = refs[-1]
    out[...] = products(refs[:-1], 1, out.shape[0], rows).astype(bf16)


def own_kernel(groups, rows, places, *refs):
    packed, back, outs, total = refs[:groups], refs[groups], refs[groups + 1 : -1], refs[-1]
    width = outs[0].shape[1]
    total[...] = (products(packed, 0, back.shape[0], rows) + back[...].astype(f32)).astype(bf16)
    for d, out in enumerate(outs):
        out[...] = total[:, pl.ds(pl.multiple_of(lax.rem(places[3] + d, len(outs)) * width, width), width)]


def sum_kernel(query_parts, *refs):
    parts, query_total, total = refs[:-2], refs[-2], refs[-1]
    query_total[...] = sum(query_parts[i].astype(f32) for i in range(query_parts.shape[0])).astype(bf16)
    total[...] = sum(part[...].astype(f32) for part in parts).astype(bf16)


def per_device(queries, passages, teacher, teacher_rows, positives):
    own_rows, depth = queries.shape[1:]
    block_rows = passages.shape[0]
    chips = lax.axis_size("yl") * lax.axis_size("z")
    x_size, yh_size = lax.axis_size("x"), lax.axis_size("yh")
    rows, wide = chips * own_rows, CORES * block_rows
    chip = lax.axis_index("yl") * lax.axis_size("z") + lax.axis_index("z")
    core, x, yh = lax.axis_index("core"), lax.axis_index("x"), lax.axis_index("yh")
    places = jnp.stack(
        [(chip * CORES + core) * block_rows, (chip * CORES + 1 - core) * block_rows, x, yh]
    ).astype(i32)

    codes = jnp.concatenate([teacher_rows & 255, positives & 255, lax.shift_right_logical(positives, 8) & 255], axis=0)
    codes = jnp.pad(codes, ((0, own_rows - codes.shape[0]), (0, LANES - own_rows)))
    sent = jnp.concatenate([queries[0], codes.astype(bf16)], axis=1)
    passages_other = shift(passages, "core", 1)
    query = lax.all_to_all(
        jnp.broadcast_to(sent[None], (chips,) + sent.shape), CHIPS, 0, 0, tiled=True
    ).reshape(rows, depth + LANES)

    table = pl.pallas_call(
        teacher_kernel,
        out_shape=jax.ShapeDtypeStruct((PIECES, block_rows, teacher.shape[1]), bf16),
        in_specs=[VMEM],
        out_specs=VMEM,
        compiler_params=PARAMS,
        cost_estimate=pl.CostEstimate(flops=10**11, bytes_accessed=2**21, transcendentals=0),
    )(teacher[0])
    table_other = shift(table, "core", 1)
    logits, positive, stats = pl.pallas_call(
        score_kernel,
        out_shape=(
            jax.ShapeDtypeStruct((2 * CORES, block_rows, rows), f32),
            jax.ShapeDtypeStruct((1, rows), i32),
            jax.ShapeDtypeStruct((chips, STATS, rows), f32),
        ),
        in_specs=[SMEM] + [VMEM] * 5,
        out_specs=(VMEM,) * 3,
        compiler_params=PARAMS,
    )(places, query, passages, passages_other, table, table_other)
    stats = lax.all_to_all(stats, CHIPS, 0, 0, tiled=True)
    width = depth // x_size
    grads, losses, *packed = pl.pallas_call(
        grad_kernel,
        out_shape=(
            jax.ShapeDtypeStruct((CORES, block_rows, rows), bf16),
            jax.ShapeDtypeStruct((1, rows), f32),
        )
        + (jax.ShapeDtypeStruct((rows + wide * rows // width, width), bf16),) * x_size,
        in_specs=[SMEM] + [VMEM] * 4,
        out_specs=(VMEM,) * (2 + x_size),
        compiler_params=PARAMS,
    )(places, query, logits, positive, stats)
    loss = lax.dynamic_slice_in_dim(losses[0], chip * own_rows, own_rows)

    width = depth // x_size
    query_part = pl.pallas_call(
        query_kernel,
        out_shape=jax.ShapeDtypeStruct((rows, depth), bf16),
        in_specs=[VMEM] * 3 + [ANY],
        out_specs=VMEM,
        compiler_params=PARAMS,
    )(grads, passages, passages_other, packed[0])
    query_parts = lax.all_to_all(query_part.reshape(chips, own_rows, depth), CHIPS, 0, 0, tiled=True)
    packed = shifts(packed, "x")
    part_other = pl.pallas_call(
        functools.partial(other_kernel, rows),
        out_shape=jax.ShapeDtypeStruct((block_rows, width), bf16),
        in_specs=[VMEM] * x_size,
        out_specs=VMEM,
        compiler_params=PARAMS,
        cost_estimate=pl.CostEstimate(flops=10**11, bytes_accessed=2**21, transcendentals=0),
    )(*packed)
    parts = pl.pallas_call(
        functools.partial(own_kernel, x_size, rows),
        out_shape=(jax.ShapeDtypeStruct((block_rows, width // yh_size), bf16),) * yh_size,
        in_specs=[SMEM] + [VMEM] * (x_size + 1),
        out_specs=(VMEM,) * yh_size,
        scratch_shapes=[pltpu.VMEM((block_rows, width), bf16)],
        compiler_params=PARAMS,
    )(places, *packed, shift(part_other, "core", 1))
    parts = shifts(parts, "yh")
    query_total, passage_total = pl.pallas_call(
        sum_kernel,
        out_shape=(
            jax.ShapeDtypeStruct((own_rows, depth), bf16),
            jax.ShapeDtypeStruct(parts[0].shape, bf16),
        ),
        in_specs=[VMEM] * (1 + yh_size),
        out_specs=(VMEM,) * 2,
        compiler_params=PARAMS,
    )(query_parts, *parts)
    return loss[None], query_total[None], passage_total


def solution(mesh):
    blk, qgroup = mesh.devices.shape
    split = Mesh(
        mesh.devices.reshape(YL, blk // (YL * CORES), CORES, X, qgroup // X),
        ("yl", "z", "core", "x", "yh"),
    )
    blk, qgroup = ("yl", "z", "core"), ("x", "yh")
    in_specs = (
        P(qgroup, blk, None),
        P(blk, None),
        P(qgroup, None, blk),
        P(qgroup, blk),
        P(qgroup, blk),
    )
    out_specs = (P(qgroup, blk), P(qgroup, blk, None), P(blk, qgroup))
    return jax.shard_map(per_device, mesh=split, in_specs=in_specs, out_specs=out_specs, check_vma=False)
```

```python
import functools

import jax
import jax.numpy as jnp
from jax import lax
from jax.experimental import pallas as pl
from jax.experimental.pallas import tpu as pltpu
from jax.sharding import Mesh, PartitionSpec as P

inv_temp = 50.0
YL, CORES, X = 2, 2, 4
LANES = 128
STATS = 8
PIECES = 3
CHIPS = ("yl", "z")
f32, bf16, i32 = jnp.float32, jnp.bfloat16, jnp.int32
VMEM = pl.BlockSpec(memory_space=pltpu.VMEM)
ANY = pl.BlockSpec(memory_space=pl.ANY)
SMEM = pl.BlockSpec(memory_space=pltpu.SMEM)
PARAMS = pltpu.CompilerParams(vmem_limit_bytes=16 * 1024 * 1024)


def shift(value, axis, by):
    if by == 0:
        return value
    size = lax.axis_size(axis)
    return lax.ppermute(value, axis, [(i, (i + by) % size) for i in range(size)])


def shifts(values, axis):
    size = len(values)
    order = list(reversed(range(size)))
    return [shift(values[d], axis, d) for d in order]


def hits(positive, place, shape):
    return lax.broadcasted_iota(i32, shape, 0) + place == positive


def teacher_kernel(teacher, out):
    rest = teacher[...].T
    for i in range(PIECES):
        piece = rest.astype(bf16)
        out[i] = piece
        rest = rest - piece.astype(f32)


def indices(codes, own_rows):
    rows, lanes = codes.shape
    first, second = (lax.broadcasted_iota(i32, (lanes, rows), k) for k in (0, 1))
    spread = (lax.rem(second, own_rows) == first).astype(f32).astype(bf16)
    spread = jnp.dot(codes, spread, preferred_element_type=f32)
    first, second = (lax.broadcasted_iota(i32, (rows, rows), k) for k in (0, 1))
    begin = second - lax.rem(second, own_rows)
    return [
        jnp.sum(jnp.where(first == begin + kind, spread, 0.0), axis=0, keepdims=True).astype(i32) for kind in range(3)
    ]


def score_kernel(places, query, passages, passages_other, teacher, teacher_other, values, positives, stats):
    depth = passages.shape[1]
    rows = query.shape[0]
    row_index, low, high = indices(query[:, depth:], rows // stats.shape[0])
    positive = low + 256 * high
    positives[...] = positive
    pick = (lax.broadcasted_iota(i32, (teacher.shape[2], rows), 0) == row_index).astype(f32).astype(bf16)
    parts = []
    for half, (block, table) in enumerate(((passages, teacher), (passages_other, teacher_other))):
        s = inv_temp * lax.dot_general(
            block[...], query[:, :depth], (((1,), (1,)), ((), ())), preferred_element_type=f32
        )
        t = sum(jnp.dot(table[i], pick, preferred_element_type=f32) for i in range(PIECES))
        values[half] = s
        values[CORES + half] = t
        parts.append((s, t, hits(positive, places[half], s.shape)))
    top_s, top_t = (jnp.maximum(*[jnp.max(p[i], axis=0, keepdims=True) for p in parts]) for i in (0, 1))
    sums = []
    for s, t, hot in parts:
        below_s, below_t = s - top_s, t - top_t
        weight = jnp.exp(below_t)
        terms = (jnp.exp(below_s), weight, weight * (below_t - below_s), jnp.where(hot, s, 0.0))
        sums.append([jnp.sum(v, axis=0, keepdims=True) for v in terms])
    sums = [a + b for a, b in zip(*sums)]
    whole = jnp.concatenate([top_s, top_t] + sums + [jnp.zeros((STATS - 6, rows), f32)], axis=0)
    stats[...] = jnp.broadcast_to(whole[None], stats.shape)


def grad_kernel(places, query, logits, positives, stats, grads, losses, *packed):
    rows, width = query.shape[0], packed[0].shape[1]
    for d, out in enumerate(packed):
        out[:rows] = query[:, pl.ds(pl.multiple_of(lax.rem(places[2] + d, len(packed)) * width, width), width)]
    tall = packed[0].shape[0] - rows
    tops_s, tops_t, sums_s, sums_t, cross, hit = (stats[:, i, :] for i in range(6))
    top_s, top_t = jnp.max(tops_s, axis=0, keepdims=True), jnp.max(tops_t, axis=0, keepdims=True)
    lower_s, lower_t = tops_s - top_s, tops_t - top_t
    total_s = jnp.sum(jnp.exp(lower_s) * sums_s, axis=0, keepdims=True)
    weight_t = jnp.exp(lower_t)
    total_t = jnp.sum(weight_t * sums_t, axis=0, keepdims=True)
    cross = jnp.sum(weight_t * (cross + (lower_t - lower_s) * sums_t), axis=0, keepdims=True)
    log_s = jnp.log(total_s)
    own = jnp.sum(hit, axis=0, keepdims=True)
    losses[...] = cross / total_t - jnp.log(total_t) + log_s - (own - top_s - log_s)
    scale_s, scale_t = 2.0 * inv_temp / total_s, inv_temp / total_t
    block_rows = logits.shape[1]
    for half in range(CORES):
        hot = hits(positives[...], places[half], logits.shape[1:])
        values = (
            jnp.exp(logits[half] - top_s) * scale_s
            - jnp.exp(logits[CORES + half] - top_t) * scale_t
            - jnp.where(hot, inv_temp, 0.0)
        )
        values = values.astype(bf16)
        grads[half] = values
        steps = block_rows // tall
        for k in range(steps):
            lane = (half * steps + k) * rows
            for out in packed:
                out[rows:, lane : lane + rows] = values[k * tall : (k + 1) * tall]


def query_kernel(grads, passages, passages_other, after, out):
    del after
    total = 0.0
    for half, block in enumerate((passages, passages_other)):
        total += lax.dot_general(grads[half], block[...], (((0,), (0,)), ((), ())), preferred_element_type=f32)
    out[...] = total.astype(bf16)


def products(packed, half, block_rows, rows):
    tall = packed[0].shape[0] - rows
    total = 0.0
    for ref in packed:
        steps = block_rows // tall
        grads = jnp.concatenate(
            [ref[rows:, k * rows : (k + 1) * rows] for k in range(half * steps, (half + 1) * steps)], axis=0
        )
        total += jnp.dot(grads, ref[:rows], preferred_element_type=f32)
    return total


def other_kernel(rows, *refs):
    out = refs[-1]
    out[...] = products(refs[:-1], 1, out.shape[0], rows).astype(bf16)


def own_kernel(groups, rows, places, *refs):
    packed, back, outs, total = refs[:groups], refs[groups], refs[groups + 1 : -1], refs[-1]
    width = outs[0].shape[1]
    total[...] = (products(packed, 0, back.shape[0], rows) + back[...].astype(f32)).astype(bf16)
    for d, out in enumerate(outs):
        out[...] = total[:, pl.ds(pl.multiple_of(lax.rem(places[3] + d, len(outs)) * width, width), width)]


def sum_kernel(query_parts, *refs):
    parts, query_total, total = refs[:-2], refs[-2], refs[-1]
    query_total[...] = sum(query_parts[i].astype(f32) for i in range(query_parts.shape[0])).astype(bf16)
    total[...] = sum(part[...].astype(f32) for part in parts).astype(bf16)


def per_device(queries, passages, teacher, teacher_rows, positives):
    own_rows, depth = queries.shape[1:]
    block_rows = passages.shape[0]
    chips = lax.axis_size("yl") * lax.axis_size("z")
    x_size, yh_size = lax.axis_size("x"), lax.axis_size("yh")
    rows, wide = chips * own_rows, CORES * block_rows
    chip = lax.axis_index("yl") * lax.axis_size("z") + lax.axis_index("z")
    core, x, yh = lax.axis_index("core"), lax.axis_index("x"), lax.axis_index("yh")
    places = jnp.stack(
        [(chip * CORES + core) * block_rows, (chip * CORES + 1 - core) * block_rows, x, yh]
    ).astype(i32)

    codes = jnp.concatenate([teacher_rows & 255, positives & 255, lax.shift_right_logical(positives, 8) & 255], axis=0)
    codes = jnp.pad(codes, ((0, own_rows - codes.shape[0]), (0, LANES - own_rows)))
    sent = jnp.concatenate([queries[0], codes.astype(bf16)], axis=1)
    passages_other = shift(passages, "core", 1)
    query = lax.all_to_all(
        jnp.broadcast_to(sent[None], (chips,) + sent.shape), CHIPS, 0, 0, tiled=True
    ).reshape(rows, depth + LANES)

    table = pl.pallas_call(
        teacher_kernel,
        out_shape=jax.ShapeDtypeStruct((PIECES, block_rows, teacher.shape[1]), bf16),
        in_specs=[VMEM],
        out_specs=VMEM,
        compiler_params=PARAMS,
        cost_estimate=pl.CostEstimate(flops=10**11, bytes_accessed=2**21, transcendentals=0),
    )(teacher[0])
    table_other = shift(table, "core", 1)
    logits, positive, stats = pl.pallas_call(
        score_kernel,
        out_shape=(
            jax.ShapeDtypeStruct((2 * CORES, block_rows, rows), f32),
            jax.ShapeDtypeStruct((1, rows), i32),
            jax.ShapeDtypeStruct((chips, STATS, rows), f32),
        ),
        in_specs=[SMEM] + [VMEM] * 5,
        out_specs=(VMEM,) * 3,
        compiler_params=PARAMS,
    )(places, query, passages, passages_other, table, table_other)
    stats = lax.all_to_all(stats, CHIPS, 0, 0, tiled=True)
    width = depth // x_size
    grads, losses, *packed = pl.pallas_call(
        grad_kernel,
        out_shape=(
            jax.ShapeDtypeStruct((CORES, block_rows, rows), bf16),
            jax.ShapeDtypeStruct((1, rows), f32),
        )
        + (jax.ShapeDtypeStruct((rows + wide * rows // width, width), bf16),) * x_size,
        in_specs=[SMEM] + [VMEM] * 4,
        out_specs=(VMEM,) * (2 + x_size),
        compiler_params=PARAMS,
    )(places, query, logits, positive, stats)
    loss = lax.dynamic_slice_in_dim(losses[0], chip * own_rows, own_rows)

    width = depth // x_size
    query_part = pl.pallas_call(
        query_kernel,
        out_shape=jax.ShapeDtypeStruct((rows, depth), bf16),
        in_specs=[VMEM] * 3 + [ANY],
        out_specs=VMEM,
        compiler_params=PARAMS,
    )(grads, passages, passages_other, packed[0])
    query_parts = lax.all_to_all(query_part.reshape(chips, own_rows, depth), CHIPS, 0, 0, tiled=True)
    packed = shifts(packed, "x")
    part_other = pl.pallas_call(
        functools.partial(other_kernel, rows),
        out_shape=jax.ShapeDtypeStruct((block_rows, width), bf16),
        in_specs=[VMEM] * x_size,
        out_specs=VMEM,
        compiler_params=PARAMS,
        cost_estimate=pl.CostEstimate(flops=10**11, bytes_accessed=2**21, transcendentals=0),
    )(*packed)
    parts = pl.pallas_call(
        functools.partial(own_kernel, x_size, rows),
        out_shape=(jax.ShapeDtypeStruct((block_rows, width // yh_size), bf16),) * yh_size,
        in_specs=[SMEM] + [VMEM] * (x_size + 1),
        out_specs=(VMEM,) * yh_size,
        scratch_shapes=[pltpu.VMEM((block_rows, width), bf16)],
        compiler_params=PARAMS,
    )(places, *packed, shift(part_other, "core", 1))
    parts = shifts(parts, "yh")
    query_total, passage_total = pl.pallas_call(
        sum_kernel,
        out_shape=(
            jax.ShapeDtypeStruct((own_rows, depth), bf16),
            jax.ShapeDtypeStruct(parts[0].shape, bf16),
        ),
        in_specs=[VMEM] * (1 + yh_size),
        out_specs=(VMEM,) * 2,
        compiler_params=PARAMS,
    )(query_parts, *parts)
    return loss[None], query_total[None], passage_total


def solution(mesh):
    blk, qgroup = mesh.devices.shape
    split = Mesh(
        mesh.devices.reshape(YL, blk // (YL * CORES), CORES, X, qgroup // X),
        ("yl", "z", "core", "x", "yh"),
    )
    blk, qgroup = ("yl", "z", "core"), ("x", "yh")
    in_specs = (
        P(qgroup, blk, None),
        P(blk, None),
        P(qgroup, None, blk),
        P(qgroup, blk),
        P(qgroup, blk),
    )
    out_specs = (P(qgroup, blk), P(qgroup, blk, None), P(blk, qgroup))
    return jax.shard_map(per_device, mesh=split, in_specs=in_specs, out_specs=out_specs, check_vma=False)
```

```python
import functools

import jax
import jax.numpy as jnp
from jax import lax
from jax.experimental import pallas as pl
from jax.experimental.pallas import tpu as pltpu
from jax.sharding import Mesh, PartitionSpec as P

inv_temp = 50.0
YL, CORES, X = 2, 2, 4
LANES = 128
STATS = 8
PIECES = 3
CHIPS = ("yl", "z")
f32, bf16, i32 = jnp.float32, jnp.bfloat16, jnp.int32
VMEM = pl.BlockSpec(memory_space=pltpu.VMEM)
ANY = pl.BlockSpec(memory_space=pl.ANY)
SMEM = pl.BlockSpec(memory_space=pltpu.SMEM)
PARAMS = pltpu.CompilerParams(vmem_limit_bytes=16 * 1024 * 1024)


def shift(value, axis, by):
    if by == 0:
        return value
    size = lax.axis_size(axis)
    return lax.ppermute(value, axis, [(i, (i + by) % size) for i in range(size)])


def shifts(values, axis):
    size = len(values)
    order = sorted(range(size), key=lambda d: (-min(d, size - d), d))
    return [shift(values[d], axis, d) for d in order]


def hits(positive, place, shape):
    return lax.broadcasted_iota(i32, shape, 0) + place == positive


def teacher_kernel(teacher, out):
    rest = teacher[...].T
    for i in range(PIECES):
        piece = rest.astype(bf16)
        out[i] = piece
        rest = rest - piece.astype(f32)


def indices(codes, own_rows):
    rows, lanes = codes.shape
    first, second = (lax.broadcasted_iota(i32, (lanes, rows), k) for k in (0, 1))
    spread = (lax.rem(second, own_rows) == first).astype(f32).astype(bf16)
    spread = jnp.dot(codes, spread, preferred_element_type=f32)
    first, second = (lax.broadcasted_iota(i32, (rows, rows), k) for k in (0, 1))
    begin = second - lax.rem(second, own_rows)
    return [
        jnp.sum(jnp.where(first == begin + kind, spread, 0.0), axis=0, keepdims=True).astype(i32) for kind in range(3)
    ]


def score_kernel(places, query, passages, passages_other, teacher, teacher_other, values, positives, stats):
    depth = passages.shape[1]
    rows = query.shape[0]
    row_index, low, high = indices(query[:, depth:], rows // stats.shape[0])
    positive = low + 256 * high
    positives[...] = positive
    pick = (lax.broadcasted_iota(i32, (teacher.shape[2], rows), 0) == row_index).astype(f32).astype(bf16)
    parts = []
    for half, (block, table) in enumerate(((passages, teacher), (passages_other, teacher_other))):
        s = inv_temp * lax.dot_general(
            block[...], query[:, :depth], (((1,), (1,)), ((), ())), preferred_element_type=f32
        )
        t = sum(jnp.dot(table[i], pick, preferred_element_type=f32) for i in range(PIECES))
        values[half] = s
        values[CORES + half] = t
        parts.append((s, t, hits(positive, places[half], s.shape)))
    top_s, top_t = (jnp.maximum(*[jnp.max(p[i], axis=0, keepdims=True) for p in parts]) for i in (0, 1))
    sums = []
    for s, t, hot in parts:
        below_s, below_t = s - top_s, t - top_t
        weight = jnp.exp(below_t)
        terms = (jnp.exp(below_s), weight, weight * (below_t - below_s), jnp.where(hot, s, 0.0))
        sums.append([jnp.sum(v, axis=0, keepdims=True) for v in terms])
    sums = [a + b for a, b in zip(*sums)]
    whole = jnp.concatenate([top_s, top_t] + sums + [jnp.zeros((STATS - 6, rows), f32)], axis=0)
    stats[...] = jnp.broadcast_to(whole[None], stats.shape)


def grad_kernel(places, query, logits, positives, stats, grads, losses, *packed):
    rows, width = query.shape[0], packed[0].shape[1]
    for d, out in enumerate(packed):
        out[:rows] = query[:, pl.ds(pl.multiple_of(lax.rem(places[2] + d, len(packed)) * width, width), width)]
    tall = packed[0].shape[0] - rows
    tops_s, tops_t, sums_s, sums_t, cross, hit = (stats[:, i, :] for i in range(6))
    top_s, top_t = jnp.max(tops_s, axis=0, keepdims=True), jnp.max(tops_t, axis=0, keepdims=True)
    lower_s, lower_t = tops_s - top_s, tops_t - top_t
    total_s = jnp.sum(jnp.exp(lower_s) * sums_s, axis=0, keepdims=True)
    weight_t = jnp.exp(lower_t)
    total_t = jnp.sum(weight_t * sums_t, axis=0, keepdims=True)
    cross = jnp.sum(weight_t * (cross + (lower_t - lower_s) * sums_t), axis=0, keepdims=True)
    log_s = jnp.log(total_s)
    own = jnp.sum(hit, axis=0, keepdims=True)
    losses[...] = cross / total_t - jnp.log(total_t) + log_s - (own - top_s - log_s)
    scale_s, scale_t = 2.0 * inv_temp / total_s, inv_temp / total_t
    block_rows = logits.shape[1]
    for half in range(CORES):
        hot = hits(positives[...], places[half], logits.shape[1:])
        values = (
            jnp.exp(logits[half] - top_s) * scale_s
            - jnp.exp(logits[CORES + half] - top_t) * scale_t
            - jnp.where(hot, inv_temp, 0.0)
        )
        values = values.astype(bf16)
        grads[half] = values
        steps = block_rows // tall
        for k in range(steps):
            lane = (half * steps + k) * rows
            for out in packed:
                out[rows:, lane : lane + rows] = values[k * tall : (k + 1) * tall]


def query_kernel(grads, passages, passages_other, after, out):
    del after
    total = 0.0
    for half, block in enumerate((passages, passages_other)):
        total += lax.dot_general(grads[half], block[...], (((0,), (0,)), ((), ())), preferred_element_type=f32)
    out[...] = total.astype(bf16)


def products(packed, half, block_rows, rows):
    tall = packed[0].shape[0] - rows
    total = 0.0
    for ref in packed:
        steps = block_rows // tall
        grads = jnp.concatenate(
            [ref[rows:, k * rows : (k + 1) * rows] for k in range(half * steps, (half + 1) * steps)], axis=0
        )
        total += jnp.dot(grads, ref[:rows], preferred_element_type=f32)
    return total


def other_kernel(rows, *refs):
    out = refs[-1]
    out[...] = products(refs[:-1], 1, out.shape[0], rows).astype(bf16)


def own_kernel(groups, rows, places, *refs):
    packed, back, outs, total = refs[:groups], refs[groups], refs[groups + 1 : -1], refs[-1]
    width = outs[0].shape[1]
    total[...] = (products(packed, 0, back.shape[0], rows) + back[...].astype(f32)).astype(bf16)
    for d, out in enumerate(outs):
        out[...] = total[:, pl.ds(pl.multiple_of(lax.rem(places[3] + d, len(outs)) * width, width), width)]


def sum_kernel(query_parts, *refs):
    parts, query_total, total = refs[:-2], refs[-2], refs[-1]
    query_total[...] = sum(query_parts[i].astype(f32) for i in range(query_parts.shape[0])).astype(bf16)
    total[...] = sum(part[...].astype(f32) for part in parts).astype(bf16)


def per_device(queries, passages, teacher, teacher_rows, positives):
    own_rows, depth = queries.shape[1:]
    block_rows = passages.shape[0]
    chips = lax.axis_size("yl") * lax.axis_size("z")
    x_size, yh_size = lax.axis_size("x"), lax.axis_size("yh")
    rows, wide = chips * own_rows, CORES * block_rows
    chip = lax.axis_index("yl") * lax.axis_size("z") + lax.axis_index("z")
    core, x, yh = lax.axis_index("core"), lax.axis_index("x"), lax.axis_index("yh")
    places = jnp.stack(
        [(chip * CORES + core) * block_rows, (chip * CORES + 1 - core) * block_rows, x, yh]
    ).astype(i32)

    codes = jnp.concatenate([teacher_rows & 255, positives & 255, lax.shift_right_logical(positives, 8) & 255], axis=0)
    codes = jnp.pad(codes, ((0, own_rows - codes.shape[0]), (0, LANES - own_rows)))
    sent = jnp.concatenate([queries[0], codes.astype(bf16)], axis=1)
    passages_other = shift(passages, "core", 1)
    query = lax.all_to_all(
        jnp.broadcast_to(sent[None], (chips,) + sent.shape), CHIPS, 0, 0, tiled=True
    ).reshape(rows, depth + LANES)

    table = pl.pallas_call(
        teacher_kernel,
        out_shape=jax.ShapeDtypeStruct((PIECES, block_rows, teacher.shape[1]), bf16),
        in_specs=[VMEM],
        out_specs=VMEM,
        compiler_params=PARAMS,
        cost_estimate=pl.CostEstimate(flops=10**11, bytes_accessed=2**21, transcendentals=0),
    )(teacher[0])
    table_other = shift(table, "core", 1)
    logits, positive, stats = pl.pallas_call(
        score_kernel,
        out_shape=(
            jax.ShapeDtypeStruct((2 * CORES, block_rows, rows), f32),
            jax.ShapeDtypeStruct((1, rows), i32),
            jax.ShapeDtypeStruct((chips, STATS, rows), f32),
        ),
        in_specs=[SMEM] + [VMEM] * 5,
        out_specs=(VMEM,) * 3,
        compiler_params=PARAMS,
    )(places, query, passages, passages_other, table, table_other)
    stats = lax.all_to_all(stats, CHIPS, 0, 0, tiled=True)
    width = depth // x_size
    grads, losses, *packed = pl.pallas_call(
        grad_kernel,
        out_shape=(
            jax.ShapeDtypeStruct((CORES, block_rows, rows), bf16),
            jax.ShapeDtypeStruct((1, rows), f32),
        )
        + (jax.ShapeDtypeStruct((rows + wide * rows // width, width), bf16),) * x_size,
        in_specs=[SMEM] + [VMEM] * 4,
        out_specs=(VMEM,) * (2 + x_size),
        compiler_params=PARAMS,
    )(places, query, logits, positive, stats)
    loss = lax.dynamic_slice_in_dim(losses[0], chip * own_rows, own_rows)

    width = depth // x_size
    query_part = pl.pallas_call(
        query_kernel,
        out_shape=jax.ShapeDtypeStruct((rows, depth), bf16),
        in_specs=[VMEM] * 3 + [ANY],
        out_specs=VMEM,
        compiler_params=PARAMS,
    )(grads, passages, passages_other, packed[0])
    query_parts = lax.all_to_all(query_part.reshape(chips, own_rows, depth), CHIPS, 0, 0, tiled=True)
    packed = shifts(packed, "x")
    part_other = pl.pallas_call(
        functools.partial(other_kernel, rows),
        out_shape=jax.ShapeDtypeStruct((block_rows, width), bf16),
        in_specs=[VMEM] * x_size,
        out_specs=VMEM,
        compiler_params=PARAMS,
        cost_estimate=pl.CostEstimate(flops=10**11, bytes_accessed=2**21, transcendentals=0),
    )(*packed)
    parts = pl.pallas_call(
        functools.partial(own_kernel, x_size, rows),
        out_shape=(jax.ShapeDtypeStruct((block_rows, width // yh_size), bf16),) * yh_size,
        in_specs=[SMEM] + [VMEM] * (x_size + 1),
        out_specs=(VMEM,) * yh_size,
        scratch_shapes=[pltpu.VMEM((block_rows, width), bf16)],
        compiler_params=PARAMS,
    )(places, *packed, shift(part_other, "core", 1))
    parts = shifts(parts, "yh")
    query_total, passage_total = pl.pallas_call(
        sum_kernel,
        out_shape=(
            jax.ShapeDtypeStruct((own_rows, depth), bf16),
            jax.ShapeDtypeStruct(parts[0].shape, bf16),
        ),
        in_specs=[VMEM] * (1 + yh_size),
        out_specs=(VMEM,) * 2,
        compiler_params=PARAMS,
    )(query_parts, *parts)
    return loss[None], query_total[None], passage_total


def solution(mesh):
    blk, qgroup = mesh.devices.shape
    split = Mesh(
        mesh.devices.reshape(YL, blk // (YL * CORES), CORES, X, qgroup // X),
        ("yl", "z", "core", "x", "yh"),
    )
    blk, qgroup = ("yl", "z", "core"), ("x", "yh")
    in_specs = (
        P(qgroup, blk, None),
        P(blk, None),
        P(qgroup, None, blk),
        P(qgroup, blk),
        P(qgroup, blk),
    )
    out_specs = (P(qgroup, blk), P(qgroup, blk, None), P(blk, qgroup))
    return jax.shard_map(per_device, mesh=split, in_specs=in_specs, out_specs=out_specs, check_vma=False)
```

```python
import functools

import jax
import jax.numpy as jnp
from jax import lax
from jax.experimental import pallas as pl
from jax.experimental.pallas import tpu as pltpu
from jax.sharding import Mesh, PartitionSpec as P

inv_temp = 50.0
YL, CORES, X = 2, 2, 4
LANES = 128
STATS = 8
PIECES = 3
CHIPS = ("yl", "z")
f32, bf16, i32 = jnp.float32, jnp.bfloat16, jnp.int32
VMEM = pl.BlockSpec(memory_space=pltpu.VMEM)
ANY = pl.BlockSpec(memory_space=pl.ANY)
SMEM = pl.BlockSpec(memory_space=pltpu.SMEM)
PARAMS = pltpu.CompilerParams(vmem_limit_bytes=16 * 1024 * 1024)


def shift(value, axis, by):
    if by == 0:
        return value
    size = lax.axis_size(axis)
    return lax.ppermute(value, axis, [(i, (i + by) % size) for i in range(size)])


def shifts(values, axis):
    size = len(values)
    order = sorted(range(size), key=lambda d: (-min(d, size - d), -d))
    return [shift(values[d], axis, d) for d in order]


def hits(positive, place, shape):
    return lax.broadcasted_iota(i32, shape, 0) + place == positive


def teacher_kernel(teacher, out):
    rest = teacher[...].T
    for i in range(PIECES):
        piece = rest.astype(bf16)
        out[i] = piece
        rest = rest - piece.astype(f32)


def indices(codes, own_rows):
    rows, lanes = codes.shape
    first, second = (lax.broadcasted_iota(i32, (lanes, rows), k) for k in (0, 1))
    spread = (lax.rem(second, own_rows) == first).astype(f32).astype(bf16)
    spread = jnp.dot(codes, spread, preferred_element_type=f32)
    first, second = (lax.broadcasted_iota(i32, (rows, rows), k) for k in (0, 1))
    begin = second - lax.rem(second, own_rows)
    return [
        jnp.sum(jnp.where(first == begin + kind, spread, 0.0), axis=0, keepdims=True).astype(i32) for kind in range(3)
    ]


def score_kernel(places, query, passages, passages_other, teacher, teacher_other, values, positives, stats):
    depth = passages.shape[1]
    rows = query.shape[0]
    row_index, low, high = indices(query[:, depth:], rows // stats.shape[0])
    positive = low + 256 * high
    positives[...] = positive
    pick = (lax.broadcasted_iota(i32, (teacher.shape[2], rows), 0) == row_index).astype(f32).astype(bf16)
    parts = []
    for half, (block, table) in enumerate(((passages, teacher), (passages_other, teacher_other))):
        s = inv_temp * lax.dot_general(
            block[...], query[:, :depth], (((1,), (1,)), ((), ())), preferred_element_type=f32
        )
        t = sum(jnp.dot(table[i], pick, preferred_element_type=f32) for i in range(PIECES))
        values[half] = s
        values[CORES + half] = t
        parts.append((s, t, hits(positive, places[half], s.shape)))
    top_s, top_t = (jnp.maximum(*[jnp.max(p[i], axis=0, keepdims=True) for p in parts]) for i in (0, 1))
    sums = []
    for s, t, hot in parts:
        below_s, below_t = s - top_s, t - top_t
        weight = jnp.exp(below_t)
        terms = (jnp.exp(below_s), weight, weight * (below_t - below_s), jnp.where(hot, s, 0.0))
        sums.append([jnp.sum(v, axis=0, keepdims=True) for v in terms])
    sums = [a + b for a, b in zip(*sums)]
    whole = jnp.concatenate([top_s, top_t] + sums + [jnp.zeros((STATS - 6, rows), f32)], axis=0)
    stats[...] = jnp.broadcast_to(whole[None], stats.shape)


def grad_kernel(places, query, logits, positives, stats, grads, losses, *packed):
    rows, width = query.shape[0], packed[0].shape[1]
    for d, out in enumerate(packed):
        out[:rows] = query[:, pl.ds(pl.multiple_of(lax.rem(places[2] + d, len(packed)) * width, width), width)]
    tall = packed[0].shape[0] - rows
    tops_s, tops_t, sums_s, sums_t, cross, hit = (stats[:, i, :] for i in range(6))
    top_s, top_t = jnp.max(tops_s, axis=0, keepdims=True), jnp.max(tops_t, axis=0, keepdims=True)
    lower_s, lower_t = tops_s - top_s, tops_t - top_t
    total_s = jnp.sum(jnp.exp(lower_s) * sums_s, axis=0, keepdims=True)
    weight_t = jnp.exp(lower_t)
    total_t = jnp.sum(weight_t * sums_t, axis=0, keepdims=True)
    cross = jnp.sum(weight_t * (cross + (lower_t - lower_s) * sums_t), axis=0, keepdims=True)
    log_s = jnp.log(total_s)
    own = jnp.sum(hit, axis=0, keepdims=True)
    losses[...] = cross / total_t - jnp.log(total_t) + log_s - (own - top_s - log_s)
    scale_s, scale_t = 2.0 * inv_temp / total_s, inv_temp / total_t
    block_rows = logits.shape[1]
    for half in range(CORES):
        hot = hits(positives[...], places[half], logits.shape[1:])
        values = (
            jnp.exp(logits[half] - top_s) * scale_s
            - jnp.exp(logits[CORES + half] - top_t) * scale_t
            - jnp.where(hot, inv_temp, 0.0)
        )
        values = values.astype(bf16)
        grads[half] = values
        steps = block_rows // tall
        for k in range(steps):
            lane = (half * steps + k) * rows
            for out in packed:
                out[rows:, lane : lane + rows] = values[k * tall : (k + 1) * tall]


def query_kernel(grads, passages, passages_other, after, out):
    del after
    total = 0.0
    for half, block in enumerate((passages, passages_other)):
        total += lax.dot_general(grads[half], block[...], (((0,), (0,)), ((), ())), preferred_element_type=f32)
    out[...] = total.astype(bf16)


def products(packed, half, block_rows, rows):
    tall = packed[0].shape[0] - rows
    total = 0.0
    for ref in packed:
        steps = block_rows // tall
        grads = jnp.concatenate(
            [ref[rows:, k * rows : (k + 1) * rows] for k in range(half * steps, (half + 1) * steps)], axis=0
        )
        total += jnp.dot(grads, ref[:rows], preferred_element_type=f32)
    return total


def product_kernel(half, rows, *refs):
    out = refs[-1]
    out[...] = products(refs[:-1], half, out.shape[0], rows).astype(out.dtype)


def add_kernel(places, part, back, *outs):
    width = outs[0].shape[1]
    for d, out in enumerate(outs):
        columns = pl.ds(pl.multiple_of(lax.rem(places[3] + d, len(outs)) * width, width), width)
        out[...] = (part[:, columns] + back[:, columns].astype(f32)).astype(bf16)


def sum_kernel(query_parts, *refs):
    parts, query_total, total = refs[:-2], refs[-2], refs[-1]
    query_total[...] = sum(query_parts[i].astype(f32) for i in range(query_parts.shape[0])).astype(bf16)
    total[...] = sum(part[...].astype(f32) for part in parts).astype(bf16)


def per_device(queries, passages, teacher, teacher_rows, positives):
    own_rows, depth = queries.shape[1:]
    block_rows = passages.shape[0]
    chips = lax.axis_size("yl") * lax.axis_size("z")
    x_size, yh_size = lax.axis_size("x"), lax.axis_size("yh")
    rows, wide = chips * own_rows, CORES * block_rows
    chip = lax.axis_index("yl") * lax.axis_size("z") + lax.axis_index("z")
    core, x, yh = lax.axis_index("core"), lax.axis_index("x"), lax.axis_index("yh")
    places = jnp.stack(
        [(chip * CORES + core) * block_rows, (chip * CORES + 1 - core) * block_rows, x, yh]
    ).astype(i32)

    codes = jnp.concatenate([teacher_rows & 255, positives & 255, lax.shift_right_logical(positives, 8) & 255], axis=0)
    codes = jnp.pad(codes, ((0, own_rows - codes.shape[0]), (0, LANES - own_rows)))
    sent = jnp.concatenate([queries[0], codes.astype(bf16)], axis=1)
    passages_other = shift(passages, "core", 1)
    query = lax.all_to_all(
        jnp.broadcast_to(sent[None], (chips,) + sent.shape), CHIPS, 0, 0, tiled=True
    ).reshape(rows, depth + LANES)

    table = pl.pallas_call(
        teacher_kernel,
        out_shape=jax.ShapeDtypeStruct((PIECES, block_rows, teacher.shape[1]), bf16),
        in_specs=[VMEM],
        out_specs=VMEM,
        compiler_params=PARAMS,
        cost_estimate=pl.CostEstimate(flops=10**11, bytes_accessed=2**21, transcendentals=0),
    )(teacher[0])
    table_other = shift(table, "core", 1)
    logits, positive, stats = pl.pallas_call(
        score_kernel,
        out_shape=(
            jax.ShapeDtypeStruct((2 * CORES, block_rows, rows), f32),
            jax.ShapeDtypeStruct((1, rows), i32),
            jax.ShapeDtypeStruct((chips, STATS, rows), f32),
        ),
        in_specs=[SMEM] + [VMEM] * 5,
        out_specs=(VMEM,) * 3,
        compiler_params=PARAMS,
    )(places, query, passages, passages_other, table, table_other)
    stats = lax.all_to_all(stats, CHIPS, 0, 0, tiled=True)
    width = depth // x_size
    grads, losses, *packed = pl.pallas_call(
        grad_kernel,
        out_shape=(
            jax.ShapeDtypeStruct((CORES, block_rows, rows), bf16),
            jax.ShapeDtypeStruct((1, rows), f32),
        )
        + (jax.ShapeDtypeStruct((rows + wide * rows // width, width), bf16),) * x_size,
        in_specs=[SMEM] + [VMEM] * 4,
        out_specs=(VMEM,) * (2 + x_size),
        compiler_params=PARAMS,
    )(places, query, logits, positive, stats)
    loss = lax.dynamic_slice_in_dim(losses[0], chip * own_rows, own_rows)

    width = depth // x_size
    query_part = pl.pallas_call(
        query_kernel,
        out_shape=jax.ShapeDtypeStruct((rows, depth), bf16),
        in_specs=[VMEM] * 3 + [ANY],
        out_specs=VMEM,
        compiler_params=PARAMS,
    )(grads, passages, passages_other, packed[0])
    query_parts = lax.all_to_all(query_part.reshape(chips, own_rows, depth), CHIPS, 0, 0, tiled=True)
    packed = shifts(packed, "x")
    part, part_other = (
        pl.pallas_call(
            functools.partial(product_kernel, half, rows),
            out_shape=jax.ShapeDtypeStruct((block_rows, width), dtype),
            in_specs=[VMEM] * x_size,
            out_specs=VMEM,
            compiler_params=PARAMS,
            cost_estimate=pl.CostEstimate(flops=10 ** (11 if half else 9), bytes_accessed=2**21, transcendentals=0),
        )(*packed)
        for half, dtype in enumerate((f32, bf16))
    )
    parts = pl.pallas_call(
        add_kernel,
        out_shape=(jax.ShapeDtypeStruct((block_rows, width // yh_size), bf16),) * yh_size,
        in_specs=[SMEM] + [VMEM] * 2,
        out_specs=(VMEM,) * yh_size,
        compiler_params=PARAMS,
    )(places, part, shift(part_other, "core", 1))
    parts = shifts(parts, "yh")
    query_total, passage_total = pl.pallas_call(
        sum_kernel,
        out_shape=(
            jax.ShapeDtypeStruct((own_rows, depth), bf16),
            jax.ShapeDtypeStruct(parts[0].shape, bf16),
        ),
        in_specs=[VMEM] * (1 + yh_size),
        out_specs=(VMEM,) * 2,
        compiler_params=PARAMS,
    )(query_parts, *parts)
    return loss[None], query_total[None], passage_total


def solution(mesh):
    blk, qgroup = mesh.devices.shape
    split = Mesh(
        mesh.devices.reshape(YL, blk // (YL * CORES), CORES, X, qgroup // X),
        ("yl", "z", "core", "x", "yh"),
    )
    blk, qgroup = ("yl", "z", "core"), ("x", "yh")
    in_specs = (
        P(qgroup, blk, None),
        P(blk, None),
        P(qgroup, None, blk),
        P(qgroup, blk),
        P(qgroup, blk),
    )
    out_specs = (P(qgroup, blk), P(qgroup, blk, None), P(blk, qgroup))
    return jax.shard_map(per_device, mesh=split, in_specs=in_specs, out_specs=out_specs, check_vma=False)
```
